32 devices in a mesh: dp: 4 (over y, x), blk: 8 (over z, core).
Axes of the slice: x: 2, y: 2, z: 4, core: 2. Of those that a mesh axis runs over, the one named last changes fastest.
Arguments:
- frames: bfloat16 [8192, 1024], P(('dp', 'blk')), may hold values from -6 to 6
- skip_feats: bfloat16 [8192, 1024], P(('dp', 'blk')), may hold values from -6 to 6
- w_skip: bfloat16 [2048, 1024], replicated, may hold values from -0.125 to 0.125
- gain_attn: float32 [1024], replicated, may hold values from 0.1 to 1.9
- w_query: bfloat16 [1024, 1024], replicated, may hold values from -0.1875 to 0.1875
- w_key: bfloat16 [1024, 1024], replicated, may hold values from -0.1875 to 0.1875
- w_value: bfloat16 [1024, 1024], replicated, may hold values from -0.1875 to 0.1875
- w_output: bfloat16 [1024, 1024], replicated, may hold values from -0.75 to 0.75
- gain_ffn: float32 [1024], replicated, may hold values from 0.1 to 1.9
- w_up: bfloat16 [1024, 4096], replicated, may hold values from -0.1875 to 0.1875
- w_down: bfloat16 [4096, 1024], replicated, may hold values from -0.09375 to 0.09375
- cotangent: bfloat16 [8192, 1024], P(('dp', 'blk')), may hold values from -6 to 6
- utt_lengths: int32 [4, 4], P('dp'), may hold values from 1 to 2045, as said below
- padded_lengths: int32 [4, 4], P('dp'), may hold values from 1 to 2045, as said below
Outputs:
- mixed: bfloat16 [8192, 1024], P(('dp', 'blk'))
- grad_frames: bfloat16 [8192, 1024], P(('dp', 'blk'))
- grad_skip: bfloat16 [8192, 1024], P(('dp', 'blk'))
- grad_w_skip: float32 [2048, 1024], P(None, 'dp')
- grad_gain_attn: float32 [1024], P('dp')
- grad_w_query: float32 [1024, 1024], P(None, 'dp')
- grad_w_key: float32 [1024, 1024], P(None, 'dp')
- grad_w_value: float32 [1024, 1024], P(None, 'dp')
- grad_w_output: float32 [1024, 1024], P(None, 'dp')
- grad_gain_ffn: float32 [1024], P('dp')
- grad_w_up: float32 [1024, 4096], P(None, 'dp')
- grad_w_down: float32 [4096, 1024], P(None, 'dp')
The draws below stay inside these ranges and needn't reach their ends.
Inputs may be any that keep to these rules, and one draw needn't show every extreme that they name: `utt_lengths`: each utterance has from 1 to its padded length of live frames; in every group one utterance, which one varies, covers the first frame block and the last one of the group. `padded_lengths`: A group's 4 padded lengths add up to 2048.
All inputs are finite; a program needn't handle non-finite values.
Results may differ from the reference program's by a relative error of at most 0.022.
Values may be sent and summed in bfloat16 or wider, within the bound.
No kernel may reach another device: no remote copies, remote signals or barrier semaphores. Data moves between devices by JAX's collectives and lax.ppermute only.
A program may use at most 192 MiB of HBM per device.

```python
import math
import jax
import jax.numpy as jnp
from jax import lax

D = 1024
HEADS = 16
HEAD_DIM = 64
FF = 4096
TOK_DEV = 256
UTT = 4
SEQ = 2048
TOKENS = 8192
N_DP = 4
N_BLK = 8


def utterance_layout(key):
    pick_key, small_key, cut_key, long_key, force_key = jax.random.split(key, 5)
    longest = jax.random.randint(pick_key, (N_DP, 1), 0, UTT)
    forced_group = jax.random.randint(force_key, (), 0, N_DP)
    is_forced = jnp.arange(N_DP, dtype=jnp.int32)[:, None] == forced_group
    small_most = TOK_DEV // 2 // (UTT - 1)
    small_slots = jax.random.randint(small_key, (N_DP, UTT), 1, small_most + 1)
    small_slots = jnp.where(is_forced, 1, small_slots)
    is_long = jnp.arange(UTT, dtype=jnp.int32)[None, :] == longest
    small_slots = jnp.where(is_long, 0, small_slots)
    padded = jnp.where(is_long, SEQ - jnp.sum(small_slots, axis=1, keepdims=True), small_slots)
    raw_cut = jax.random.randint(cut_key, (N_DP, UTT), 0, 1 << 20)
    small_live = 1 + raw_cut % jnp.maximum(padded, 1)
    long_cut = jax.random.randint(long_key, (N_DP, UTT), 0, TOK_DEV // 4 + 1)
    long_cut = jnp.where(is_forced, 0, long_cut)
    lengths = jnp.where(is_long, padded - long_cut, small_live)
    return (lengths.astype(jnp.int32), padded.astype(jnp.int32))


def draw_utt_lengths(key, part):
    layout = utterance_layout(key)
    return layout[0]


def draw_padded_lengths(key, part):
    layout = utterance_layout(key)
    return layout[1]


def levels(rng, extent, shards, low, largest):
    loudness = 1.0
    for axis_at, blocks in shards:
        heights = jax.random.uniform(jax.random.fold_in(jax.random.fold_in(rng, 6), axis_at), (blocks,), jnp.float32, low / len(shards), largest / len(shards))
        loudness = loudness * jnp.repeat(jnp.exp(heights), extent[axis_at] // blocks).reshape((-1,) + (1,) * (len(extent) - 1 - axis_at))
    return loudness


def scatter_about(own_key, extent, spread, bound, pieces=(), held_as=jnp.bfloat16):
    entries = spread * jax.random.normal(own_key, extent, jnp.float32)
    if pieces:
        entries = entries * levels(own_key, extent, pieces, -0.22, 0.18)
    return jnp.clip(entries, -bound, bound).astype(held_as)


def setup_inputs(seed: int = 0) -> dict:
    streams_of = jax.random.split(jax.random.key(seed), 15)
    return {
        "frames": scatter_about(streams_of[0], (TOKENS, D), 1.0, 6.0, ((0, 32),)),
        "skip_feats": scatter_about(streams_of[1], (TOKENS, D), 1.0, 6.0, ((0, 32),)),
        "w_skip": scatter_about(streams_of[2], (2 * D, D), (2 * D) ** -0.5, 0.125),
        "gain_attn": jnp.clip(1.0 + 0.18 * jax.random.normal(streams_of[3], (D,), jnp.float32), 0.1, 1.9),
        "w_query": scatter_about(streams_of[4], (D, D), D ** -0.5, 0.1875),
        "w_key": scatter_about(streams_of[5], (D, D), D ** -0.5, 0.1875),
        "w_value": scatter_about(streams_of[6], (D, D), D ** -0.5, 0.1875),
        "w_output": scatter_about(streams_of[7], (D, D), (D // 16) ** -0.5, 0.75),
        "gain_ffn": jnp.clip(1.0 + 0.18 * jax.random.normal(streams_of[8], (D,), jnp.float32), 0.1, 1.9),
        "w_up": scatter_about(streams_of[9], (D, FF), D ** -0.5, 0.1875),
        "w_down": scatter_about(streams_of[10], (FF, D), FF ** -0.5, 0.09375),
        "cotangent": scatter_about(streams_of[11], (TOKENS, D), 1.0, 6.0, ((0, 32),)),
        "utt_lengths": draw_utt_lengths(jax.random.fold_in(streams_of[14], 71), 0),
        "padded_lengths": draw_padded_lengths(jax.random.fold_in(streams_of[14], 71), 0),
    }


NEG_FILL = -1e+30
NORM_EPS = 1e-05

@jax.custom_vjp
def low(v):
    return lax.optimization_barrier(v.astype(jnp.bfloat16)).astype(jnp.float32)

@jax.custom_vjp
def low_back(v):
    return v

def low_keep(v):
    return (low(v), None)

def low_pass(kept, grad):
    return (grad,)

def back_keep(v):
    return (v, None)

def back_low(kept, grad):
    return (low(grad),)
low.defvjp(low_keep, low_pass)
low_back.defvjp(back_keep, back_low)

def layer_norm(values, gain_vec):
    centred = values - lax.optimization_barrier(jnp.mean(values, axis=-1, keepdims=True))
    variance = lax.optimization_barrier(jnp.mean(centred * centred, axis=-1, keepdims=True))
    return centred * lax.rsqrt(variance + NORM_EPS) * gain_vec

def matmul(left, right):
    return jnp.dot(left, right, precision=lax.Precision.HIGHEST, preferred_element_type=jnp.float32)

def alibi_slopes(seq_len):
    head_rank = jnp.arange(1, HEADS + 1, dtype=jnp.float32)
    return jnp.exp2(-8.0 * head_rank / HEADS) * (256.0 / seq_len)

def utterance_tables(lengths, padded, positions):
    starts = (jnp.cumsum(padded) - padded).astype(jnp.int32)
    utt_owner = lax.optimization_barrier(jnp.sum((positions[:, None] >= starts[None, :]).astype(jnp.int32), axis=1)) - 1
    is_member = utt_owner[:, None] == jnp.arange(lengths.shape[0], dtype=jnp.int32)[None, :]
    offset_in = positions - lax.optimization_barrier(jnp.sum(jnp.where(is_member, starts[None, :], 0), axis=1))
    is_live = offset_in < lax.optimization_barrier(jnp.sum(jnp.where(is_member, lengths[None, :], 0), axis=1))
    return (utt_owner, is_live)

def group_forward(params, frames_in, skip_in, utt_owner, is_live):
    w_skip, gain_attn, w_query, w_key, w_value, w_output, gain_ffn, w_up, w_down = params
    seq_len = frames_in.shape[0]
    joined = jnp.concatenate([frames_in, skip_in], axis=1)
    hidden = low_back(matmul(joined, w_skip))
    normed = low(layer_norm(hidden, gain_attn))
    queries = low(low_back(matmul(normed, w_query))).reshape(seq_len, HEADS, HEAD_DIM)
    key_rows = low(low_back(matmul(normed, w_key))).reshape(seq_len, HEADS, HEAD_DIM)
    value_rows = low(low_back(matmul(normed, w_value))).reshape(seq_len, HEADS, HEAD_DIM)
    slopes = alibi_slopes(seq_len)
    positions = jnp.arange(seq_len, dtype=jnp.int32)
    block_rows = math.gcd(seq_len, 512)
    inv_root = 1.0 / math.sqrt(HEAD_DIM)

    def attend(row_start):
        query_block = lax.dynamic_slice_in_dim(queries, row_start, block_rows, 0)
        row_pos = row_start + jnp.arange(block_rows, dtype=jnp.int32)
        row_owner = lax.dynamic_slice_in_dim(utt_owner, row_start, block_rows, 0)
        distance = jnp.abs(row_pos[:, None] - positions[None, :]).astype(jnp.float32)
        scores = jnp.einsum('qhd,khd->hqk', query_block, key_rows, precision=lax.Precision.HIGHEST) * inv_root
        scores = low_back(scores - slopes[:, None, None] * distance[None])
        allowed = (row_owner[:, None] == utt_owner[None, :]) & is_live[None, :]
        masked = jnp.where(allowed[None], scores, NEG_FILL)
        row_max = lax.optimization_barrier(jnp.max(masked, axis=-1, keepdims=True))
        exp_scores = jnp.where(allowed[None], jnp.exp(masked - row_max), 0.0)
        probs = exp_scores / lax.optimization_barrier(jnp.sum(exp_scores, axis=-1, keepdims=True))
        mixed_heads = jnp.einsum('hqk,khd->qhd', low(probs), value_rows, precision=lax.Precision.HIGHEST)
        return mixed_heads.reshape(block_rows, HEADS * HEAD_DIM)
    row_starts = jnp.arange(0, seq_len, block_rows, dtype=jnp.int32)
    attn = lax.map(jax.checkpoint(attend), row_starts).reshape(seq_len, HEADS * HEAD_DIM)
    attn = low(low_back(attn))
    residual = hidden + low_back(matmul(attn, w_output))
    normed_ffn = low(layer_norm(residual, gain_ffn))
    pre_act = low_back(matmul(normed_ffn, w_up))
    activ = low(jax.nn.gelu(pre_act, approximate=False))
    return residual + matmul(activ, w_down)

def add_pair(first, second):
    return first + second

def reference(frames, skip_feats, w_skip, gain_attn, w_query, w_key, w_value, w_output, gain_ffn, w_up, w_down, cotangent, utt_lengths, padded_lengths):
    params = tuple((weight.astype(jnp.float32) for weight in (w_skip, gain_attn, w_query, w_key, w_value, w_output, gain_ffn, w_up, w_down)))
    seq_len = TOK_DEV * N_BLK
    frames_grp = frames.astype(jnp.float32).reshape(N_DP, seq_len, D)
    skip_grp = skip_feats.astype(jnp.float32).reshape(N_DP, seq_len, D)
    cot_grp = cotangent.astype(jnp.float32).reshape(N_DP, seq_len, D)
    positions = jnp.arange(seq_len, dtype=jnp.int32)

    def one_group(totals, inputs):
        frames_one, skip_one, cot_one, len_one, pad_one = inputs
        utt_owner, is_live = utterance_tables(len_one.astype(jnp.int32), pad_one.astype(jnp.int32), positions)

        def forward(params_in, frames_in, skip_in):
            return group_forward(params_in, frames_in, skip_in, utt_owner, is_live)
        output, pullback = jax.vjp(forward, params, frames_one, skip_one)
        grad_params, grad_in, grad_side = pullback(cot_one)
        totals = jax.tree.map(add_pair, totals, grad_params)
        return (totals, (output.astype(jnp.bfloat16), grad_in.astype(jnp.bfloat16), grad_side.astype(jnp.bfloat16)))
    zeros_init = jax.tree.map(jnp.zeros_like, params)
    totals, outputs = lax.scan(one_group, zeros_init, (frames_grp, skip_grp, cot_grp, utt_lengths, padded_lengths))
    mixed = outputs[0].reshape(N_DP * seq_len, D)
    grad_frames = outputs[1].reshape(N_DP * seq_len, D)
    grad_skip = outputs[2].reshape(N_DP * seq_len, D)
    return (mixed, grad_frames, grad_skip, totals[0], totals[1], totals[2], totals[3], totals[4], totals[5], totals[6], totals[7], totals[8])
```

```python
from functools import partial
import math

import jax
import jax.numpy as jnp
from jax import lax
from jax.experimental import pallas as pl
from jax.experimental.pallas import tpu as pltpu
from jax.sharding import PartitionSpec as P

HEADS = 16
HEAD_DIM = 64


NEG_FILL = -1e30
NORM_EPS = 1e-05


def shifted(array, axis, by):
    size = lax.axis_size(axis)
    return lax.ppermute(array, axis, [(i, (i + by) % size) for i in range(size)])


def layer_norm(values, gain_vec):
    centred = values - jnp.mean(values, axis=-1, keepdims=True)
    variance = jnp.mean(centred * centred, axis=-1, keepdims=True)
    return centred * lax.rsqrt(variance + NORM_EPS) * gain_vec


def alibi_slopes(seq_len):
    head_rank = jnp.arange(1, HEADS + 1, dtype=jnp.float32)
    return jnp.exp2(-8.0 * head_rank / HEADS) * (256.0 / seq_len)


def utterance_tables(lengths, padded, positions):
    starts = jnp.cumsum(padded) - padded
    utt_owner = jnp.sum((positions[:, None] >= starts[None, :]).astype(jnp.int32), axis=1) - 1
    is_member = utt_owner[:, None] == jnp.arange(lengths.shape[0], dtype=jnp.int32)[None, :]
    offset_in = positions - jnp.sum(jnp.where(is_member, starts[None, :], 0), axis=1)
    is_live = offset_in < jnp.sum(jnp.where(is_member, lengths[None, :], 0), axis=1)
    return (utt_owner, is_live)


def product(form, left, right):
    return jnp.einsum(form, left, right, preferred_element_type=jnp.float32)


def on_device_general(
    frames,
    skip_feats,
    w_skip,
    gain_attn,
    w_query,
    w_key,
    w_value,
    w_output,
    gain_ffn,
    w_up,
    w_down,
    cotangent,
    utt_lengths,
    padded_lengths,
):
    row_count = frames.shape[0]
    blocks = lax.axis_size("blk")
    seq_len = row_count * blocks
    inv_root = 1.0 / math.sqrt(HEAD_DIM)
    lengths = utt_lengths[0]
    padded = padded_lengths[0]
    my_block = lax.axis_index("blk")
    row_pos = my_block * row_count + jnp.arange(row_count, dtype=jnp.int32)
    row_owner, row_live = utterance_tables(lengths, padded, row_pos)
    slopes = alibi_slopes(seq_len)
    joined = jnp.concatenate([frames, skip_feats], axis=1)
    hidden = product("rc,cd->rd", joined, w_skip)
    normed = layer_norm(hidden, gain_attn).astype(jnp.bfloat16)
    queries = (
        product("rd,de->re", normed, w_query)
        .astype(jnp.bfloat16)
        .reshape(row_count, HEADS, HEAD_DIM)
    )
    key_rows = (
        product("rd,de->re", normed, w_key).astype(jnp.bfloat16).reshape(row_count, HEADS, HEAD_DIM)
    )
    value_rows = (
        product("rd,de->re", normed, w_value)
        .astype(jnp.bfloat16)
        .reshape(row_count, HEADS, HEAD_DIM)
    )

    def score_block(keys_part, key_start):
        key_count = keys_part.shape[0]
        key_pos = key_start + jnp.arange(key_count, dtype=jnp.int32)
        key_owner, key_live = utterance_tables(lengths, padded, key_pos)
        allowed = (row_owner[:, None] == key_owner[None, :]) & key_live[None, :]
        distance = jnp.abs(row_pos[:, None] - key_pos[None, :]).astype(jnp.float32)
        scores = (
            product("qhd,khd->hqk", queries, keys_part) * inv_root
            - slopes[:, None, None] * distance[None]
        )
        return (scores, allowed)

    start_state = (
        jnp.full((HEADS, row_count), NEG_FILL, jnp.float32),
        jnp.zeros((HEADS, row_count), jnp.float32),
        jnp.zeros((row_count, HEADS, HEAD_DIM), jnp.float32),
    )
    pieces = (
        lax.all_gather(key_rows, "blk", axis=0, tiled=True),
        lax.all_gather(value_rows, "blk", axis=0, tiled=True),
    )
    key_count = pieces[0].shape[0]
    step_rows = math.gcd(key_count, 512)

    def one_block(block_index, state_now):
        running_max, running_sum, accumulated = state_now
        offset_rows = block_index * step_rows
        keys_part = lax.dynamic_slice_in_dim(pieces[0], offset_rows, step_rows, 0)
        vals_part = lax.dynamic_slice_in_dim(pieces[1], offset_rows, step_rows, 0)
        scores, allowed = score_block(keys_part, offset_rows)
        masked = jnp.where(allowed[None], scores, NEG_FILL)
        new_max = jnp.maximum(running_max, jnp.max(masked, axis=-1))
        exp_scores = jnp.where(allowed[None], jnp.exp(masked - new_max[:, :, None]), 0.0)
        rescale = jnp.exp(running_max - new_max)
        running_sum = running_sum * rescale + jnp.sum(exp_scores, axis=-1)
        accumulated = accumulated * rescale.T[:, :, None] + product(
            "hqk,khd->qhd", exp_scores.astype(jnp.bfloat16), vals_part
        )
        return (new_max, running_sum, accumulated)

    running_max, running_sum, accumulated = lax.fori_loop(
        0, key_count // step_rows, one_block, start_state
    )
    attn_full = accumulated / running_sum.T[:, :, None]
    log_total = running_max + jnp.log(running_sum)
    attn = attn_full.reshape(row_count, HEADS * HEAD_DIM).astype(jnp.bfloat16)
    residual = hidden + product("rd,de->re", attn, w_output)
    normed_ffn = layer_norm(residual, gain_ffn).astype(jnp.bfloat16)
    pre_act = product("rd,df->rf", normed_ffn, w_up)
    activ = jax.nn.gelu(pre_act, approximate=False).astype(jnp.bfloat16)
    mixed = (residual + product("rf,fd->rd", activ, w_down)).astype(jnp.bfloat16)
    grad_w_down = product("rf,rd->fd", activ, cotangent)
    grad_activ = product("rd,fd->rf", cotangent, w_down)
    gelu_out, gelu_pull = jax.vjp(partial(jax.nn.gelu, approximate=False), pre_act)
    grad_pre = gelu_pull(grad_activ)[0].astype(jnp.bfloat16)
    grad_w_up = product("rd,rf->df", normed_ffn, grad_pre)
    grad_normed_ffn = product("rf,df->rd", grad_pre, w_up)
    norm_out, norm_pull = jax.vjp(layer_norm, residual, gain_ffn)
    grad_resid_rows, grad_gain_ffn = norm_pull(grad_normed_ffn)
    grad_residual = cotangent.astype(jnp.float32) + grad_resid_rows
    grad_branch = grad_residual.astype(jnp.bfloat16)
    grad_w_output = product("rd,re->de", attn, grad_branch)
    grad_attn = (
        product("re,de->rd", grad_branch, w_output)
        .astype(jnp.bfloat16)
        .reshape(row_count, HEADS, HEAD_DIM)
    )
    delta = jnp.sum(grad_attn.astype(jnp.float32) * attn_full, axis=-1).T

    def back_turn(turn_index, state_now):
        keys_now, vals_now, grad_keys, grad_vals, grad_queries = state_now
        source = (my_block - turn_index) % blocks
        scores, allowed = score_block(keys_now, source * row_count)
        probs = jnp.where(allowed[None], jnp.exp(scores - log_total[:, :, None]), 0.0)
        grad_vals = grad_vals + product("hqk,qhd->khd", probs.astype(jnp.bfloat16), grad_attn)
        grad_probs = product("qhd,khd->hqk", grad_attn, vals_now)
        grad_scores = (probs * (grad_probs - delta[:, :, None])).astype(jnp.bfloat16)
        grad_queries = grad_queries + product("hqk,khd->qhd", grad_scores, keys_now) * inv_root
        grad_keys = grad_keys + product("hqk,qhd->khd", grad_scores, queries) * inv_root
        keys_now, vals_now = shifted((keys_now, vals_now), "blk", 1)
        grad_keys, grad_vals = (
            shifted(grad_keys.astype(jnp.bfloat16), "blk", 1).astype(grad_keys.dtype),
            shifted(grad_vals.astype(jnp.bfloat16), "blk", 1).astype(grad_vals.dtype),
        )
        return (keys_now, vals_now, grad_keys, grad_vals, grad_queries)

    zero_heads = jnp.zeros((row_count, HEADS, HEAD_DIM), jnp.float32)
    cycle_state = lax.fori_loop(
        0, blocks, back_turn, (key_rows, value_rows, zero_heads, zero_heads, zero_heads)
    )
    grad_keys_low = cycle_state[2].reshape(row_count, HEADS * HEAD_DIM).astype(jnp.bfloat16)
    grad_vals_low = cycle_state[3].reshape(row_count, HEADS * HEAD_DIM).astype(jnp.bfloat16)
    grad_query_low = cycle_state[4].reshape(row_count, HEADS * HEAD_DIM).astype(jnp.bfloat16)
    grad_w_query = product("rd,re->de", normed, grad_query_low)
    grad_w_key = product("rd,re->de", normed, grad_keys_low)
    grad_w_value = product("rd,re->de", normed, grad_vals_low)
    grad_normed = (
        product("re,de->rd", grad_query_low, w_query)
        + product("re,de->rd", grad_keys_low, w_key)
        + product("re,de->rd", grad_vals_low, w_value)
    )
    norm_first, first_pull = jax.vjp(layer_norm, hidden, gain_attn)
    grad_hidden_rows, grad_gain_attn = first_pull(grad_normed)
    grad_hidden = (grad_residual + grad_hidden_rows).astype(jnp.bfloat16)
    grad_w_skip = product("rc,rd->cd", joined, grad_hidden)
    grad_joined = product("rd,cd->rc", grad_hidden, w_skip)
    model_width = frames.shape[1]
    grad_frames = grad_joined[:, :model_width].astype(jnp.bfloat16)
    grad_skip = grad_joined[:, model_width:].astype(jnp.bfloat16)
    shares = (
        lax.psum_scatter(
            grad_w_skip.astype(jnp.bfloat16), "dp", scatter_dimension=1, tiled=True
        ).astype(jnp.float32),
        lax.psum_scatter(
            grad_w_query.astype(jnp.bfloat16), "dp", scatter_dimension=1, tiled=True
        ).astype(jnp.float32),
        lax.psum_scatter(
            grad_w_key.astype(jnp.bfloat16), "dp", scatter_dimension=1, tiled=True
        ).astype(jnp.float32),
        lax.psum_scatter(
            grad_w_value.astype(jnp.bfloat16), "dp", scatter_dimension=1, tiled=True
        ).astype(jnp.float32),
        lax.psum_scatter(
            grad_w_output.astype(jnp.bfloat16), "dp", scatter_dimension=1, tiled=True
        ).astype(jnp.float32),
        lax.psum_scatter(
            grad_w_up.astype(jnp.bfloat16), "dp", scatter_dimension=1, tiled=True
        ).astype(jnp.float32),
        lax.psum_scatter(
            grad_w_down.astype(jnp.bfloat16), "dp", scatter_dimension=1, tiled=True
        ).astype(jnp.float32),
        lax.psum_scatter(
            grad_gain_attn.astype(jnp.bfloat16), "dp", scatter_dimension=0, tiled=True
        ).astype(jnp.float32),
        lax.psum_scatter(
            grad_gain_ffn.astype(jnp.bfloat16), "dp", scatter_dimension=0, tiled=True
        ).astype(jnp.float32),
    )
    totals = (
        lax.psum(shares[0].astype(jnp.bfloat16), "blk").astype(jnp.float32),
        lax.psum(shares[1].astype(jnp.bfloat16), "blk").astype(jnp.float32),
        lax.psum(shares[2].astype(jnp.bfloat16), "blk").astype(jnp.float32),
        lax.psum(shares[3].astype(jnp.bfloat16), "blk").astype(jnp.float32),
        lax.psum(shares[4].astype(jnp.bfloat16), "blk").astype(jnp.float32),
        lax.psum(shares[5].astype(jnp.bfloat16), "blk").astype(jnp.float32),
        lax.psum(shares[6].astype(jnp.bfloat16), "blk").astype(jnp.float32),
        lax.psum(shares[7].astype(jnp.bfloat16), "blk").astype(jnp.float32),
        lax.psum(shares[8].astype(jnp.bfloat16), "blk").astype(jnp.float32),
    )
    return (
        mixed,
        grad_frames,
        grad_skip,
        totals[0],
        totals[7],
        totals[1],
        totals[2],
        totals[3],
        totals[4],
        totals[8],
        totals[5],
        totals[6],
    )


BF = jnp.bfloat16
F32 = jnp.float32
NT = (((1,), (1,)), ((), ()))
NN = (((1,), (0,)), ((), ()))
TN = (((0,), (0,)), ((), ()))
TILE = 512
LANES = 128
VMEM_SPEC = pl.BlockSpec(memory_space=pltpu.VMEM)
SMEM_SPEC = pl.BlockSpec(memory_space=pltpu.SMEM)


def mm(left, right, form):
    return lax.dot_general(left, right, form, preferred_element_type=F32)


def split3(value):
    first = value.astype(BF)
    rest = value - first.astype(F32)
    second = rest.astype(BF)
    return first, second, (rest - second.astype(F32)).astype(BF)


def tables_kernel(seg_ref, slope_ref, qx_ref, kx_ref):
    heads = qx_ref.shape[0]
    seq_len = kx_ref.shape[0]
    n_utt = seg_ref.shape[1]

    def one(b, carry):
        rows = pl.ds(pl.multiple_of(b * TILE, TILE), TILE)
        lane = lax.broadcasted_iota(jnp.int32, (TILE, LANES), 1) - HEAD_DIM
        pos = lax.broadcasted_iota(jnp.int32, (TILE, LANES), 0) + b * TILE
        coarse = (pos >> 8).astype(F32)
        fine = (pos & 255).astype(F32)
        first = jnp.zeros_like(lane)
        last = jnp.zeros_like(lane)
        last_live = jnp.zeros_like(lane)
        for u in range(n_utt):
            here = lane == 9 + u
            first = jnp.where(here, seg_ref[0, u], first)
            last = jnp.where(here, seg_ref[1, u], last)
            last_live = jnp.where(here, seg_ref[2, u], last_live)
        member = jnp.where((pos >= first) & (pos < last), 1.0, 0.0)
        is_utt = (lane >= 9) & (lane < 9 + n_utt)
        closed = jnp.where((pos >= first) & (pos < last_live), 0.0, NEG_FILL)
        digits = jnp.where((lane & 1) == 0, coarse, fine)
        keys = jnp.where(is_utt, closed, jnp.where(lane < 6, digits, 1.0))
        keys = jnp.where((lane >= 0) & (lane < 9 + n_utt), keys, 0.0)
        kx_ref[rows, :] = keys.astype(BF)
        for h in range(heads):
            for s in range(2):
                sign = 1.0 if s == 0 else -1.0
                out = jnp.where(is_utt, member, 0.0)
                for e in range(6):
                    out = jnp.where(lane == e, slope_ref[h, e] * sign, out)
                for p, piece in enumerate(split3(pos.astype(F32) * (slope_ref[h, 6] * -sign))):
                    out = jnp.where(lane == 6 + p, piece.astype(F32), out)
                qx_ref[h, s, rows, :] = out.astype(BF)
        return carry

    lax.fori_loop(0, seq_len // TILE, one, 0)


def attn_tables(lengths, padded, slopes, seq_len):
    starts = jnp.cumsum(padded) - padded
    segments = jnp.stack([starts, starts + padded, starts + lengths]).astype(jnp.int32)
    heads = slopes.shape[0]
    cols = []
    rest = slopes
    for _ in range(3):
        piece = lax.reduce_precision(rest, 8, 7)
        rest = rest - piece
        cols += [piece * 256.0, piece]
    coefs = jnp.stack(cols + [slopes], axis=1)
    qx, kx = pl.pallas_call(
        tables_kernel,
        out_shape=(
            jax.ShapeDtypeStruct((heads, 2, seq_len, LANES), BF),
            jax.ShapeDtypeStruct((seq_len, LANES), BF),
        ),
        in_specs=[SMEM_SPEC, SMEM_SPEC],
        out_specs=(VMEM_SPEC, VMEM_SPEC),
        compiler_params=pltpu.CompilerParams(vmem_limit_bytes=24 * 2**20),
        name="attn_tables",
    )(segments, coefs)
    return coefs, qx, kx


def head_first(tile, h):
    wide = tile.astype(F32)
    return pltpu.roll(wide, HEAD_DIM, 1) if h else wide


def ahead_of(rows, cols, axis):
    return jnp.maximum(
        lax.broadcasted_iota(jnp.int32, (rows, cols), axis)
        - lax.broadcasted_iota(jnp.int32, (rows, cols), 1 - axis),
        0,
    ).astype(F32)


def fwd_kernel(coef_ref, qkv_ref, qx_ref, kx_ref, o_ref, olow_ref, qb_ref, ka_ref, va_ref, s_ref):
    seq_len = qkv_ref.shape[0]
    blocks = seq_len // TILE
    heads = qx_ref.shape[0]
    for h in range(heads):
        lo = h * HEAD_DIM

        def prepare(b, carry, h=h):
            rows = pl.ds(pl.multiple_of(b * TILE, TILE), TILE)
            low_lane = lax.broadcasted_iota(jnp.int32, (TILE, LANES), 1) < HEAD_DIM
            q = head_first(qkv_ref[rows, :LANES], h) * 0.125
            k = head_first(qkv_ref[rows, LANES : 2 * LANES], h)
            v = head_first(qkv_ref[rows, 2 * LANES :], h)
            lane = lax.broadcasted_iota(jnp.int32, (TILE, LANES), 1)
            ka_ref[h, rows, :] = jnp.where(low_lane, k, kx_ref[rows, :].astype(F32)).astype(BF)
            va_ref[h, rows, :] = jnp.where(
                low_lane, v, jnp.where(lane < HEAD_DIM + 3, 1.0, 0.0)
            ).astype(BF)
            for s in range(2):
                qb_ref[h, s, rows, :] = jnp.where(
                    low_lane, q, qx_ref[h, s, rows, :].astype(F32)
                ).astype(BF)
            return carry

        lax.fori_loop(0, blocks, prepare, 0)

        def one(qb, carry, h=h, lo=lo):
            rows = pl.ds(pl.multiple_of(qb * TILE, TILE), TILE)
            slope = coef_ref[h, 6]
            top = None
            for t in range(blocks):
                kb = lax.rem(qb + t, blocks)
                krows = pl.ds(pl.multiple_of(kb * TILE, TILE), TILE)
                side = (kb > qb).astype(jnp.int32)
                scores = mm(qb_ref[h, side, rows, :], ka_ref[h, krows, :], NT)
                if t == 0:
                    scores = scores - ahead_of(TILE, TILE, 1) * (2.0 * slope)
                s_ref[:, t * TILE : (t + 1) * TILE] = scores
                part = jnp.max(scores, axis=1, keepdims=True)
                top = part if top is None else jnp.maximum(top, part)
            acc = jnp.zeros((TILE, LANES), F32)
            for t in range(blocks):
                kb = lax.rem(qb + t, blocks)
                krows = pl.ds(pl.multiple_of(kb * TILE, TILE), TILE)
                probs = jnp.exp(s_ref[:, t * TILE : (t + 1) * TILE] - top).astype(BF)
                acc = acc + mm(probs, va_ref[h, krows, :], NN)
            total = acc[:, HEAD_DIM : HEAD_DIM + 1]
            out = acc[:, :HEAD_DIM] / total
            o_ref[rows, lo : lo + HEAD_DIM] = out
            olow_ref[rows, lo : lo + HEAD_DIM] = out.astype(BF)
            log_total = top + jnp.log(total)
            lane = lax.broadcasted_iota(jnp.int32, (TILE, LANES), 1)
            row_pos = (qb * TILE + lax.broadcasted_iota(jnp.int32, (TILE, 1), 0)).astype(F32)
            for s in range(2):
                base = row_pos * (slope * (1.0 if s else -1.0)) - log_total
                full = qb_ref[h, s, rows, :].astype(F32)
                for p, piece in enumerate(split3(base)):
                    full = jnp.where(lane == HEAD_DIM + 6 + p, piece.astype(F32), full)
                qb_ref[h, s, rows, :] = full.astype(BF)
            return carry

        lax.fori_loop(0, blocks, one, 0)


def attn_fwd(coefs, qkv, qx, kx):
    seq_len = qkv.shape[0]
    heads = coefs.shape[0]
    width = heads * HEAD_DIM
    return pl.pallas_call(
        fwd_kernel,
        out_shape=(
            jax.ShapeDtypeStruct((seq_len, width), F32),
            jax.ShapeDtypeStruct((seq_len, width), BF),
            jax.ShapeDtypeStruct((heads, 2, seq_len, LANES), BF),
            jax.ShapeDtypeStruct((heads, seq_len, LANES), BF),
            jax.ShapeDtypeStruct((heads, seq_len, LANES), BF),
        ),
        in_specs=[SMEM_SPEC, VMEM_SPEC, VMEM_SPEC, VMEM_SPEC],
        out_specs=(VMEM_SPEC,) * 5,
        scratch_shapes=[pltpu.VMEM((TILE, seq_len), F32)],
        compiler_params=pltpu.CompilerParams(vmem_limit_bytes=36 * 2**20),
        cost_estimate=pl.CostEstimate(
            flops=16 * seq_len * seq_len * width,
            bytes_accessed=10 * 2**20,
            transcendentals=heads * seq_len * seq_len,
        ),
        name="attn_fwd",
    )(coefs, qkv, qx, kx)


def bwd_kernel(coef_ref, go_ref, o_ref, qb_ref, ka_ref, va_ref, dqkv_ref, ga_ref, dq_ref, kt_ref):
    seq_len = go_ref.shape[0]
    blocks = seq_len // TILE
    heads = ka_ref.shape[0]
    width = heads * HEAD_DIM
    for h in range(heads):
        lo = h * HEAD_DIM

        def prepare(b, carry, h=h, lo=lo):
            rows = pl.ds(pl.multiple_of(b * TILE, TILE), TILE)
            go = go_ref[rows, lo : lo + HEAD_DIM].astype(F32)
            delta = jnp.sum(go * o_ref[rows, lo : lo + HEAD_DIM], axis=1, keepdims=True)
            lane = lax.broadcasted_iota(jnp.int32, (TILE, LANES), 1)
            full = jnp.where(lane < HEAD_DIM, head_first(go_ref[rows, :], h), 0.0)
            for p, piece in enumerate(split3(-delta)):
                full = jnp.where(lane == HEAD_DIM + p, piece.astype(F32), full)
            ga_ref[h, rows, :] = full.astype(BF)
            kt_ref[h, :, rows] = ka_ref[h, rows, :].astype(F32).T.astype(BF)
            return carry

        lax.fori_loop(0, blocks, prepare, 0)
        dq_ref[...] = jnp.zeros_like(dq_ref)

        def one(kb, carry, h=h, lo=lo):
            krows = pl.ds(pl.multiple_of(kb * TILE, TILE), TILE)
            slope = coef_ref[h, 6]
            ka = ka_ref[h, krows, :]
            va = va_ref[h, krows, :]
            kt = kt_ref[h, :HEAD_DIM, krows]
            dv = jnp.zeros((TILE, LANES), F32)
            dk = jnp.zeros((TILE, LANES), F32)
            for t in range(blocks):
                qb = lax.rem(kb + t, blocks)
                rows = pl.ds(pl.multiple_of(qb * TILE, TILE), TILE)
                ga = ga_ref[h, rows, :]
                qa = qb_ref[h, (kb > qb).astype(jnp.int32), rows, :]
                scores = mm(ka, qa, NT)
                if t == 0:
                    scores = scores - ahead_of(TILE, TILE, 0) * (2.0 * slope)
                probs = jnp.exp(scores)
                ds = (probs * mm(va, ga, NT)).astype(BF)
                dv = dv + mm(probs.astype(BF), ga, NN)
                dk = dk + mm(ds, qa, NN)
                dq_ref[:, rows] += mm(kt, ds, NN)
            dqkv_ref[krows, width + lo : width + lo + HEAD_DIM] = dk[:, :HEAD_DIM].astype(BF)
            dqkv_ref[krows, 2 * width + lo : 2 * width + lo + HEAD_DIM] = dv[
                :, :HEAD_DIM
            ].astype(BF)
            return carry

        lax.fori_loop(0, blocks, one, 0)

        def finish(b, carry, lo=lo):
            rows = pl.ds(pl.multiple_of(b * TILE, TILE), TILE)
            dqkv_ref[rows, lo : lo + HEAD_DIM] = (dq_ref[:, rows].T * 0.125).astype(BF)
            return carry

        lax.fori_loop(0, blocks, finish, 0)


def attn_bwd(coefs, go, o, qb, ka, va):
    seq_len = go.shape[0]
    heads = coefs.shape[0]
    width = heads * HEAD_DIM
    return pl.pallas_call(
        bwd_kernel,
        out_shape=jax.ShapeDtypeStruct((seq_len, 3 * width), BF),
        in_specs=[SMEM_SPEC] + [VMEM_SPEC] * 5,
        out_specs=VMEM_SPEC,
        scratch_shapes=[
            pltpu.VMEM((heads, seq_len, LANES), BF),
            pltpu.VMEM((HEAD_DIM, seq_len), F32),
            pltpu.VMEM((heads, LANES, seq_len), BF),
        ],
        compiler_params=pltpu.CompilerParams(vmem_limit_bytes=36 * 2**20),
        cost_estimate=pl.CostEstimate(
            flops=40 * seq_len * seq_len * width,
            bytes_accessed=10 * 2**20,
            transcendentals=heads * seq_len * seq_len,
        ),
        name="attn_bwd",
    )(coefs, go, o, qb, ka, va)


def ffn_kernel(nf_ref, cot_ref, up_ref, down_ref, mix_in, gnf_in, mix_ref, gnf_ref, gwd_ref, gwu_ref):
    @pl.when(pl.program_id(0) == 0)
    def _():
        mix_ref[...] = mix_in[...]
        gnf_ref[...] = gnf_in[...]

    nf = nf_ref[...]
    cot = cot_ref[...]
    up = up_ref[...]
    down = down_ref[...]
    pre = mm(nf, up, NN)
    phi = 0.5 + 0.5 * lax.erf(pre * math.sqrt(0.5))
    activ = (pre * phi).astype(BF)
    slope = phi + pre * (jnp.exp(-0.5 * pre * pre) * (1.0 / math.sqrt(2.0 * math.pi)))
    grad_pre = (slope * mm(cot, down, NT)).astype(BF)
    mix_ref[...] += mm(activ, down, NN)
    gnf_ref[...] += mm(grad_pre, up, NT)
    shards, _, cols = gwd_ref.shape
    gwd = mm(activ, cot, TN).astype(BF)
    for s in range(shards):
        gwd_ref[s] = gwd[:, s * cols : (s + 1) * cols]
    gwu = mm(nf, grad_pre, TN).astype(BF)
    for j in range(gwu_ref.shape[1]):
        gwu_ref[0, j] = gwu[:, j * cols : (j + 1) * cols]


def ffn_part(nf, cot, w_up, w_down, mix, gnf, shards, parts, part):
    rows, width = nf.shape
    ff = w_up.shape[1]
    tile = ff // (shards * parts)
    cols = width // shards
    whole = pl.BlockSpec((rows, width), lambda d: (0, 0))
    return pl.pallas_call(
        ffn_kernel,
        grid=(shards,),
        out_shape=(
            jax.ShapeDtypeStruct((rows, width), F32),
            jax.ShapeDtypeStruct((rows, width), F32),
            jax.ShapeDtypeStruct((shards, shards * tile, cols), BF),
            jax.ShapeDtypeStruct((shards, tile // cols, width, cols), BF),
        ),
        in_specs=[
            whole,
            whole,
            pl.BlockSpec((width, tile), lambda d: (0, d * parts + part)),
            pl.BlockSpec((tile, width), lambda d: (d * parts + part, 0)),
            whole,
            whole,
        ],
        out_specs=(
            whole,
            whole,
            pl.BlockSpec((shards, tile, cols), lambda d: (0, d, 0)),
            pl.BlockSpec((1, tile // cols, width, cols), lambda d: (d, 0, 0, 0)),
        ),
        compiler_params=pltpu.CompilerParams(vmem_limit_bytes=40 * 2**20),
        cost_estimate=pl.CostEstimate(
            flops=12 * rows * width * tile * shards,
            bytes_accessed=8 * width * tile * shards,
            transcendentals=2 * rows * tile * shards,
        ),
        name="ffn",
    )(nf, cot, w_up, w_down, mix, gnf)


def add_low(left, right):
    return (left.astype(F32) + right.astype(F32)).astype(BF)


def pick(array, index, axis):
    return lax.dynamic_index_in_dim(array, index, axis, keepdims=False)


BOTH = ("dp", "blk")
CORE_SWAP = [(i, i ^ 1) for i in range(8)]
X_SWAP = [(i, i ^ 1) for i in range(4)]
Y_SWAP = [(i, i ^ 2) for i in range(4)]
Z_STEPS = [[(i, (i + 2 * k) % 8) for i in range(8)] for k in (1, 2, 3)]


def scatter_grad(share):
    shards, rows, cols = share.shape
    part = rows // 16
    blk = lax.axis_index("blk")
    core, level = blk % 2, blk // 2
    dp = lax.axis_index("dp")
    at_x, at_y = dp % 2, dp // 2
    share = share.reshape(2, 2, 4, 2, 2, part, cols)
    came = lax.ppermute(pick(share, 1 - core, 3), "blk", CORE_SWAP)
    share = add_low(pick(share, core, 3), came)
    x_first, y_first = share[:, :, :, 0], share[:, :, :, 1]
    came_x = lax.ppermute(pick(x_first, 1 - at_x, 1), "dp", X_SWAP)
    came_y = lax.ppermute(pick(y_first, 1 - at_y, 0), "dp", Y_SWAP)
    x_first = add_low(pick(x_first, at_x, 1), came_x)
    y_first = add_low(pick(y_first, at_y, 0), came_y)
    came_y = lax.ppermute(pick(x_first, 1 - at_y, 0), "dp", Y_SWAP)
    came_x = lax.ppermute(pick(y_first, 1 - at_x, 0), "dp", X_SWAP)
    x_first = add_low(pick(x_first, at_y, 0), came_y)
    y_first = add_low(pick(y_first, at_x, 0), came_x)
    both = jnp.stack([x_first, y_first], axis=1)
    total = pick(both, level, 0).astype(F32)
    for k in (1, 2, 3):
        total = total + lax.ppermute(
            pick(both, (level + k) % 4, 0), "blk", Z_STEPS[k - 1]
        ).astype(F32)
    return total.astype(BF).reshape(2 * part, cols)


def gather_grads(pieces):
    sizes = [piece.shape[0] for piece in pieces]
    joined = jnp.concatenate(pieces, axis=0) if len(pieces) > 1 else pieces[0]
    whole = lax.all_gather(joined, "blk", axis=0, tiled=False)
    out, at = [], 0
    for size in sizes:
        out.append(whole[:, at : at + size].reshape(8 * size, -1).astype(F32))
        at += size
    return out


def sum_everywhere(values):
    for axis, perm in (("blk", CORE_SWAP), ("dp", X_SWAP), ("dp", Y_SWAP)):
        values = values + lax.ppermute(values, axis, perm)
    parts = [lax.ppermute(values, "blk", perm) for perm in Z_STEPS]
    return values + parts[0] + parts[1] + parts[2]


def heads_to_columns(slab):
    blk = lax.axis_index("blk")
    core, level = blk % 2, blk // 2
    dp = lax.axis_index("dp")
    rows = slab.shape[0] // 2
    halves = [slab[:rows], slab[rows:]]
    for first, half in ((0, 0), (1, 1)):
        mask = 1
        value = halves[half]
        done = 0
        for bit in ((1, 2) if first == 0 else (2, 1)):
            pairs = [
                (p * 8 + b, (p ^ bit) * 8 + b)
                for p in range(4)
                for b in range(8)
                if ((p ^ (b // 2)) & bit) and not ((p ^ (b // 2)) & done)
            ]
            value = add_low(value, lax.ppermute(value, BOTH, pairs))
            done |= bit
        halves[half] = value
    total = jnp.concatenate(halves, axis=0)
    mine = jnp.where(dp == level, total, jnp.zeros_like(total))
    for k in (1, 2, 3):
        pairs = [
            (d * 8 + d * 2 + c, d * 8 + ((d + k) % 4) * 2 + c) for d in range(4) for c in range(2)
        ]
        mine = mine + lax.ppermute(total, BOTH, pairs)
    other = lax.ppermute(mine, "blk", CORE_SWAP)
    return jnp.where(core == 0, mine, other), jnp.where(core == 0, other, mine)


def norm_stats(values):
    centred = values - jnp.mean(values, axis=-1, keepdims=True)
    scale = lax.rsqrt(jnp.mean(centred * centred, axis=-1, keepdims=True) + NORM_EPS)
    return centred * scale, scale


def norm_back(grad, xhat, scale, gain):
    scaled = grad * gain
    inner = jnp.mean(scaled * xhat, axis=-1, keepdims=True)
    rows = scale * (scaled - jnp.mean(scaled, axis=-1, keepdims=True) - xhat * inner)
    return rows, jnp.sum(grad * xhat, axis=0)


def on_device_grid(
    frames,
    skip_feats,
    w_skip,
    gain_attn,
    w_query,
    w_key,
    w_value,
    w_output,
    gain_ffn,
    w_up,
    w_down,
    cotangent,
    utt_lengths,
    padded_lengths,
):
    row_count, width = frames.shape
    blocks = lax.axis_size("blk")
    shards = lax.axis_size("dp")
    seq_len = row_count * blocks
    pair = width // blocks
    blk = lax.axis_index("blk")
    dp = lax.axis_index("dp")

    joined = jnp.concatenate([frames, skip_feats], axis=1)
    hidden = product("rc,cd->rd", joined, w_skip)
    xhat_attn, scale_attn = norm_stats(hidden)
    normed = (xhat_attn * gain_attn).astype(BF)
    normed_all = lax.all_gather(normed, "blk", axis=0, tiled=True)

    slopes = lax.dynamic_slice_in_dim(alibi_slopes(seq_len), blk * 2, 2, 0)
    coefs, qx, kx = attn_tables(utt_lengths[0], padded_lengths[0], slopes, seq_len)
    w_mine = jnp.concatenate(
        [lax.dynamic_slice_in_dim(w, blk * pair, pair, 1) for w in (w_query, w_key, w_value)],
        axis=1,
    )
    qkv = product("rd,de->re", normed_all, w_mine).astype(BF)
    attn_wide, attn_low, qb, ka, va = attn_fwd(coefs, qkv, qx, kx)

    def to_rows(values):
        k = values.shape[1]
        came = lax.all_to_all(values.reshape(blocks, row_count, k), "blk", 0, 0, tiled=True)
        return came

    attn = to_rows(attn_low).transpose(1, 0, 2).reshape(row_count, width)
    residual = hidden + product("rd,de->re", attn, w_output)
    xhat_ffn, scale_ffn = norm_stats(residual)
    normed_ffn = (xhat_ffn * gain_ffn).astype(BF)

    mix, gnf = residual, jnp.zeros_like(residual)
    parts = 2
    scattered = []
    for part in range(parts):
        mix, gnf, gwd, gwu = ffn_part(
            normed_ffn, cotangent, w_up, w_down, mix, gnf, shards, parts, part
        )
        scattered.append(scatter_grad(gwd))
        scattered.append(scatter_grad(gwu.reshape(shards, -1, gwu.shape[-1])))
    mixed = mix.astype(BF)

    rows_ffn, grad_gain_ffn = norm_back(gnf, xhat_ffn, scale_ffn, gain_ffn)
    grad_residual = cotangent.astype(F32) + rows_ffn
    grad_branch = grad_residual.astype(BF)
    grad_attn = product("re,de->rd", grad_branch, w_output).astype(BF)
    grad_attn = lax.all_to_all(
        grad_attn.reshape(row_count, blocks, pair).transpose(1, 0, 2), "blk", 0, 0, tiled=True
    ).reshape(seq_len, pair)
    grad_w_output = product("rd,rse->sde", attn, grad_branch.reshape(row_count, shards, -1))
    scattered.append(scatter_grad(grad_w_output.astype(BF)))

    dqkv = attn_bwd(coefs, grad_attn, attn_wide, qb, ka, va)
    slab = product("rd,re->de", normed_all, dqkv).astype(BF)
    came = to_rows(dqkv)
    grad_normed = jnp.zeros_like(hidden)
    for i, w in enumerate((w_query, w_key, w_value)):
        part = came[:, :, i * pair : (i + 1) * pair].transpose(1, 0, 2).reshape(row_count, width)
        grad_normed = grad_normed + product("re,de->rd", part, w)
    first, second = heads_to_columns(slab)

    rows_attn, grad_gain_attn = norm_back(grad_normed, xhat_attn, scale_attn, gain_attn)
    grad_hidden = (grad_residual + rows_attn).astype(BF)
    grad_w_skip = product("rc,rse->sce", joined, grad_hidden.reshape(row_count, shards, -1))
    skip_piece = scatter_grad(grad_w_skip.astype(BF))
    gains = jnp.concatenate([grad_gain_attn, grad_gain_ffn]).reshape(16, -1)
    gains = sum_everywhere(gains).reshape(2, shards, -1)
    gains = pick(gains, dp, 1)

    grad_joined = product("rd,cd->rc", grad_hidden, w_skip)
    grad_frames = grad_joined[:, :width].astype(BF)
    grad_skip = grad_joined[:, width:].astype(BF)

    early = gather_grads(scattered[:2])
    late = gather_grads(scattered[2:])
    (g_skip,) = gather_grads([skip_piece])
    downs = [early[0], late[0]]
    ups = [early[1], late[1]]
    cols = width // shards
    g_down = jnp.stack([d.reshape(shards, -1, cols) for d in downs], axis=1).reshape(-1, cols)
    g_up = jnp.concatenate(
        [u.reshape(-1, width, cols)[j] for u in ups for j in range(u.shape[0] // width)], axis=1
    )
    g_output = late[2]
    g_heads = [
        jnp.concatenate(
            [piece[:, i * pair : (i + 1) * pair] for piece in (first, second)], axis=1
        ).astype(F32)
        for i in range(3)
    ]
    return (
        mixed,
        grad_frames,
        grad_skip,
        g_skip,
        gains[0],
        g_heads[0],
        g_heads[1],
        g_heads[2],
        g_output,
        gains[1],
        g_up,
        g_down,
    )


def solution(mesh):
    shape = dict(mesh.shape)
    grid = (shape["dp"], shape["blk"])
    body = on_device_grid if grid == (4, 8) else on_device_general
    return jax.shard_map(
        body,
        mesh=mesh,
        in_specs=(
            P(("dp", "blk"), None),
            P(("dp", "blk"), None),
            P(),
            P(),
            P(),
            P(),
            P(),
            P(),
            P(),
            P(),
            P(),
            P(("dp", "blk"), None),
            P("dp", None),
            P("dp", None),
        ),
        out_specs=(
            P(("dp", "blk"), None),
            P(("dp", "blk"), None),
            P(("dp", "blk"), None),
            P(None, "dp"),
            P("dp"),
            P(None, "dp"),
            P(None, "dp"),
            P(None, "dp"),
            P(None, "dp"),
            P("dp"),
            P(None, "dp"),
            P(None, "dp"),
        ),
        check_vma=False,
    )
```

```python
from functools import partial
import math

import jax
import jax.numpy as jnp
from jax import lax
from jax.experimental import pallas as pl
from jax.experimental.pallas import tpu as pltpu
from jax.sharding import PartitionSpec as P

HEADS = 16
HEAD_DIM = 64


NEG_FILL = -1e30
NORM_EPS = 1e-05


def shifted(array, axis, by):
    size = lax.axis_size(axis)
    return lax.ppermute(array, axis, [(i, (i + by) % size) for i in range(size)])


def layer_norm(values, gain_vec):
    centred = values - jnp.mean(values, axis=-1, keepdims=True)
    variance = jnp.mean(centred * centred, axis=-1, keepdims=True)
    return centred * lax.rsqrt(variance + NORM_EPS) * gain_vec


def alibi_slopes(seq_len):
    head_rank = jnp.arange(1, HEADS + 1, dtype=jnp.float32)
    return jnp.exp2(-8.0 * head_rank / HEADS) * (256.0 / seq_len)


def utterance_tables(lengths, padded, positions):
    starts = jnp.cumsum(padded) - padded
    utt_owner = jnp.sum((positions[:, None] >= starts[None, :]).astype(jnp.int32), axis=1) - 1
    is_member = utt_owner[:, None] == jnp.arange(lengths.shape[0], dtype=jnp.int32)[None, :]
    offset_in = positions - jnp.sum(jnp.where(is_member, starts[None, :], 0), axis=1)
    is_live = offset_in < jnp.sum(jnp.where(is_member, lengths[None, :], 0), axis=1)
    return (utt_owner, is_live)


def product(form, left, right):
    return jnp.einsum(form, left, right, preferred_element_type=jnp.float32)


def on_device_general(
    frames,
    skip_feats,
    w_skip,
    gain_attn,
    w_query,
    w_key,
    w_value,
    w_output,
    gain_ffn,
    w_up,
    w_down,
    cotangent,
    utt_lengths,
    padded_lengths,
):
    row_count = frames.shape[0]
    blocks = lax.axis_size("blk")
    seq_len = row_count * blocks
    inv_root = 1.0 / math.sqrt(HEAD_DIM)
    lengths = utt_lengths[0]
    padded = padded_lengths[0]
    my_block = lax.axis_index("blk")
    row_pos = my_block * row_count + jnp.arange(row_count, dtype=jnp.int32)
    row_owner, row_live = utterance_tables(lengths, padded, row_pos)
    slopes = alibi_slopes(seq_len)
    joined = jnp.concatenate([frames, skip_feats], axis=1)
    hidden = product("rc,cd->rd", joined, w_skip)
    normed = layer_norm(hidden, gain_attn).astype(jnp.bfloat16)
    queries = (
        product("rd,de->re", normed, w_query)
        .astype(jnp.bfloat16)
        .reshape(row_count, HEADS, HEAD_DIM)
    )
    key_rows = (
        product("rd,de->re", normed, w_key).astype(jnp.bfloat16).reshape(row_count, HEADS, HEAD_DIM)
    )
    value_rows = (
        product("rd,de->re", normed, w_value)
        .astype(jnp.bfloat16)
        .reshape(row_count, HEADS, HEAD_DIM)
    )

    def score_block(keys_part, key_start):
        key_count = keys_part.shape[0]
        key_pos = key_start + jnp.arange(key_count, dtype=jnp.int32)
        key_owner, key_live = utterance_tables(lengths, padded, key_pos)
        allowed = (row_owner[:, None] == key_owner[None, :]) & key_live[None, :]
        distance = jnp.abs(row_pos[:, None] - key_pos[None, :]).astype(jnp.float32)
        scores = (
            product("qhd,khd->hqk", queries, keys_part) * inv_root
            - slopes[:, None, None] * distance[None]
        )
        return (scores, allowed)

    start_state = (
        jnp.full((HEADS, row_count), NEG_FILL, jnp.float32),
        jnp.zeros((HEADS, row_count), jnp.float32),
        jnp.zeros((row_count, HEADS, HEAD_DIM), jnp.float32),
    )
    pieces = (
        lax.all_gather(key_rows, "blk", axis=0, tiled=True),
        lax.all_gather(value_rows, "blk", axis=0, tiled=True),
    )
    key_count = pieces[0].shape[0]
    step_rows = math.gcd(key_count, 512)

    def one_block(block_index, state_now):
        running_max, running_sum, accumulated = state_now
        offset_rows = block_index * step_rows
        keys_part = lax.dynamic_slice_in_dim(pieces[0], offset_rows, step_rows, 0)
        vals_part = lax.dynamic_slice_in_dim(pieces[1], offset_rows, step_rows, 0)
        scores, allowed = score_block(keys_part, offset_rows)
        masked = jnp.where(allowed[None], scores, NEG_FILL)
        new_max = jnp.maximum(running_max, jnp.max(masked, axis=-1))
        exp_scores = jnp.where(allowed[None], jnp.exp(masked - new_max[:, :, None]), 0.0)
        rescale = jnp.exp(running_max - new_max)
        running_sum = running_sum * rescale + jnp.sum(exp_scores, axis=-1)
        accumulated = accumulated * rescale.T[:, :, None] + product(
            "hqk,khd->qhd", exp_scores.astype(jnp.bfloat16), vals_part
        )
        return (new_max, running_sum, accumulated)

    running_max, running_sum, accumulated = lax.fori_loop(
        0, key_count // step_rows, one_block, start_state
    )
    attn_full = accumulated / running_sum.T[:, :, None]
    log_total = running_max + jnp.log(running_sum)
    attn = attn_full.reshape(row_count, HEADS * HEAD_DIM).astype(jnp.bfloat16)
    residual = hidden + product("rd,de->re", attn, w_output)
    normed_ffn = layer_norm(residual, gain_ffn).astype(jnp.bfloat16)
    pre_act = product("rd,df->rf", normed_ffn, w_up)
    activ = jax.nn.gelu(pre_act, approximate=False).astype(jnp.bfloat16)
    mixed = (residual + product("rf,fd->rd", activ, w_down)).astype(jnp.bfloat16)
    grad_w_down = product("rf,rd->fd", activ, cotangent)
    grad_activ = product("rd,fd->rf", cotangent, w_down)
    gelu_out, gelu_pull = jax.vjp(partial(jax.nn.gelu, approximate=False), pre_act)
    grad_pre = gelu_pull(grad_activ)[0].astype(jnp.bfloat16)
    grad_w_up = product("rd,rf->df", normed_ffn, grad_pre)
    grad_normed_ffn = product("rf,df->rd", grad_pre, w_up)
    norm_out, norm_pull = jax.vjp(layer_norm, residual, gain_ffn)
    grad_resid_rows, grad_gain_ffn = norm_pull(grad_normed_ffn)
    grad_residual = cotangent.astype(jnp.float32) + grad_resid_rows
    grad_branch = grad_residual.astype(jnp.bfloat16)
    grad_w_output = product("rd,re->de", attn, grad_branch)
    grad_attn = (
        product("re,de->rd", grad_branch, w_output)
        .astype(jnp.bfloat16)
        .reshape(row_count, HEADS, HEAD_DIM)
    )
    delta = jnp.sum(grad_attn.astype(jnp.float32) * attn_full, axis=-1).T

    def back_turn(turn_index, state_now):
        keys_now, vals_now, grad_keys, grad_vals, grad_queries = state_now
        source = (my_block - turn_index) % blocks
        scores, allowed = score_block(keys_now, source * row_count)
        probs = jnp.where(allowed[None], jnp.exp(scores - log_total[:, :, None]), 0.0)
        grad_vals = grad_vals + product("hqk,qhd->khd", probs.astype(jnp.bfloat16), grad_attn)
        grad_probs = product("qhd,khd->hqk", grad_attn, vals_now)
        grad_scores = (probs * (grad_probs - delta[:, :, None])).astype(jnp.bfloat16)
        grad_queries = grad_queries + product("hqk,khd->qhd", grad_scores, keys_now) * inv_root
        grad_keys = grad_keys + product("hqk,qhd->khd", grad_scores, queries) * inv_root
        keys_now, vals_now = shifted((keys_now, vals_now), "blk", 1)
        grad_keys, grad_vals = (
            shifted(grad_keys.astype(jnp.bfloat16), "blk", 1).astype(grad_keys.dtype),
            shifted(grad_vals.astype(jnp.bfloat16), "blk", 1).astype(grad_vals.dtype),
        )
        return (keys_now, vals_now, grad_keys, grad_vals, grad_queries)

    zero_heads = jnp.zeros((row_count, HEADS, HEAD_DIM), jnp.float32)
    cycle_state = lax.fori_loop(
        0, blocks, back_turn, (key_rows, value_rows, zero_heads, zero_heads, zero_heads)
    )
    grad_keys_low = cycle_state[2].reshape(row_count, HEADS * HEAD_DIM).astype(jnp.bfloat16)
    grad_vals_low = cycle_state[3].reshape(row_count, HEADS * HEAD_DIM).astype(jnp.bfloat16)
    grad_query_low = cycle_state[4].reshape(row_count, HEADS * HEAD_DIM).astype(jnp.bfloat16)
    grad_w_query = product("rd,re->de", normed, grad_query_low)
    grad_w_key = product("rd,re->de", normed, grad_keys_low)
    grad_w_value = product("rd,re->de", normed, grad_vals_low)
    grad_normed = (
        product("re,de->rd", grad_query_low, w_query)
        + product("re,de->rd", grad_keys_low, w_key)
        + product("re,de->rd", grad_vals_low, w_value)
    )
    norm_first, first_pull = jax.vjp(layer_norm, hidden, gain_attn)
    grad_hidden_rows, grad_gain_attn = first_pull(grad_normed)
    grad_hidden = (grad_residual + grad_hidden_rows).astype(jnp.bfloat16)
    grad_w_skip = product("rc,rd->cd", joined, grad_hidden)
    grad_joined = product("rd,cd->rc", grad_hidden, w_skip)
    model_width = frames.shape[1]
    grad_frames = grad_joined[:, :model_width].astype(jnp.bfloat16)
    grad_skip = grad_joined[:, model_width:].astype(jnp.bfloat16)
    shares = (
        lax.psum_scatter(
            grad_w_skip.astype(jnp.bfloat16), "dp", scatter_dimension=1, tiled=True
        ).astype(jnp.float32),
        lax.psum_scatter(
            grad_w_query.astype(jnp.bfloat16), "dp", scatter_dimension=1, tiled=True
        ).astype(jnp.float32),
        lax.psum_scatter(
            grad_w_key.astype(jnp.bfloat16), "dp", scatter_dimension=1, tiled=True
        ).astype(jnp.float32),
        lax.psum_scatter(
            grad_w_value.astype(jnp.bfloat16), "dp", scatter_dimension=1, tiled=True
        ).astype(jnp.float32),
        lax.psum_scatter(
            grad_w_output.astype(jnp.bfloat16), "dp", scatter_dimension=1, tiled=True
        ).astype(jnp.float32),
        lax.psum_scatter(
            grad_w_up.astype(jnp.bfloat16), "dp", scatter_dimension=1, tiled=True
        ).astype(jnp.float32),
        lax.psum_scatter(
            grad_w_down.astype(jnp.bfloat16), "dp", scatter_dimension=1, tiled=True
        ).astype(jnp.float32),
        lax.psum_scatter(
            grad_gain_attn.astype(jnp.bfloat16), "dp", scatter_dimension=0, tiled=True
        ).astype(jnp.float32),
        lax.psum_scatter(
            grad_gain_ffn.astype(jnp.bfloat16), "dp", scatter_dimension=0, tiled=True
        ).astype(jnp.float32),
    )
    totals = (
        lax.psum(shares[0].astype(jnp.bfloat16), "blk").astype(jnp.float32),
        lax.psum(shares[1].astype(jnp.bfloat16), "blk").astype(jnp.float32),
        lax.psum(shares[2].astype(jnp.bfloat16), "blk").astype(jnp.float32),
        lax.psum(shares[3].astype(jnp.bfloat16), "blk").astype(jnp.float32),
        lax.psum(shares[4].astype(jnp.bfloat16), "blk").astype(jnp.float32),
        lax.psum(shares[5].astype(jnp.bfloat16), "blk").astype(jnp.float32),
        lax.psum(shares[6].astype(jnp.bfloat16), "blk").astype(jnp.float32),
        lax.psum(shares[7].astype(jnp.bfloat16), "blk").astype(jnp.float32),
        lax.psum(shares[8].astype(jnp.bfloat16), "blk").astype(jnp.float32),
    )
    return (
        mixed,
        grad_frames,
        grad_skip,
        totals[0],
        totals[7],
        totals[1],
        totals[2],
        totals[3],
        totals[4],
        totals[8],
        totals[5],
        totals[6],
    )


BF = jnp.bfloat16
F32 = jnp.float32
NT = (((1,), (1,)), ((), ()))
NN = (((1,), (0,)), ((), ()))
TN = (((0,), (0,)), ((), ()))
TILE = 512
LANES = 128
SMALL_COST = pl.CostEstimate(flops=1, bytes_accessed=1, transcendentals=0)
SMEM_SPEC = pl.BlockSpec(memory_space=pltpu.SMEM)


def shape_of(shape, dtype):
    return jax.ShapeDtypeStruct(shape, dtype)


def whole_spec(array):
    return pl.BlockSpec(array.shape, lambda *at: (0,) * len(array.shape))


def in_hbm(shapes):
    return [pltpu.HBM(s.shape, s.dtype) for s in shapes]


def from_hbm(arrays):
    return [pltpu.with_memory_space_constraint(a, pltpu.HBM) for a in arrays]


def mm(left, right, form):
    return lax.dot_general(left, right, form, preferred_element_type=F32)


def split3(value):
    first = value.astype(BF)
    rest = value - first.astype(F32)
    second = rest.astype(BF)
    return first, second, (rest - second.astype(F32)).astype(BF)


def tables_kernel(seg_ref, slope_ref, qx_ref, kx_ref):
    heads = qx_ref.shape[0]
    seq_len = kx_ref.shape[0]
    n_utt = seg_ref.shape[1]

    def one(b, carry):
        rows = pl.ds(pl.multiple_of(b * TILE, TILE), TILE)
        lane = lax.broadcasted_iota(jnp.int32, (TILE, LANES), 1) - HEAD_DIM
        pos = lax.broadcasted_iota(jnp.int32, (TILE, LANES), 0) + b * TILE
        coarse = (pos >> 8).astype(F32)
        fine = (pos & 255).astype(F32)
        first = jnp.zeros_like(lane)
        last = jnp.zeros_like(lane)
        last_live = jnp.zeros_like(lane)
        for u in range(n_utt):
            here = lane == 9 + u
            first = jnp.where(here, seg_ref[0, u], first)
            last = jnp.where(here, seg_ref[1, u], last)
            last_live = jnp.where(here, seg_ref[2, u], last_live)
        member = jnp.where((pos >= first) & (pos < last), 1.0, 0.0)
        is_utt = (lane >= 9) & (lane < 9 + n_utt)
        closed = jnp.where((pos >= first) & (pos < last_live), 0.0, NEG_FILL)
        digits = jnp.where((lane & 1) == 0, coarse, fine)
        keys = jnp.where(is_utt, closed, jnp.where(lane < 6, digits, 1.0))
        keys = jnp.where((lane >= 0) & (lane < 9 + n_utt), keys, 0.0)
        kx_ref[rows, :] = keys.astype(BF)
        for h in range(heads):
            for s in range(2):
                sign = 1.0 if s == 0 else -1.0
                out = jnp.where(is_utt, member, 0.0)
                for e in range(6):
                    out = jnp.where(lane == e, slope_ref[h, e] * sign, out)
                for p, piece in enumerate(split3(pos.astype(F32) * (slope_ref[h, 6] * -sign))):
                    out = jnp.where(lane == 6 + p, piece.astype(F32), out)
                qx_ref[h, s, rows, :] = out.astype(BF)
        return carry

    lax.fori_loop(0, seq_len // TILE, one, 0)


def attn_tables(lengths, padded, slopes, seq_len):
    starts = jnp.cumsum(padded) - padded
    segments = jnp.stack([starts, starts + padded, starts + lengths]).astype(jnp.int32)
    heads = slopes.shape[0]
    cols = []
    rest = slopes
    for _ in range(3):
        piece = lax.reduce_precision(rest, 8, 7)
        rest = rest - piece
        cols += [piece * 256.0, piece]
    coefs = jnp.stack(cols + [slopes], axis=1)
    outs = [shape_of((heads, 2, seq_len, LANES), BF), shape_of((seq_len, LANES), BF)]
    qx, kx = pl.pallas_call(
        tables_kernel,
        grid=(1,),
        out_shape=in_hbm(outs),
        in_specs=[SMEM_SPEC, SMEM_SPEC],
        out_specs=[whole_spec(a) for a in outs],
        compiler_params=pltpu.CompilerParams(vmem_limit_bytes=24 * 2**20),
        name="attn_tables",
    )(segments, coefs)
    return coefs, qx, kx


def head_first(tile, h):
    wide = tile.astype(F32)
    return pltpu.roll(wide, HEAD_DIM, 1) if h else wide


def ahead_of(rows, cols, axis):
    return jnp.maximum(
        lax.broadcasted_iota(jnp.int32, (rows, cols), axis)
        - lax.broadcasted_iota(jnp.int32, (rows, cols), 1 - axis),
        0,
    ).astype(F32)


def fwd_kernel(coef_ref, qkv_ref, qx_ref, kx_ref, o_ref, olow_ref, qb_ref, ka_ref, va_ref, s_ref):
    seq_len = qkv_ref.shape[0]
    blocks = seq_len // TILE
    heads = qx_ref.shape[0]
    for h in range(heads):
        lo = h * HEAD_DIM

        def prepare(b, carry, h=h):
            rows = pl.ds(pl.multiple_of(b * TILE, TILE), TILE)
            low_lane = lax.broadcasted_iota(jnp.int32, (TILE, LANES), 1) < HEAD_DIM
            q = head_first(qkv_ref[rows, :LANES], h) * 0.125
            k = head_first(qkv_ref[rows, LANES : 2 * LANES], h)
            v = head_first(qkv_ref[rows, 2 * LANES :], h)
            lane = lax.broadcasted_iota(jnp.int32, (TILE, LANES), 1)
            ka_ref[h, rows, :] = jnp.where(low_lane, k, kx_ref[rows, :].astype(F32)).astype(BF)
            va_ref[h, rows, :] = jnp.where(
                low_lane, v, jnp.where(lane < HEAD_DIM + 3, 1.0, 0.0)
            ).astype(BF)
            for s in range(2):
                qb_ref[h, s, rows, :] = jnp.where(
                    low_lane, q, qx_ref[h, s, rows, :].astype(F32)
                ).astype(BF)
            return carry

        lax.fori_loop(0, blocks, prepare, 0)

        def one(qb, carry, h=h, lo=lo):
            rows = pl.ds(pl.multiple_of(qb * TILE, TILE), TILE)
            slope = coef_ref[h, 6]
            top = None
            for t in range(blocks):
                kb = lax.rem(qb + t, blocks)
                krows = pl.ds(pl.multiple_of(kb * TILE, TILE), TILE)
                side = (kb > qb).astype(jnp.int32)
                scores = mm(qb_ref[h, side, rows, :], ka_ref[h, krows, :], NT)
                if t == 0:
                    scores = scores - ahead_of(TILE, TILE, 1) * (2.0 * slope)
                s_ref[:, t * TILE : (t + 1) * TILE] = scores
                part = jnp.max(scores, axis=1, keepdims=True)
                top = part if top is None else jnp.maximum(top, part)
            acc = jnp.zeros((TILE, LANES), F32)
            for t in range(blocks):
                kb = lax.rem(qb + t, blocks)
                krows = pl.ds(pl.multiple_of(kb * TILE, TILE), TILE)
                probs = jnp.exp(s_ref[:, t * TILE : (t + 1) * TILE] - top).astype(BF)
                acc = acc + mm(probs, va_ref[h, krows, :], NN)
            total = acc[:, HEAD_DIM : HEAD_DIM + 1]
            out = acc[:, :HEAD_DIM] / total
            o_ref[rows, lo : lo + HEAD_DIM] = out
            low = out.astype(BF)
            per = olow_ref.shape[1]
            for p in range(TILE // per):
                olow_ref[qb * (TILE // per) + p, :, lo : lo + HEAD_DIM] = low[p * per : (p + 1) * per]
            log_total = top + jnp.log(total)
            lane = lax.broadcasted_iota(jnp.int32, (TILE, LANES), 1)
            row_pos = (qb * TILE + lax.broadcasted_iota(jnp.int32, (TILE, 1), 0)).astype(F32)
            for s in range(2):
                base = row_pos * (slope * (1.0 if s else -1.0)) - log_total
                full = qb_ref[h, s, rows, :].astype(F32)
                for p, piece in enumerate(split3(base)):
                    full = jnp.where(lane == HEAD_DIM + 6 + p, piece.astype(F32), full)
                qb_ref[h, s, rows, :] = full.astype(BF)
            return carry

        lax.fori_loop(0, blocks, one, 0)


def attn_fwd(coefs, qkv, qx, kx, blocks):
    seq_len = qkv.shape[0]
    heads = coefs.shape[0]
    width = heads * HEAD_DIM
    outs = [
        shape_of((seq_len, width), F32),
        shape_of((blocks, seq_len // blocks, width), BF),
        shape_of((heads, 2, seq_len, LANES), BF),
        shape_of((heads, seq_len, LANES), BF),
        shape_of((heads, seq_len, LANES), BF),
    ]
    return pl.pallas_call(
        fwd_kernel,
        grid=(1,),
        out_shape=in_hbm(outs),
        in_specs=[SMEM_SPEC, *[whole_spec(a) for a in (qkv, qx, kx)]],
        out_specs=[whole_spec(a) for a in outs],
        scratch_shapes=[pltpu.VMEM((TILE, seq_len), F32)],
        compiler_params=pltpu.CompilerParams(vmem_limit_bytes=48 * 2**20),
        cost_estimate=SMALL_COST,
        name="attn_fwd",
    )(coefs, *from_hbm([qkv, qx, kx]))


def pack_rows(ref, b, part, values):
    half = ref.shape[1]
    for p in range(TILE // half):
        lane = part * LANES + (p % 2) * HEAD_DIM
        ref[b * (TILE // (2 * half)) + p // 2, :, lane : lane + HEAD_DIM] = values[
            p * half : (p + 1) * half
        ]


def unpack_pair(first, second):
    low_lane = lax.broadcasted_iota(jnp.int32, first.shape, 1) < HEAD_DIM
    first, second = first.astype(F32), second.astype(F32)
    upper = jnp.where(low_lane, first, pltpu.roll(second, HEAD_DIM, 1))
    lower = jnp.where(low_lane, pltpu.roll(first, HEAD_DIM, 1), second)
    return upper.astype(BF), lower.astype(BF)


def bwd_kernel(h, coef_ref, go_ref, o_ref, qb_ref, ka_ref, va_ref, out_ref, ga_ref, dq_ref, kt_ref):
    seq_len = go_ref.shape[0]
    blocks = seq_len // TILE
    lo = h * HEAD_DIM
    slope = coef_ref[h, 6]

    def prepare(b, carry):
        rows = pl.ds(pl.multiple_of(b * TILE, TILE), TILE)
        go = go_ref[rows, lo : lo + HEAD_DIM].astype(F32)
        delta = jnp.sum(go * o_ref[rows, lo : lo + HEAD_DIM], axis=1, keepdims=True)
        lane = lax.broadcasted_iota(jnp.int32, (TILE, LANES), 1)
        full = jnp.where(lane < HEAD_DIM, head_first(go_ref[rows, :], h), 0.0)
        for p, piece in enumerate(split3(-delta)):
            full = jnp.where(lane == HEAD_DIM + p, piece.astype(F32), full)
        ga_ref[rows, :] = full.astype(BF)
        kt_ref[:, rows] = ka_ref[0, rows, :].astype(F32).T.astype(BF)
        dq_ref[:, rows] = jnp.zeros((HEAD_DIM, TILE), F32)
        return carry

    lax.fori_loop(0, blocks, prepare, 0)

    def one(kb, carry):
        krows = pl.ds(pl.multiple_of(kb * TILE, TILE), TILE)
        ka = ka_ref[0, krows, :]
        va = va_ref[0, krows, :]
        kt = kt_ref[:HEAD_DIM, krows]
        dv = jnp.zeros((TILE, LANES), F32)
        dk = jnp.zeros((TILE, LANES), F32)
        for t in range(blocks):
            qb = lax.rem(kb + t, blocks)
            rows = pl.ds(pl.multiple_of(qb * TILE, TILE), TILE)
            ga = ga_ref[rows, :]
            qa = qb_ref[0, (kb > qb).astype(jnp.int32), rows, :]
            scores = mm(ka, qa, NT)
            if t == 0:
                scores = scores - ahead_of(TILE, TILE, 0) * (2.0 * slope)
            probs = jnp.exp(scores)
            ds = (probs * mm(va, ga, NT)).astype(BF)
            dv = dv + mm(probs.astype(BF), ga, NN)
            dk = dk + mm(ds, qa, NN)
            dq_ref[:, rows] += mm(kt, ds, NN)
        pack_rows(out_ref, kb, 1, dk[:, :HEAD_DIM].astype(BF))
        pack_rows(out_ref, kb, 2, dv[:, :HEAD_DIM].astype(BF))
        return carry

    lax.fori_loop(0, blocks, one, 0)

    def finish(b, carry):
        rows = pl.ds(pl.multiple_of(b * TILE, TILE), TILE)
        pack_rows(out_ref, b, 0, (dq_ref[:, rows].T * 0.125).astype(BF))
        return carry

    lax.fori_loop(0, blocks, finish, 0)


def attn_bwd(h, coefs, go, o, qb, ka, va, blocks):
    seq_len = go.shape[0]
    half = seq_len // (2 * blocks)

    def of_head(array):
        zeros = (0,) * (len(array.shape) - 1)
        return pl.BlockSpec((1, *array.shape[1:]), lambda i: (h, *zeros))

    return pl.pallas_call(
        partial(bwd_kernel, h),
        grid=(1,),
        out_shape=pltpu.HBM((blocks, half, 3 * LANES), BF),
        in_specs=[SMEM_SPEC, whole_spec(go), whole_spec(o), of_head(qb), of_head(ka), of_head(va)],
        out_specs=pl.BlockSpec((blocks, half, 3 * LANES), lambda i: (0, 0, 0)),
        scratch_shapes=[
            pltpu.VMEM((seq_len, LANES), BF),
            pltpu.VMEM((HEAD_DIM, seq_len), F32),
            pltpu.VMEM((LANES, seq_len), BF),
        ],
        compiler_params=pltpu.CompilerParams(vmem_limit_bytes=36 * 2**20),
        cost_estimate=SMALL_COST,
        name="attn_bwd",
    )(coefs, *from_hbm([go, o, qb, ka, va]))


def slab_kernel(left_ref, first_ref, second_ref, out_ref, right_ref):
    @pl.when(pl.program_id(0) == 0)
    def _():
        half = first_ref.shape[1]
        for b in range(first_ref.shape[0]):
            for i in range(3):
                lanes = slice(i * LANES, (i + 1) * LANES)
                upper, lower = unpack_pair(first_ref[b, :, lanes], second_ref[b, :, lanes])
                right_ref[2 * b * half : (2 * b + 1) * half, lanes] = upper
                right_ref[(2 * b + 1) * half : (2 * b + 2) * half, lanes] = lower

    grad = mm(left_ref[...], right_ref[...], TN).astype(BF)
    block = grad.shape[0]
    for i in range(3):
        out_ref[0, i * block : (i + 1) * block] = grad[:, i * LANES : (i + 1) * LANES]


def slab_call(left, first, second):
    seq_len, width = left.shape
    blocks = first.shape[0]
    block = width // blocks
    packed = pl.BlockSpec(first.shape, lambda b: (0, 0, 0))
    return pl.pallas_call(
        slab_kernel,
        grid=(blocks,),
        out_shape=pltpu.HBM((blocks, 3 * block, LANES), BF),
        in_specs=[pl.BlockSpec((seq_len, block), lambda b: (0, b)), packed, packed],
        out_specs=pl.BlockSpec((1, 3 * block, LANES), lambda b: (b, 0, 0)),
        scratch_shapes=[pltpu.VMEM((seq_len, 3 * LANES), BF)],
        compiler_params=pltpu.CompilerParams(vmem_limit_bytes=24 * 2**20),
        cost_estimate=SMALL_COST,
        name="slab",
    )(*from_hbm([left, first, second]))


def norm_stats(values):
    centred = values - jnp.mean(values, axis=-1, keepdims=True)
    scale = lax.rsqrt(jnp.mean(centred * centred, axis=-1, keepdims=True) + NORM_EPS)
    return centred * scale, scale


def norm_back(grad, xhat, scale, gain):
    scaled = grad * gain
    inner = jnp.mean(scaled * xhat, axis=-1, keepdims=True)
    rows = scale * (scaled - jnp.mean(scaled, axis=-1, keepdims=True) - xhat * inner)
    return rows, jnp.sum(grad * xhat, axis=0, keepdims=True)


def put_columns(outs, dp, level, first, wide_ref):
    rows = wide_ref.shape[0]
    cols = outs[0].shape[-1]
    if len(outs) == 1:
        for s in range(outs[0].shape[0]):
            outs[0][s, level, first : first + rows, :] = wide_ref[:, s * cols : (s + 1) * cols]
        return
    for k, out in enumerate(outs):
        at = pl.multiple_of(jnp.bitwise_xor(dp, k) * cols, cols)
        out[level, first : first + rows, :] = wide_ref[:, pl.ds(at, cols)]


def row_kernel(came_ref, hidden_ref, wo_ref, gain_ref, attn_ref, xhat_ref, scale_ref, nf_ref, res_ref):
    for s in range(came_ref.shape[0]):
        attn_ref[:, s * LANES : (s + 1) * LANES] = came_ref[s]
    residual = hidden_ref[...] + mm(attn_ref[...], wo_ref[...], NN)
    xhat, scale = norm_stats(residual)
    xhat_ref[...] = xhat
    scale_ref[...] = scale
    nf_ref[...] = (xhat * gain_ref[...]).astype(BF)
    res_ref[...] = residual


def row_call(came, hidden, w_output, gain):
    rows, width = hidden.shape
    wide, low = shape_of((rows, width), F32), shape_of((rows, width), BF)
    inputs = [came, hidden, w_output, gain]
    outs = [low, wide, shape_of((rows, 1), F32), low, wide]
    return pl.pallas_call(
        row_kernel,
        grid=(1,),
        out_shape=in_hbm(outs),
        in_specs=[whole_spec(a) for a in inputs],
        out_specs=[whole_spec(a) for a in outs],
        compiler_params=pltpu.CompilerParams(vmem_limit_bytes=16 * 2**20),
        cost_estimate=SMALL_COST,
        name="attn_rows",
    )(*from_hbm(inputs))


def ffn_kernel(
    ids_ref, nf_a, nf_b, cot_a, cot_b, up_ref, down_ref, *refs
):
    sums, out, (nf_ref, cot_ref) = refs[:4], refs[4], refs[5:]
    step = pl.program_id(0)
    rows = nf_a.shape[0]

    @pl.when(step == 0)
    def _():
        nf_ref[:rows] = nf_a[...]
        nf_ref[rows:] = nf_b[...]
        cot_ref[:rows] = cot_a[...]
        cot_ref[rows:] = cot_b[...]
        for ref in sums:
            ref[...] = jnp.zeros(ref.shape, F32)

    nf = nf_ref[...]
    cot = cot_ref[...]
    up = up_ref[...]
    down = down_ref[...]
    pre = mm(nf, up, NN)
    phi = 0.5 + 0.5 * lax.erf(pre * math.sqrt(0.5))
    activ = (pre * phi).astype(BF)
    slope = phi + pre * (jnp.exp(-0.5 * pre * pre) * (1.0 / math.sqrt(2.0 * math.pi)))
    grad_pre = (slope * mm(cot, down, NT)).astype(BF)
    mix = mm(activ, down, NN)
    gnf = mm(grad_pre, up, NT)
    for i, part in enumerate((mix[:rows], mix[rows:], gnf[:rows], gnf[rows:])):
        sums[i][...] += part
    gwd = mm(activ, cot, TN).astype(BF)
    gwu = mm(nf, grad_pre, TN).astype(BF)
    shards, levels, _, cols = out.shape
    tile = gwd.shape[0]
    block = gwu.shape[0] // levels
    for s in range(shards):
        out[s, step, :tile, :] = gwd[:, s * cols : (s + 1) * cols]
    for level in range(levels):
        out[step, level, tile:, :] = gwu[level * block : (level + 1) * block]


def ffn_call(ids, nf, cot, w_up, w_down, shards, part):
    rows, width = nf[0].shape
    ff = w_up.shape[1]
    tile = ff // (shards * 4)
    inputs = [*nf, *cot]
    out_sum = shape_of((rows, width), F32)
    out_grad = shape_of((shards, shards, 2 * tile, width // shards), BF)

    def tile_at(d, ids):
        return d * 4 + part * 2 + ids[1]

    return pl.pallas_call(
        ffn_kernel,
        grid_spec=pltpu.PrefetchScalarGridSpec(
            num_scalar_prefetch=1,
            grid=(shards,),
            in_specs=[
                *[whole_spec(array) for array in inputs],
                pl.BlockSpec((width, tile), lambda d, ids: (0, tile_at(d, ids))),
                pl.BlockSpec((tile, width), lambda d, ids: (tile_at(d, ids), 0)),
            ],
            out_specs=[whole_spec(out_sum)] * 4 + [whole_spec(out_grad)],
            scratch_shapes=[
                pltpu.VMEM((2 * rows, width), BF),
                pltpu.VMEM((2 * rows, width), BF),
            ],
        ),
        out_shape=in_hbm([out_sum] * 4 + [out_grad]),
        compiler_params=pltpu.CompilerParams(vmem_limit_bytes=44 * 2**20),
        cost_estimate=SMALL_COST,
        name="ffn",
    )(ids, *from_hbm([*inputs, w_up, w_down]))


def branch_kernel(
    gnf_a, came_a, gnf_b, came_b, xhat_ref, scale_ref, gain_ref, cot_ref, wo_ref,
    resid_ref, branch_ref, gattn_ref, ggain_ref,
):
    gnf = gnf_a[...] + came_a[...] + gnf_b[...] + came_b[...]
    rows, ggain = norm_back(gnf, xhat_ref[...], scale_ref[...], gain_ref[...])
    ggain_ref[...] = ggain
    resid = cot_ref[...].astype(F32) + rows
    resid_ref[...] = resid
    branch = resid.astype(BF)
    branch_ref[...] = branch
    gattn = mm(branch, wo_ref[...], NT).astype(BF)
    for s in range(gattn_ref.shape[0]):
        gattn_ref[s] = gattn[:, s * LANES : (s + 1) * LANES]


def branch_call(gnf, xhat, scale, gain, cot, w_output, blocks):
    rows, width = xhat.shape
    wide, low = shape_of((rows, width), F32), shape_of((rows, width), BF)
    inputs = [*gnf, xhat, scale, gain, cot, w_output]
    outs = [wide, low, shape_of((blocks, rows, width // blocks), BF), shape_of((1, width), F32)]
    return pl.pallas_call(
        branch_kernel,
        grid=(1,),
        out_shape=in_hbm(outs),
        in_specs=[whole_spec(a) for a in inputs],
        out_specs=[whole_spec(a) for a in outs],
        compiler_params=pltpu.CompilerParams(vmem_limit_bytes=20 * 2**20),
        cost_estimate=SMALL_COST,
        name="branch",
    )(*from_hbm(inputs))


GAIN_ROWS = 16


def wgrad_kernel(n_left, ids_ref, *refs):
    lefts = refs[: 2 * n_left]
    rights = refs[2 * n_left : 2 * n_left + 2]
    outs, wide_ref = refs[2 * n_left + 2 : -1], refs[-1]
    dp, core = ids_ref[0], ids_ref[1]
    level = pl.program_id(0)
    rows = lefts[0].shape[0]
    block = wide_ref.shape[0]
    at = pl.ds(pl.multiple_of((level * 2 + core) * block, block), block)
    for i in range(n_left):
        wide_ref[...] = (
            mm(lefts[2 * i][:, at], rights[0][:rows], TN)
            + mm(lefts[2 * i + 1][:, at], rights[1][:rows], TN)
        ).astype(BF)
        put_columns(outs, dp, level, i * block, wide_ref)
    extra = rights[0].shape[0] - rows
    if extra:
        takes = jnp.where((level == 0) & (core == 0), 1.0, 0.0)
        gains = rights[0][rows:].astype(F32) + rights[1][rows:].astype(F32)
        wide_ref[:extra] = (gains * takes).astype(BF)
        put_columns(outs, dp, level, n_left * block, wide_ref.at[:extra])


def wgrad_call(ids, lefts, rights, shards, levels, apart):
    n_left = len(lefts)
    flat = [array for pair in lefts for array in pair]
    width = rights[0].shape[1]
    rows, columns = flat[0].shape
    block = columns // (2 * levels)
    extra = rights[0].shape[0] - rows
    shape = (levels, n_left * block + extra, width // shards)
    outs = [shape_of(shape, BF)] * shards if apart else [shape_of((shards, *shape), BF)]
    return pl.pallas_call(
        partial(wgrad_kernel, n_left),
        grid_spec=pltpu.PrefetchScalarGridSpec(
            num_scalar_prefetch=1,
            grid=(levels,),
            in_specs=[whole_spec(array) for array in (*flat, *rights)],
            out_specs=[whole_spec(out) for out in outs],
            scratch_shapes=[pltpu.VMEM((block, width), BF)],
        ),
        out_shape=in_hbm(outs),
        compiler_params=pltpu.CompilerParams(vmem_limit_bytes=24 * 2**20),
        cost_estimate=SMALL_COST,
        name="wgrad",
    )(ids, *from_hbm([*flat, *rights]))


def tail_kernel(
    first_ref, second_ref, wq_ref, wk_ref, wv_ref, xhat_ref, scale_ref, gain_ref, resid_ref, ggain_ref,
    gh_ref, wide_ref,
):
    total = None
    for i, w_ref in enumerate((wq_ref, wk_ref, wv_ref)):
        half = first_ref.shape[1]
        lanes = slice(i * LANES, (i + 1) * LANES)
        for s in range(first_ref.shape[0]):
            upper, lower = unpack_pair(first_ref[s, :, lanes], second_ref[s, :, lanes])
            wide_ref[:half, s * LANES : (s + 1) * LANES] = upper
            wide_ref[half:, s * LANES : (s + 1) * LANES] = lower
        term = mm(wide_ref[...], w_ref[...], NT)
        total = term if total is None else total + term
    rows, ggain = norm_back(total, xhat_ref[...], scale_ref[...], gain_ref[...])
    count = wide_ref.shape[0]
    gh_ref[:count] = (resid_ref[...] + rows).astype(BF)
    at = lax.broadcasted_iota(jnp.int32, (GAIN_ROWS, ggain.shape[1]), 0)
    gains = jnp.where(at == 0, ggain, jnp.where(at == 1, ggain_ref[...], 0.0))
    gh_ref[count:] = gains.astype(BF)


def tail_call(came, weights, xhat, scale, gain, resid, ggain):
    rows, width = xhat.shape
    inputs = [*came, *weights, xhat, scale, gain, resid, ggain]
    return pl.pallas_call(
        tail_kernel,
        grid=(1,),
        out_shape=pltpu.HBM((rows + GAIN_ROWS, width), BF),
        in_specs=[whole_spec(a) for a in inputs],
        out_specs=whole_spec(shape_of((rows + GAIN_ROWS, width), BF)),
        scratch_shapes=[pltpu.VMEM((rows, width), BF)],
        compiler_params=pltpu.CompilerParams(vmem_limit_bytes=32 * 2**20),
        cost_estimate=SMALL_COST,
        name="tail",
    )(*from_hbm(inputs))


def add_low(left, right):
    return (left.astype(F32) + right.astype(F32)).astype(BF)


def pick(array, index, axis):
    return lax.dynamic_index_in_dim(array, index, axis, keepdims=False)


def after(value, *others):
    return lax.optimization_barrier((value, *others))[0]


CORE_SWAP = [(i, i ^ 1) for i in range(8)]
DP_STEPS = [[(i, i ^ k) for i in range(4)] for k in (1, 2, 3)]
Z_NEAR = [(i, i ^ 2) for i in range(8)]
Z_FAR = [(i, i ^ 4) for i in range(8)]


def core_swap(values):
    return lax.ppermute(values, "blk", CORE_SWAP)


def dp_send(shares):
    return [lax.ppermute(share, "dp", perm) for share, perm in zip(shares[1:], DP_STEPS)]


def sum_low(came, own):
    total = own.astype(F32)
    for part in came:
        total = total + part.astype(F32)
    return total.astype(BF)


def z_near(total, level):
    near, far = jnp.bitwise_xor(level, 1), jnp.bitwise_xor(level, 2)
    opposite = jnp.bitwise_xor(level, 3)
    send = jnp.stack([pick(total, near, 0), pick(total, opposite, 0)])
    keep = jnp.stack([pick(total, level, 0), pick(total, far, 0)])
    return lax.ppermute(send, "blk", Z_NEAR), keep, send


def z_far(came, keep):
    send = add_low(keep[1], came[1])
    return lax.ppermute(send, "blk", Z_FAR), add_low(keep[0], came[0]), send


def gather_near(piece):
    two = jnp.stack([piece, lax.ppermute(piece, "blk", Z_FAR)])
    four = jnp.concatenate([two, lax.ppermute(two, "blk", Z_NEAR)])
    return four, core_swap(four)


def on_device_grid(
    frames,
    skip_feats,
    w_skip,
    gain_attn,
    w_query,
    w_key,
    w_value,
    w_output,
    gain_ffn,
    w_up,
    w_down,
    cotangent,
    utt_lengths,
    padded_lengths,
):
    row_count, width = frames.shape
    blocks = lax.axis_size("blk")
    shards = lax.axis_size("dp")
    seq_len = row_count * blocks
    pair = width // blocks
    blk = lax.axis_index("blk")
    dp = lax.axis_index("dp")

    joined = jnp.concatenate([frames, skip_feats], axis=1)
    hidden = product("rc,cd->rd", joined, w_skip)
    xhat_attn, scale_attn = norm_stats(hidden)
    normed = (xhat_attn * gain_attn).astype(BF)
    normed_all = lax.all_gather(normed, "blk", axis=0, tiled=True)

    slopes = lax.dynamic_slice_in_dim(alibi_slopes(seq_len), blk * 2, 2, 0)
    coefs, qx, kx = attn_tables(utt_lengths[0], padded_lengths[0], slopes, seq_len)
    w_mine = jnp.concatenate(
        [lax.dynamic_slice_in_dim(w, blk * pair, pair, 1) for w in (w_query, w_key, w_value)],
        axis=1,
    )
    qkv = product("rd,de->re", normed_all, w_mine).astype(BF)
    attn_wide, attn_low, qb, ka, va = attn_fwd(coefs, qkv, qx, kx, blocks)

    core, level = blk % 2, blk // 2
    levels = blocks // 2
    cols = width // shards
    ids = jnp.stack([dp, core]).astype(jnp.int32)
    gain_row = gain_ffn.reshape(1, width)

    def behind(values, *others):
        return [after(v, *others) for v in values]

    def exchange(values):
        return lax.all_to_all(values, "blk", 0, 0, tiled=True)

    attn, xhat_ffn, scale_ffn, nf, residual = row_call(
        exchange(attn_low), hidden, w_output, gain_row
    )
    cot = (cotangent, core_swap(cotangent))
    joined_pairs = [(frames, core_swap(frames)), (skip_feats, core_swap(skip_feats))]
    nf = (nf, core_swap(nf))
    mix_a, mix_a_send, gnf_a, gnf_a_send, share_a = ffn_call(ids, nf, cot, w_up, w_down, shards, 0)
    sum_a = lax.psum_scatter(share_a, "dp", scatter_dimension=0)
    gnf_a_came = core_swap(gnf_a_send)
    mix_b, mix_b_send, gnf_b, gnf_b_send, share_b = ffn_call(ids, nf, cot, w_up, w_down, shards, 1)
    grad_residual, grad_branch, grad_attn, ggain_ffn = branch_call(
        (gnf_a, gnf_a_came, gnf_b, core_swap(gnf_b_send)),
        xhat_ffn,
        scale_ffn,
        gain_row,
        cotangent,
        w_output,
        blocks,
    )
    grad_attn_came = exchange(grad_attn).reshape(seq_len, pair)
    mix_send = after(mix_a_send, grad_branch) + mix_b_send
    mixed = (residual + mix_a + mix_b + core_swap(mix_send)).astype(BF)
    swapped = core_swap(jnp.stack([attn, grad_branch]))
    (share_c,) = wgrad_call(
        ids, [(attn, swapped[0])], (grad_branch, swapped[1]), shards, levels, False
    )
    n_out = share_c.shape[2]
    share_b = jnp.concatenate([share_b, share_c], axis=2)
    sum_b = lax.psum_scatter(share_b, "dp", scatter_dimension=0)

    bwd = partial(attn_bwd, coefs=coefs, o=attn_wide, qb=qb, ka=ka, va=va, blocks=blocks)
    dq_first = bwd(0, go=after(grad_attn_came, share_b))
    came_first = exchange(dq_first)
    za, keep_za, send = z_near(after(sum_a, dq_first), level)
    dq_second = bwd(1, go=after(grad_attn_came, send))

    came_second = exchange(after(dq_second, came_first))
    za_far, keep_za, send = z_far(after(za, dq_second), keep_za)
    slab = slab_call(after(normed_all, send), dq_first, dq_second)
    zb, keep_zb, send = z_near(after(sum_b, slab), level)
    piece_a = add_low(keep_za, after(za_far, send))
    whole_a = lax.all_gather(piece_a, "blk", axis=0, tiled=False)
    slab = exchange(after(slab, came_second))
    gh = tail_call(
        behind((came_first, came_second), piece_a),
        (w_query, w_key, w_value),
        xhat_attn,
        scale_attn,
        gain_attn.reshape(1, width),
        grad_residual,
        ggain_ffn,
    )
    share_d = wgrad_call(ids, joined_pairs, (gh, core_swap(gh)), shards, levels, True)
    xd = dp_send(share_d)
    zb_far, keep_zb, send = z_far(after(zb, *share_d), keep_zb)
    slab = after(slab, send).reshape(shards, 2, -1, pair)
    heads = [pick(slab, jnp.bitwise_xor(dp, k), 0) for k in range(4)]
    xh = dp_send(heads)
    grad_joined = product("rd,cd->rc", after(gh, *heads)[:row_count], w_skip)
    grad_frames = grad_joined[:, :width].astype(BF)
    grad_skip = grad_joined[:, width:].astype(BF)

    sum_d = sum_low(behind(xd, grad_joined), share_d[0])
    zd, keep_zd, send = z_near(sum_d, level)
    piece_b = add_low(keep_zb, after(zb_far, send))
    piece_h = sum_low(behind(xh, piece_b), heads[0])
    piece_h = piece_h.transpose(1, 0, 2).reshape(-1, cols)
    piece_b = jnp.concatenate([piece_b, piece_h], axis=0)
    whole_b = lax.all_gather(piece_b, "blk", axis=0, tiled=False)
    zd_far, keep_zd, send = z_far(after(zd, piece_b), keep_zd)
    piece_d = add_low(keep_zd, zd_far)
    mine, others = gather_near(piece_d)
    by_core = [jnp.where(core == 0, mine, others), jnp.where(core == 0, others, mine)]

    def take(whole, first, count):
        return whole[:, first : first + count].astype(F32)

    tile = share_a.shape[2] // 2
    downs = [take(w, 0, tile).reshape(levels, 2, tile, cols) for w in (whole_a, whole_b)]
    g_down = jnp.stack(downs, axis=1).reshape(-1, cols)
    ups = [take(w, tile, tile).reshape(levels, 2, tile, cols) for w in (whole_a, whole_b)]
    g_up = jnp.concatenate([u[:, c].reshape(-1, cols) for u in ups for c in range(2)], axis=1)
    g_output = take(whole_b, 2 * tile, n_out).reshape(-1, cols)
    n_head = width // blocks
    g_heads = [
        take(whole_b, 2 * tile + n_out + i * n_head, n_head).reshape(-1, cols) for i in range(3)
    ]
    n_skip = (share_d[0].shape[1] - GAIN_ROWS) // 2
    place = [0, 2, 1, 3]
    pieces = [
        [
            pick(by_core[c], jnp.asarray(place, jnp.int32)[jnp.bitwise_xor(level, at)], 0)
            for c in range(2)
        ]
        for at in range(levels)
    ]
    g_skip = jnp.concatenate(
        [
            pieces[at][c][i * n_skip : (i + 1) * n_skip]
            for i in range(2)
            for at in range(levels)
            for c in range(2)
        ],
        axis=0,
    ).astype(F32)
    g_gains = pieces[0][0][2 * n_skip :].astype(F32)
    return (
        mixed,
        grad_frames,
        grad_skip,
        g_skip,
        g_gains[0],
        g_heads[0],
        g_heads[1],
        g_heads[2],
        g_output,
        g_gains[1],
        g_up,
        g_down,
    )


def solution(mesh):
    shape = dict(mesh.shape)
    grid = (shape["dp"], shape["blk"])
    body = on_device_grid if grid == (4, 8) else on_device_general
    return jax.shard_map(
        body,
        mesh=mesh,
        in_specs=(
            P(("dp", "blk"), None),
            P(("dp", "blk"), None),
            P(),
            P(),
            P(),
            P(),
            P(),
            P(),
            P(),
            P(),
            P(),
            P(("dp", "blk"), None),
            P("dp", None),
            P("dp", None),
        ),
        out_specs=(
            P(("dp", "blk"), None),
            P(("dp", "blk"), None),
            P(("dp", "blk"), None),
            P(None, "dp"),
            P("dp"),
            P(None, "dp"),
            P(None, "dp"),
            P(None, "dp"),
            P(None, "dp"),
            P("dp"),
            P(None, "dp"),
            P(None, "dp"),
        ),
        check_vma=False,
    )
```

```python
from functools import partial
import math

import jax
import jax.numpy as jnp
from jax import lax
from jax.experimental import pallas as pl
from jax.experimental.pallas import tpu as pltpu
from jax.sharding import PartitionSpec as P

HEADS = 16
HEAD_DIM = 64


NEG_FILL = -1e30
NORM_EPS = 1e-05


def shifted(array, axis, by):
    size = lax.axis_size(axis)
    return lax.ppermute(array, axis, [(i, (i + by) % size) for i in range(size)])


def layer_norm(values, gain_vec):
    centred = values - jnp.mean(values, axis=-1, keepdims=True)
    variance = jnp.mean(centred * centred, axis=-1, keepdims=True)
    return centred * lax.rsqrt(variance + NORM_EPS) * gain_vec


def alibi_slopes(seq_len):
    head_rank = jnp.arange(1, HEADS + 1, dtype=jnp.float32)
    return jnp.exp2(-8.0 * head_rank / HEADS) * (256.0 / seq_len)


def utterance_tables(lengths, padded, positions):
    starts = jnp.cumsum(padded) - padded
    utt_owner = jnp.sum((positions[:, None] >= starts[None, :]).astype(jnp.int32), axis=1) - 1
    is_member = utt_owner[:, None] == jnp.arange(lengths.shape[0], dtype=jnp.int32)[None, :]
    offset_in = positions - jnp.sum(jnp.where(is_member, starts[None, :], 0), axis=1)
    is_live = offset_in < jnp.sum(jnp.where(is_member, lengths[None, :], 0), axis=1)
    return (utt_owner, is_live)


def product(form, left, right):
    return jnp.einsum(form, left, right, preferred_element_type=jnp.float32)


def on_device_general(
    frames,
    skip_feats,
    w_skip,
    gain_attn,
    w_query,
    w_key,
    w_value,
    w_output,
    gain_ffn,
    w_up,
    w_down,
    cotangent,
    utt_lengths,
    padded_lengths,
):
    row_count = frames.shape[0]
    blocks = lax.axis_size("blk")
    seq_len = row_count * blocks
    inv_root = 1.0 / math.sqrt(HEAD_DIM)
    lengths = utt_lengths[0]
    padded = padded_lengths[0]
    my_block = lax.axis_index("blk")
    row_pos = my_block * row_count + jnp.arange(row_count, dtype=jnp.int32)
    row_owner, row_live = utterance_tables(lengths, padded, row_pos)
    slopes = alibi_slopes(seq_len)
    joined = jnp.concatenate([frames, skip_feats], axis=1)
    hidden = product("rc,cd->rd", joined, w_skip)
    normed = layer_norm(hidden, gain_attn).astype(jnp.bfloat16)
    queries = (
        product("rd,de->re", normed, w_query)
        .astype(jnp.bfloat16)
        .reshape(row_count, HEADS, HEAD_DIM)
    )
    key_rows = (
        product("rd,de->re", normed, w_key).astype(jnp.bfloat16).reshape(row_count, HEADS, HEAD_DIM)
    )
    value_rows = (
        product("rd,de->re", normed, w_value)
        .astype(jnp.bfloat16)
        .reshape(row_count, HEADS, HEAD_DIM)
    )

    def score_block(keys_part, key_start):
        key_count = keys_part.shape[0]
        key_pos = key_start + jnp.arange(key_count, dtype=jnp.int32)
        key_owner, key_live = utterance_tables(lengths, padded, key_pos)
        allowed = (row_owner[:, None] == key_owner[None, :]) & key_live[None, :]
        distance = jnp.abs(row_pos[:, None] - key_pos[None, :]).astype(jnp.float32)
        scores = (
            product("qhd,khd->hqk", queries, keys_part) * inv_root
            - slopes[:, None, None] * distance[None]
        )
        return (scores, allowed)

    start_state = (
        jnp.full((HEADS, row_count), NEG_FILL, jnp.float32),
        jnp.zeros((HEADS, row_count), jnp.float32),
        jnp.zeros((row_count, HEADS, HEAD_DIM), jnp.float32),
    )
    pieces = (
        lax.all_gather(key_rows, "blk", axis=0, tiled=True),
        lax.all_gather(value_rows, "blk", axis=0, tiled=True),
    )
    key_count = pieces[0].shape[0]
    step_rows = math.gcd(key_count, 512)

    def one_block(block_index, state_now):
        running_max, running_sum, accumulated = state_now
        offset_rows = block_index * step_rows
        keys_part = lax.dynamic_slice_in_dim(pieces[0], offset_rows, step_rows, 0)
        vals_part = lax.dynamic_slice_in_dim(pieces[1], offset_rows, step_rows, 0)
        scores, allowed = score_block(keys_part, offset_rows)
        masked = jnp.where(allowed[None], scores, NEG_FILL)
        new_max = jnp.maximum(running_max, jnp.max(masked, axis=-1))
        exp_scores = jnp.where(allowed[None], jnp.exp(masked - new_max[:, :, None]), 0.0)
        rescale = jnp.exp(running_max - new_max)
        running_sum = running_sum * rescale + jnp.sum(exp_scores, axis=-1)
        accumulated = accumulated * rescale.T[:, :, None] + product(
            "hqk,khd->qhd", exp_scores.astype(jnp.bfloat16), vals_part
        )
        return (new_max, running_sum, accumulated)

    running_max, running_sum, accumulated = lax.fori_loop(
        0, key_count // step_rows, one_block, start_state
    )
    attn_full = accumulated / running_sum.T[:, :, None]
    log_total = running_max + jnp.log(running_sum)
    attn = attn_full.reshape(row_count, HEADS * HEAD_DIM).astype(jnp.bfloat16)
    residual = hidden + product("rd,de->re", attn, w_output)
    normed_ffn = layer_norm(residual, gain_ffn).astype(jnp.bfloat16)
    pre_act = product("rd,df->rf", normed_ffn, w_up)
    activ = jax.nn.gelu(pre_act, approximate=False).astype(jnp.bfloat16)
    mixed = (residual + product("rf,fd->rd", activ, w_down)).astype(jnp.bfloat16)
    grad_w_down = product("rf,rd->fd", activ, cotangent)
    grad_activ = product("rd,fd->rf", cotangent, w_down)
    gelu_out, gelu_pull = jax.vjp(partial(jax.nn.gelu, approximate=False), pre_act)
    grad_pre = gelu_pull(grad_activ)[0].astype(jnp.bfloat16)
    grad_w_up = product("rd,rf->df", normed_ffn, grad_pre)
    grad_normed_ffn = product("rf,df->rd", grad_pre, w_up)
    norm_out, norm_pull = jax.vjp(layer_norm, residual, gain_ffn)
    grad_resid_rows, grad_gain_ffn = norm_pull(grad_normed_ffn)
    grad_residual = cotangent.astype(jnp.float32) + grad_resid_rows
    grad_branch = grad_residual.astype(jnp.bfloat16)
    grad_w_output = product("rd,re->de", attn, grad_branch)
    grad_attn = (
        product("re,de->rd", grad_branch, w_output)
        .astype(jnp.bfloat16)
        .reshape(row_count, HEADS, HEAD_DIM)
    )
    delta = jnp.sum(grad_attn.astype(jnp.float32) * attn_full, axis=-1).T

    def back_turn(turn_index, state_now):
        keys_now, vals_now, grad_keys, grad_vals, grad_queries = state_now
        source = (my_block - turn_index) % blocks
        scores, allowed = score_block(keys_now, source * row_count)
        probs = jnp.where(allowed[None], jnp.exp(scores - log_total[:, :, None]), 0.0)
        grad_vals = grad_vals + product("hqk,qhd->khd", probs.astype(jnp.bfloat16), grad_attn)
        grad_probs = product("qhd,khd->hqk", grad_attn, vals_now)
        grad_scores = (probs * (grad_probs - delta[:, :, None])).astype(jnp.bfloat16)
        grad_queries = grad_queries + product("hqk,khd->qhd", grad_scores, keys_now) * inv_root
        grad_keys = grad_keys + product("hqk,qhd->khd", grad_scores, queries) * inv_root
        keys_now, vals_now = shifted((keys_now, vals_now), "blk", 1)
        grad_keys, grad_vals = (
            shifted(grad_keys.astype(jnp.bfloat16), "blk", 1).astype(grad_keys.dtype),
            shifted(grad_vals.astype(jnp.bfloat16), "blk", 1).astype(grad_vals.dtype),
        )
        return (keys_now, vals_now, grad_keys, grad_vals, grad_queries)

    zero_heads = jnp.zeros((row_count, HEADS, HEAD_DIM), jnp.float32)
    cycle_state = lax.fori_loop(
        0, blocks, back_turn, (key_rows, value_rows, zero_heads, zero_heads, zero_heads)
    )
    grad_keys_low = cycle_state[2].reshape(row_count, HEADS * HEAD_DIM).astype(jnp.bfloat16)
    grad_vals_low = cycle_state[3].reshape(row_count, HEADS * HEAD_DIM).astype(jnp.bfloat16)
    grad_query_low = cycle_state[4].reshape(row_count, HEADS * HEAD_DIM).astype(jnp.bfloat16)
    grad_w_query = product("rd,re->de", normed, grad_query_low)
    grad_w_key = product("rd,re->de", normed, grad_keys_low)
    grad_w_value = product("rd,re->de", normed, grad_vals_low)
    grad_normed = (
        product("re,de->rd", grad_query_low, w_query)
        + product("re,de->rd", grad_keys_low, w_key)
        + product("re,de->rd", grad_vals_low, w_value)
    )
    norm_first, first_pull = jax.vjp(layer_norm, hidden, gain_attn)
    grad_hidden_rows, grad_gain_attn = first_pull(grad_normed)
    grad_hidden = (grad_residual + grad_hidden_rows).astype(jnp.bfloat16)
    grad_w_skip = product("rc,rd->cd", joined, grad_hidden)
    grad_joined = product("rd,cd->rc", grad_hidden, w_skip)
    model_width = frames.shape[1]
    grad_frames = grad_joined[:, :model_width].astype(jnp.bfloat16)
    grad_skip = grad_joined[:, model_width:].astype(jnp.bfloat16)
    shares = (
        lax.psum_scatter(
            grad_w_skip.astype(jnp.bfloat16), "dp", scatter_dimension=1, tiled=True
        ).astype(jnp.float32),
        lax.psum_scatter(
            grad_w_query.astype(jnp.bfloat16), "dp", scatter_dimension=1, tiled=True
        ).astype(jnp.float32),
        lax.psum_scatter(
            grad_w_key.astype(jnp.bfloat16), "dp", scatter_dimension=1, tiled=True
        ).astype(jnp.float32),
        lax.psum_scatter(
            grad_w_value.astype(jnp.bfloat16), "dp", scatter_dimension=1, tiled=True
        ).astype(jnp.float32),
        lax.psum_scatter(
            grad_w_output.astype(jnp.bfloat16), "dp", scatter_dimension=1, tiled=True
        ).astype(jnp.float32),
        lax.psum_scatter(
            grad_w_up.astype(jnp.bfloat16), "dp", scatter_dimension=1, tiled=True
        ).astype(jnp.float32),
        lax.psum_scatter(
            grad_w_down.astype(jnp.bfloat16), "dp", scatter_dimension=1, tiled=True
        ).astype(jnp.float32),
        lax.psum_scatter(
            grad_gain_attn.astype(jnp.bfloat16), "dp", scatter_dimension=0, tiled=True
        ).astype(jnp.float32),
        lax.psum_scatter(
            grad_gain_ffn.astype(jnp.bfloat16), "dp", scatter_dimension=0, tiled=True
        ).astype(jnp.float32),
    )
    totals = (
        lax.psum(shares[0].astype(jnp.bfloat16), "blk").astype(jnp.float32),
        lax.psum(shares[1].astype(jnp.bfloat16), "blk").astype(jnp.float32),
        lax.psum(shares[2].astype(jnp.bfloat16), "blk").astype(jnp.float32),
        lax.psum(shares[3].astype(jnp.bfloat16), "blk").astype(jnp.float32),
        lax.psum(shares[4].astype(jnp.bfloat16), "blk").astype(jnp.float32),
        lax.psum(shares[5].astype(jnp.bfloat16), "blk").astype(jnp.float32),
        lax.psum(shares[6].astype(jnp.bfloat16), "blk").astype(jnp.float32),
        lax.psum(shares[7].astype(jnp.bfloat16), "blk").astype(jnp.float32),
        lax.psum(shares[8].astype(jnp.bfloat16), "blk").astype(jnp.float32),
    )
    return (
        mixed,
        grad_frames,
        grad_skip,
        totals[0],
        totals[7],
        totals[1],
        totals[2],
        totals[3],
        totals[4],
        totals[8],
        totals[5],
        totals[6],
    )


BF = jnp.bfloat16
F32 = jnp.float32
NT = (((1,), (1,)), ((), ()))
NN = (((1,), (0,)), ((), ()))
TN = (((0,), (0,)), ((), ()))
TILE = 512
LANES = 128
SMEM_SPEC = pl.BlockSpec(memory_space=pltpu.SMEM)


def shape_of(shape, dtype):
    return jax.ShapeDtypeStruct(shape, dtype)


def whole_spec(array):
    return pl.BlockSpec(array.shape, lambda *at: (0,) * len(array.shape))


def takes(micros):
    return pl.CostEstimate(flops=int(micros * 1.15e9), bytes_accessed=0, transcendentals=0)


def in_hbm(shapes):
    return [pltpu.HBM(s.shape, s.dtype) for s in shapes]


def from_hbm(arrays):
    return [pltpu.with_memory_space_constraint(a, pltpu.HBM) for a in arrays]


def mm(left, right, form):
    return lax.dot_general(left, right, form, preferred_element_type=F32)


def split3(value):
    first = value.astype(BF)
    rest = value - first.astype(F32)
    second = rest.astype(BF)
    return first, second, (rest - second.astype(F32)).astype(BF)


def tables_kernel(seg_ref, slope_ref, qx_ref, kx_ref):
    heads = qx_ref.shape[0]
    seq_len = kx_ref.shape[0]
    n_utt = seg_ref.shape[1]

    def one(b, carry):
        rows = pl.ds(pl.multiple_of(b * TILE, TILE), TILE)
        lane = lax.broadcasted_iota(jnp.int32, (TILE, LANES), 1) - HEAD_DIM
        pos = lax.broadcasted_iota(jnp.int32, (TILE, LANES), 0) + b * TILE
        coarse = (pos >> 8).astype(F32)
        fine = (pos & 255).astype(F32)
        first = jnp.zeros_like(lane)
        last = jnp.zeros_like(lane)
        last_live = jnp.zeros_like(lane)
        for u in range(n_utt):
            here = lane == 9 + u
            first = jnp.where(here, seg_ref[0, u], first)
            last = jnp.where(here, seg_ref[1, u], last)
            last_live = jnp.where(here, seg_ref[2, u], last_live)
        member = jnp.where((pos >= first) & (pos < last), 1.0, 0.0)
        is_utt = (lane >= 9) & (lane < 9 + n_utt)
        closed = jnp.where((pos >= first) & (pos < last_live), 0.0, NEG_FILL)
        digits = jnp.where((lane & 1) == 0, coarse, fine)
        keys = jnp.where(is_utt, closed, jnp.where(lane < 6, digits, 1.0))
        keys = jnp.where((lane >= 0) & (lane < 9 + n_utt), keys, 0.0)
        kx_ref[rows, :] = keys.astype(BF)
        for h in range(heads):
            for s in range(2):
                sign = 1.0 if s == 0 else -1.0
                out = jnp.where(is_utt, member, 0.0)
                for e in range(6):
                    out = jnp.where(lane == e, slope_ref[h, e] * sign, out)
                for p, piece in enumerate(split3(pos.astype(F32) * (slope_ref[h, 6] * -sign))):
                    out = jnp.where(lane == 6 + p, piece.astype(F32), out)
                qx_ref[h, s, rows, :] = out.astype(BF)
        return carry

    lax.fori_loop(0, seq_len // TILE, one, 0)


def attn_tables(lengths, padded, slopes, seq_len):
    starts = jnp.cumsum(padded) - padded
    segments = jnp.stack([starts, starts + padded, starts + lengths]).astype(jnp.int32)
    heads = slopes.shape[0]
    cols = []
    rest = slopes
    for _ in range(3):
        piece = lax.reduce_precision(rest, 8, 7)
        rest = rest - piece
        cols += [piece * 256.0, piece]
    coefs = jnp.stack(cols + [slopes], axis=1)
    outs = [shape_of((heads, 2, seq_len, LANES), BF), shape_of((seq_len, LANES), BF)]
    qx, kx = pl.pallas_call(
        tables_kernel,
        grid=(1,),
        out_shape=in_hbm(outs),
        in_specs=[SMEM_SPEC, SMEM_SPEC],
        out_specs=[whole_spec(a) for a in outs],
        compiler_params=pltpu.CompilerParams(vmem_limit_bytes=24 * 2**20),
        name="attn_tables",
    )(segments, coefs)
    return coefs, qx, kx


def head_first(tile, h):
    wide = tile.astype(F32)
    return pltpu.roll(wide, HEAD_DIM, 1) if h else wide


def ahead_of(rows, cols, axis):
    return jnp.maximum(
        lax.broadcasted_iota(jnp.int32, (rows, cols), axis)
        - lax.broadcasted_iota(jnp.int32, (rows, cols), 1 - axis),
        0,
    ).astype(F32)


def qkv_kernel(ids_ref, hidden_ref, gain_ref, wq_ref, wk_ref, wv_ref, *refs):
    xhat_ref, scale_ref, normed_ref, first_ref, second_ref, held_ref, wide_ref, sems = refs
    copies = [
        pltpu.make_async_copy(w_ref, held_ref.at[i], sems.at[i])
        for i, w_ref in enumerate((wq_ref, wk_ref, wv_ref))
    ]
    for copy in copies:
        copy.start()
    xhat, scale = norm_stats(hidden_ref[...])
    xhat_ref[...] = xhat
    scale_ref[...] = scale
    normed = (xhat * gain_ref[...]).astype(BF)
    normed_ref[...] = normed
    half = first_ref.shape[1]
    low_lane = lax.broadcasted_iota(jnp.int32, (half, LANES), 1) < HEAD_DIM
    for i, copy in enumerate(copies):
        copy.wait()
        wide_ref[...] = mm(normed, held_ref[i], NN)
        lanes = slice(i * LANES, (i + 1) * LANES)
        for s in range(first_ref.shape[0]):
            at = pair_lanes(s, ids_ref[0])
            upper, lower = wide_ref[:half, at], wide_ref[half:, at]
            first = jnp.where(low_lane, upper, pltpu.roll(lower, HEAD_DIM, 1))
            second = jnp.where(low_lane, pltpu.roll(upper, HEAD_DIM, 1), lower)
            first_ref[s, :, lanes] = first.astype(BF)
            second_ref[s, :, lanes] = second.astype(BF)


def qkv_call(ids, hidden, gain, weights, blocks):
    rows, width = hidden.shape
    low = shape_of((rows, width), BF)
    packed = shape_of((blocks, rows // 2, 3 * LANES), BF)
    outs = [shape_of((rows, width), F32), shape_of((rows, 1), F32), low, packed, packed]
    return pl.pallas_call(
        qkv_kernel,
        grid=(1,),
        out_shape=in_hbm(outs),
        in_specs=[
            SMEM_SPEC,
            whole_spec(hidden),
            whole_spec(gain),
            *[pl.BlockSpec(memory_space=pl.ANY)] * 3,
        ],
        out_specs=[whole_spec(a) for a in outs],
        scratch_shapes=[
            pltpu.VMEM((3, width, width), BF),
            pltpu.VMEM((rows, width), F32),
            pltpu.SemaphoreType.DMA((3,)),
        ],
        compiler_params=pltpu.CompilerParams(vmem_limit_bytes=24 * 2**20),
        cost_estimate=takes(6),
        name="qkv",
    )(ids, *from_hbm([hidden, gain, *weights]))


def fwd_kernel(h, coef_ref, qkv_ref, qx_ref, kx_ref, o_ref, olow_ref, qb_ref, ka_ref, va_ref, s_ref):
    half = qkv_ref.shape[1]
    seq_len = 2 * half * qkv_ref.shape[0]
    blocks = seq_len // TILE
    slope = coef_ref[h, 6]

    def prepare(b, carry):
        lane = lax.broadcasted_iota(jnp.int32, (half, LANES), 1)
        low_lane = lane < HEAD_DIM
        for side in range(2):
            rows = pl.ds(pl.multiple_of((2 * b + side) * half, half), half)
            q, k, v = (
                head_first(qkv_ref[b, :, i * LANES : (i + 1) * LANES], side) for i in range(3)
            )
            ka_ref[rows, :] = jnp.where(low_lane, k, kx_ref[rows, :].astype(F32)).astype(BF)
            va_ref[rows, :] = jnp.where(
                low_lane, v, jnp.where(lane < HEAD_DIM + 3, 1.0, 0.0)
            ).astype(BF)
            q = (q.astype(BF).astype(F32) * 0.125).astype(BF).astype(F32)
            for s in range(2):
                qb_ref[s, rows, :] = jnp.where(
                    low_lane, q, qx_ref[0, s, rows, :].astype(F32)
                ).astype(BF)
        return carry

    lax.fori_loop(0, qkv_ref.shape[0], prepare, 0)

    def one(qb, carry):
        rows = pl.ds(pl.multiple_of(qb * TILE, TILE), TILE)
        top = None
        for t in range(blocks):
            kb = lax.rem(qb + t, blocks)
            krows = pl.ds(pl.multiple_of(kb * TILE, TILE), TILE)
            side = (kb > qb).astype(jnp.int32)
            scores = mm(qb_ref[side, rows, :], ka_ref[krows, :], NT)
            if t == 0:
                scores = scores - ahead_of(TILE, TILE, 1) * (2.0 * slope)
            s_ref[:, t * TILE : (t + 1) * TILE] = scores
            part = jnp.max(scores, axis=1, keepdims=True)
            top = part if top is None else jnp.maximum(top, part)
        acc = jnp.zeros((TILE, LANES), F32)
        for t in range(blocks):
            kb = lax.rem(qb + t, blocks)
            krows = pl.ds(pl.multiple_of(kb * TILE, TILE), TILE)
            probs = jnp.exp(s_ref[:, t * TILE : (t + 1) * TILE] - top).astype(BF)
            acc = acc + mm(probs, va_ref[krows, :], NN)
        total = acc[:, HEAD_DIM : HEAD_DIM + 1]
        out = acc[:, :HEAD_DIM] / total
        o_ref[rows, :] = out
        pack_rows(olow_ref, qb, 0, out.astype(BF))
        log_total = top + jnp.log(total)
        lane = lax.broadcasted_iota(jnp.int32, (TILE, LANES), 1)
        row_pos = (qb * TILE + lax.broadcasted_iota(jnp.int32, (TILE, 1), 0)).astype(F32)
        for s in range(2):
            base = row_pos * (slope * (1.0 if s else -1.0)) - log_total
            full = qb_ref[s, rows, :].astype(F32)
            for p, piece in enumerate(split3(base)):
                full = jnp.where(lane == HEAD_DIM + 6 + p, piece.astype(F32), full)
            qb_ref[s, rows, :] = full.astype(BF)
        return carry

    lax.fori_loop(0, blocks, one, 0)


def attn_fwd(h, coefs, qkv, qx, kx):
    blocks, half, _ = qkv.shape
    seq_len = 2 * half * blocks
    outs = [
        shape_of((seq_len, HEAD_DIM), F32),
        shape_of((blocks, half, LANES), BF),
        shape_of((2, seq_len, LANES), BF),
        shape_of((seq_len, LANES), BF),
        shape_of((seq_len, LANES), BF),
    ]
    return pl.pallas_call(
        partial(fwd_kernel, h),
        grid=(1,),
        out_shape=in_hbm(outs),
        in_specs=[
            SMEM_SPEC,
            whole_spec(qkv),
            pl.BlockSpec((1, *qx.shape[1:]), lambda i: (h, 0, 0, 0)),
            whole_spec(kx),
        ],
        out_specs=[whole_spec(a) for a in outs],
        scratch_shapes=[pltpu.VMEM((TILE, seq_len), F32)],
        compiler_params=pltpu.CompilerParams(vmem_limit_bytes=36 * 2**20),
        cost_estimate=takes(14),
        name="attn_fwd",
    )(coefs, *from_hbm([qkv, qx, kx]))


def pack_rows(ref, b, part, values):
    half = ref.shape[1]
    for p in range(TILE // half):
        lane = part * LANES + (p % 2) * HEAD_DIM
        ref[b * (TILE // (2 * half)) + p // 2, :, lane : lane + HEAD_DIM] = values[
            p * half : (p + 1) * half
        ]


def unpack_pair(first, second):
    low_lane = lax.broadcasted_iota(jnp.int32, first.shape, 1) < HEAD_DIM
    first, second = first.astype(F32), second.astype(F32)
    upper = jnp.where(low_lane, first, pltpu.roll(second, HEAD_DIM, 1))
    lower = jnp.where(low_lane, pltpu.roll(first, HEAD_DIM, 1), second)
    return upper.astype(BF), lower.astype(BF)


def bwd_kernel(h, coef_ref, go_ref, o_ref, qb_ref, ka_ref, va_ref, out_ref, ga_ref, dq_ref, kt_ref):
    seq_len = go_ref.shape[0]
    blocks = seq_len // TILE
    lo = h * HEAD_DIM
    slope = coef_ref[h, 6]

    def prepare(b, carry):
        rows = pl.ds(pl.multiple_of(b * TILE, TILE), TILE)
        go = go_ref[rows, lo : lo + HEAD_DIM].astype(F32)
        delta = jnp.sum(go * o_ref[rows, :], axis=1, keepdims=True)
        lane = lax.broadcasted_iota(jnp.int32, (TILE, LANES), 1)
        full = jnp.where(lane < HEAD_DIM, head_first(go_ref[rows, :], h), 0.0)
        for p, piece in enumerate(split3(-delta)):
            full = jnp.where(lane == HEAD_DIM + p, piece.astype(F32), full)
        ga_ref[rows, :] = full.astype(BF)
        kt_ref[:, rows] = ka_ref[rows, :].astype(F32).T.astype(BF)
        dq_ref[:, rows] = jnp.zeros((HEAD_DIM, TILE), F32)
        return carry

    lax.fori_loop(0, blocks, prepare, 0)

    def one(kb, carry):
        krows = pl.ds(pl.multiple_of(kb * TILE, TILE), TILE)
        ka = ka_ref[krows, :]
        va = va_ref[krows, :]
        kt = kt_ref[:HEAD_DIM, krows]
        dv = jnp.zeros((TILE, LANES), F32)
        dk = jnp.zeros((TILE, LANES), F32)
        for t in range(blocks):
            qb = lax.rem(kb + t, blocks)
            rows = pl.ds(pl.multiple_of(qb * TILE, TILE), TILE)
            ga = ga_ref[rows, :]
            qa = qb_ref[(kb > qb).astype(jnp.int32), rows, :]
            scores = mm(ka, qa, NT)
            if t == 0:
                scores = scores - ahead_of(TILE, TILE, 0) * (2.0 * slope)
            probs = jnp.exp(scores)
            ds = (probs * mm(va, ga, NT)).astype(BF)
            dv = dv + mm(probs.astype(BF), ga, NN)
            dk = dk + mm(ds, qa, NN)
            dq_ref[:, rows] += mm(kt, ds, NN)
        pack_rows(out_ref, kb, 1, dk[:, :HEAD_DIM].astype(BF))
        pack_rows(out_ref, kb, 2, dv[:, :HEAD_DIM].astype(BF))
        return carry

    lax.fori_loop(0, blocks, one, 0)

    def finish(b, carry):
        rows = pl.ds(pl.multiple_of(b * TILE, TILE), TILE)
        pack_rows(out_ref, b, 0, (dq_ref[:, rows].T * 0.125).astype(BF))
        return carry

    lax.fori_loop(0, blocks, finish, 0)


def attn_bwd(h, coefs, go, o, qb, ka, va, blocks):
    seq_len = go.shape[0]
    half = seq_len // (2 * blocks)

    return pl.pallas_call(
        partial(bwd_kernel, h),
        grid=(1,),
        out_shape=pltpu.HBM((blocks, half, 3 * LANES), BF),
        in_specs=[SMEM_SPEC, *[whole_spec(a) for a in (go, o, qb, ka, va)]],
        out_specs=pl.BlockSpec((blocks, half, 3 * LANES), lambda i: (0, 0, 0)),
        scratch_shapes=[
            pltpu.VMEM((seq_len, LANES), BF),
            pltpu.VMEM((HEAD_DIM, seq_len), F32),
            pltpu.VMEM((LANES, seq_len), BF),
        ],
        compiler_params=pltpu.CompilerParams(vmem_limit_bytes=36 * 2**20),
        cost_estimate=takes(16),
        name="attn_bwd",
    )(coefs, *from_hbm([go, o, qb, ka, va]))


def slab_kernel(left_ref, first_ref, second_ref, out_ref, right_ref):
    @pl.when(pl.program_id(0) == 0)
    def _():
        half = first_ref.shape[1]
        for b in range(first_ref.shape[0]):
            for i in range(3):
                lanes = slice(i * LANES, (i + 1) * LANES)
                upper, lower = unpack_pair(first_ref[b, :, lanes], second_ref[b, :, lanes])
                right_ref[2 * b * half : (2 * b + 1) * half, lanes] = upper
                right_ref[(2 * b + 1) * half : (2 * b + 2) * half, lanes] = lower

    grad = mm(left_ref[...], right_ref[...], TN).astype(BF)
    block = grad.shape[0]
    for i in range(3):
        out_ref[0, i * block : (i + 1) * block] = grad[:, i * LANES : (i + 1) * LANES]


def slab_call(left, first, second):
    seq_len, width = left.shape
    blocks = first.shape[0]
    block = width // blocks
    packed = pl.BlockSpec(first.shape, lambda b: (0, 0, 0))
    return pl.pallas_call(
        slab_kernel,
        grid=(blocks,),
        out_shape=pltpu.HBM((blocks // 2, 3 * block, 2 * LANES), BF),
        in_specs=[pl.BlockSpec((seq_len, block), lambda b: (0, b)), packed, packed],
        out_specs=pl.BlockSpec((1, 3 * block, LANES), lambda b: (b // 2, 0, b % 2)),
        scratch_shapes=[pltpu.VMEM((seq_len, 3 * LANES), BF)],
        compiler_params=pltpu.CompilerParams(vmem_limit_bytes=24 * 2**20),
        cost_estimate=takes(9),
        name="slab",
    )(*from_hbm([left, first, second]))


def norm_stats(values):
    centred = values - jnp.mean(values, axis=-1, keepdims=True)
    scale = lax.rsqrt(jnp.mean(centred * centred, axis=-1, keepdims=True) + NORM_EPS)
    return centred * scale, scale


def norm_back(grad, xhat, scale, gain):
    scaled = grad * gain
    inner = jnp.mean(scaled * xhat, axis=-1, keepdims=True)
    rows = scale * (scaled - jnp.mean(scaled, axis=-1, keepdims=True) - xhat * inner)
    return rows, jnp.sum(grad * xhat, axis=0, keepdims=True)


def put_columns(outs, dp, level, first, wide_ref):
    rows = wide_ref.shape[0]
    cols = outs[0].shape[-1]
    if len(outs) == 1:
        for s in range(outs[0].shape[0]):
            outs[0][s, level, first : first + rows, :] = wide_ref[:, s * cols : (s + 1) * cols]
        return
    for k, out in enumerate(outs):
        at = pl.multiple_of(jnp.bitwise_xor(dp, k) * cols, cols)
        out[level, first : first + rows, :] = wide_ref[:, pl.ds(at, cols)]


def pair_lanes(source, dp):
    at = (jnp.bitwise_xor(source // 2, dp) * 2 + source % 2) * LANES
    return pl.ds(pl.multiple_of(at, LANES), LANES)


def row_kernel(ids_ref, first_ref, second_ref, hidden_ref, wo_ref, gain_ref, attn_ref, xhat_ref, scale_ref, nf_ref, res_ref):
    half = first_ref.shape[1]
    for s in range(first_ref.shape[0]):
        upper, lower = unpack_pair(first_ref[s], second_ref[s])
        attn_ref[:half, pair_lanes(s, ids_ref[0])] = upper
        attn_ref[half:, pair_lanes(s, ids_ref[0])] = lower
    residual = hidden_ref[...] + mm(attn_ref[...], wo_ref[...], NN)
    xhat, scale = norm_stats(residual)
    xhat_ref[...] = xhat
    scale_ref[...] = scale
    nf_ref[...] = (xhat * gain_ref[...]).astype(BF)
    res_ref[...] = residual


def row_call(ids, came, hidden, w_output, gain):
    rows, width = hidden.shape
    wide, low = shape_of((rows, width), F32), shape_of((rows, width), BF)
    inputs = [*came, hidden, w_output, gain]
    outs = [low, wide, shape_of((rows, 1), F32), low, wide]
    return pl.pallas_call(
        row_kernel,
        grid=(1,),
        out_shape=in_hbm(outs),
        in_specs=[SMEM_SPEC, *[whole_spec(a) for a in inputs]],
        out_specs=[whole_spec(a) for a in outs],
        compiler_params=pltpu.CompilerParams(vmem_limit_bytes=16 * 2**20),
        cost_estimate=takes(5),
        name="attn_rows",
    )(ids, *from_hbm(inputs))


def ffn_kernel(
    ids_ref, nf_a, nf_b, cot_a, cot_b, up_ref, down_ref, *refs
):
    sums, out, (nf_ref, cot_ref) = refs[:4], refs[4], refs[5:]
    step = pl.program_id(0)
    rows = nf_a.shape[0]

    @pl.when(step == 0)
    def _():
        nf_ref[:rows] = nf_a[...]
        nf_ref[rows:] = nf_b[...]
        cot_ref[:rows] = cot_a[...]
        cot_ref[rows:] = cot_b[...]
        for ref in sums:
            ref[...] = jnp.zeros(ref.shape, F32)

    nf = nf_ref[...]
    cot = cot_ref[...]
    up = up_ref[...]
    down = down_ref[...]
    pre = mm(nf, up, NN)
    phi = 0.5 + 0.5 * lax.erf(pre * math.sqrt(0.5))
    activ = (pre * phi).astype(BF)
    slope = phi + pre * (jnp.exp(-0.5 * pre * pre) * (1.0 / math.sqrt(2.0 * math.pi)))
    grad_pre = (slope * mm(cot, down, NT)).astype(BF)
    mix = mm(activ, down, NN)
    gnf = mm(grad_pre, up, NT)
    for i, part in enumerate((mix[:rows], mix[rows:], gnf[:rows], gnf[rows:])):
        sums[i][...] += part
    gwd = mm(activ, cot, TN).astype(BF)
    gwu = mm(nf, grad_pre, TN).astype(BF)
    shards, levels, _, cols = out.shape
    tile = gwd.shape[0]
    block = gwu.shape[0] // levels
    for s in range(shards):
        out[s, step, :tile, :] = gwd[:, s * cols : (s + 1) * cols]
    for level in range(levels):
        out[step, level, tile:, :] = gwu[level * block : (level + 1) * block]


def ffn_call(ids, nf, cot, w_up, w_down, shards, part):
    rows, width = nf[0].shape
    ff = w_up.shape[1]
    tile = ff // (shards * 4)
    inputs = [*nf, *cot]
    out_sum = shape_of((rows, width), F32)
    out_grad = shape_of((shards, shards, 2 * tile, width // shards), BF)

    def tile_at(d, ids):
        return d * 4 + part * 2 + ids[1]

    return pl.pallas_call(
        ffn_kernel,
        grid_spec=pltpu.PrefetchScalarGridSpec(
            num_scalar_prefetch=1,
            grid=(shards,),
            in_specs=[
                *[whole_spec(array) for array in inputs],
                pl.BlockSpec((width, tile), lambda d, ids: (0, tile_at(d, ids))),
                pl.BlockSpec((tile, width), lambda d, ids: (tile_at(d, ids), 0)),
            ],
            out_specs=[whole_spec(out_sum)] * 4 + [whole_spec(out_grad)],
            scratch_shapes=[
                pltpu.VMEM((2 * rows, width), BF),
                pltpu.VMEM((2 * rows, width), BF),
            ],
        ),
        out_shape=in_hbm([out_sum] * 4 + [out_grad]),
        compiler_params=pltpu.CompilerParams(vmem_limit_bytes=44 * 2**20),
        cost_estimate=takes(13),
        name="ffn",
    )(ids, *from_hbm([*inputs, w_up, w_down]))


def branch_kernel(
    ids_ref, gnf_a, came_a, gnf_b, came_b, xhat_ref, scale_ref, gain_ref, cot_ref, wo_ref,
    resid_ref, branch_ref, gattn_ref, ggain_ref, wide_ref,
):
    gnf = gnf_a[...] + came_a[...] + gnf_b[...] + came_b[...]
    rows, ggain = norm_back(gnf, xhat_ref[...], scale_ref[...], gain_ref[...])
    ggain_ref[...] = ggain
    resid = cot_ref[...].astype(F32) + rows
    resid_ref[...] = resid
    branch = resid.astype(BF)
    branch_ref[...] = branch
    wide_ref[...] = mm(branch, wo_ref[...], NT).astype(BF)
    for s in range(gattn_ref.shape[0]):
        gattn_ref[s] = wide_ref[:, pair_lanes(s, ids_ref[0])]


def branch_call(ids, gnf, xhat, scale, gain, cot, w_output, blocks):
    rows, width = xhat.shape
    wide, low = shape_of((rows, width), F32), shape_of((rows, width), BF)
    inputs = [*gnf, xhat, scale, gain, cot, w_output]
    outs = [wide, low, shape_of((blocks, rows, width // blocks), BF), shape_of((1, width), F32)]
    return pl.pallas_call(
        branch_kernel,
        grid=(1,),
        out_shape=in_hbm(outs),
        in_specs=[SMEM_SPEC, *[whole_spec(a) for a in inputs]],
        out_specs=[whole_spec(a) for a in outs],
        scratch_shapes=[pltpu.VMEM((rows, width), BF)],
        compiler_params=pltpu.CompilerParams(vmem_limit_bytes=20 * 2**20),
        cost_estimate=takes(6),
        name="branch",
    )(ids, *from_hbm(inputs))


GAIN_ROWS = 16


def wgrad_kernel(n_left, ids_ref, *refs):
    lefts = refs[: 2 * n_left]
    rights = refs[2 * n_left : 2 * n_left + 2]
    outs, wide_ref = refs[2 * n_left + 2 : -1], refs[-1]
    dp, core = ids_ref[0], ids_ref[1]
    level = pl.program_id(0)
    rows = lefts[0].shape[0]
    block = wide_ref.shape[0]
    at = pl.ds(pl.multiple_of((level * 2 + core) * block, block), block)
    for i in range(n_left):
        wide_ref[...] = (
            mm(lefts[2 * i][:, at], rights[0][:rows], TN)
            + mm(lefts[2 * i + 1][:, at], rights[1][:rows], TN)
        ).astype(BF)
        put_columns(outs, dp, level, i * block, wide_ref)
    extra = rights[0].shape[0] - rows
    if extra:
        takes = jnp.where((level == 0) & (core == 0), 1.0, 0.0)
        gains = rights[0][rows:].astype(F32) + rights[1][rows:].astype(F32)
        wide_ref[:extra] = (gains * takes).astype(BF)
        put_columns(outs, dp, level, n_left * block, wide_ref.at[:extra])


def wgrad_call(ids, lefts, rights, shards, levels, apart):
    n_left = len(lefts)
    flat = [array for pair in lefts for array in pair]
    width = rights[0].shape[1]
    rows, columns = flat[0].shape
    block = columns // (2 * levels)
    extra = rights[0].shape[0] - rows
    shape = (levels, n_left * block + extra, width // shards)
    outs = [shape_of(shape, BF)] * shards if apart else [shape_of((shards, *shape), BF)]
    return pl.pallas_call(
        partial(wgrad_kernel, n_left),
        grid_spec=pltpu.PrefetchScalarGridSpec(
            num_scalar_prefetch=1,
            grid=(levels,),
            in_specs=[whole_spec(array) for array in (*flat, *rights)],
            out_specs=[whole_spec(out) for out in outs],
            scratch_shapes=[pltpu.VMEM((block, width), BF)],
        ),
        out_shape=in_hbm(outs),
        compiler_params=pltpu.CompilerParams(vmem_limit_bytes=24 * 2**20),
        cost_estimate=takes(6),
        name="wgrad",
    )(ids, *from_hbm([*flat, *rights]))


def tail_kernel(
    ids_ref, first_ref, second_ref, wq_ref, wk_ref, wv_ref, xhat_ref, scale_ref, gain_ref, resid_ref, ggain_ref,
    gh_ref, wide_ref,
):
    total = None
    for i, w_ref in enumerate((wq_ref, wk_ref, wv_ref)):
        half = first_ref.shape[1]
        lanes = slice(i * LANES, (i + 1) * LANES)
        for s in range(first_ref.shape[0]):
            upper, lower = unpack_pair(first_ref[s, :, lanes], second_ref[s, :, lanes])
            wide_ref[:half, pair_lanes(s, ids_ref[0])] = upper
            wide_ref[half:, pair_lanes(s, ids_ref[0])] = lower
        term = mm(wide_ref[...], w_ref[...], NT)
        total = term if total is None else total + term
    rows, ggain = norm_back(total, xhat_ref[...], scale_ref[...], gain_ref[...])
    count = wide_ref.shape[0]
    gh_ref[:count] = (resid_ref[...] + rows).astype(BF)
    at = lax.broadcasted_iota(jnp.int32, (GAIN_ROWS, ggain.shape[1]), 0)
    gains = jnp.where(at == 0, ggain, jnp.where(at == 1, ggain_ref[...], 0.0))
    gh_ref[count:] = gains.astype(BF)


def tail_call(ids, came, weights, xhat, scale, gain, resid, ggain):
    rows, width = xhat.shape
    inputs = [*came, *weights, xhat, scale, gain, resid, ggain]
    return pl.pallas_call(
        tail_kernel,
        grid=(1,),
        out_shape=pltpu.HBM((rows + GAIN_ROWS, width), BF),
        in_specs=[SMEM_SPEC, *[whole_spec(a) for a in inputs]],
        out_specs=whole_spec(shape_of((rows + GAIN_ROWS, width), BF)),
        scratch_shapes=[pltpu.VMEM((rows, width), BF)],
        compiler_params=pltpu.CompilerParams(vmem_limit_bytes=32 * 2**20),
        cost_estimate=takes(8),
        name="tail",
    )(ids, *from_hbm(inputs))


def add_low(left, right):
    return (left.astype(F32) + right.astype(F32)).astype(BF)


def pick(array, index, axis):
    return lax.dynamic_index_in_dim(array, index, axis, keepdims=False)


def after(value, *others):
    return lax.optimization_barrier((value, *others))[0]


CORE_SWAP = [(i, i ^ 1) for i in range(8)]
TO_OWNERS = [(p * 8 + b, (p ^ (b // 2)) * 8 + b) for p in range(4) for b in range(8)]
DP_STEPS = [[(i, i ^ k) for i in range(4)] for k in (1, 2, 3)]
Z_NEAR = [(i, i ^ 2) for i in range(8)]
Z_FAR = [(i, i ^ 4) for i in range(8)]


def core_swap(values):
    return lax.ppermute(values, "blk", CORE_SWAP)


def dp_send(shares):
    return [lax.ppermute(share, "dp", perm) for share, perm in zip(shares[1:], DP_STEPS)]


def sum_low(came, own):
    total = own.astype(F32)
    for part in came:
        total = total + part.astype(F32)
    return total.astype(BF)


def z_near(totals, level):
    def two(first, second):
        picked = [jnp.stack([pick(t, first, 0), pick(t, second, 0)]) for t in totals]
        return jnp.concatenate(picked, axis=1) if len(picked) > 1 else picked[0]

    send = two(jnp.bitwise_xor(level, 1), jnp.bitwise_xor(level, 3))
    return lax.ppermute(send, "blk", Z_NEAR), two(level, jnp.bitwise_xor(level, 2)), send


def z_far(came, keep):
    send = add_low(keep[1], came[1])
    return lax.ppermute(send, "blk", Z_FAR), add_low(keep[0], came[0]), send


def gather_near(piece):
    two = jnp.stack([piece, lax.ppermute(piece, "blk", Z_FAR)])
    four = jnp.concatenate([two, lax.ppermute(two, "blk", Z_NEAR)])
    return four, core_swap(four)


def assemble_kernel(n_out, a_ref, b_ref, down_ref, up_ref, out_ref, *head_refs):
    core = pl.program_id(1)
    cols = a_ref.shape[2]
    tile = a_ref.shape[1] // 2
    for part, ref in enumerate((a_ref, b_ref)):
        down_ref[0, part, 0] = ref[0, :tile].astype(F32)
        at = pl.multiple_of((part * 2 + core) * cols, cols)
        up_ref[:, pl.ds(at, cols)] = ref[0, tile : 2 * tile].astype(F32)
    out_ref[...] = b_ref[0, 2 * tile : 2 * tile + n_out].astype(F32)
    half = head_refs[0].shape[0] // 2
    for i, ref in enumerate(head_refs):
        first = 2 * tile + n_out + i * half
        lanes = pl.ds(pl.multiple_of(core * LANES, LANES), LANES)
        for side in range(2):
            ref[side * half : (side + 1) * half, lanes] = b_ref[
                0, first : first + half, side * LANES : (side + 1) * LANES
            ].astype(F32)


def assemble_call(whole_a, whole_b, n_out):
    blocks, rows_a, cols = whole_a.shape
    levels, tile = blocks // 2, rows_a // 2
    outs = [
        shape_of((levels, 2, 2, tile, cols), F32),
        shape_of((levels * tile, 4 * cols), F32),
        shape_of((blocks * n_out, cols), F32),
        *[shape_of((levels * tile, cols), F32)] * 3,
    ]
    return pl.pallas_call(
        partial(assemble_kernel, n_out),
        grid=(levels, 2),
        out_shape=in_hbm(outs),
        in_specs=[
            pl.BlockSpec((1, *w.shape[1:]), lambda z, c: (z * 2 + c, 0, 0))
            for w in (whole_a, whole_b)
        ],
        out_specs=[
            pl.BlockSpec((1, 2, 1, tile, cols), lambda z, c: (z, 0, c, 0, 0)),
            pl.BlockSpec((tile, 4 * cols), lambda z, c: (z, 0)),
            pl.BlockSpec((n_out, cols), lambda z, c: (z * 2 + c, 0)),
            *[pl.BlockSpec((tile, cols), lambda z, c: (z, 0))] * 3,
        ],
        compiler_params=pltpu.CompilerParams(vmem_limit_bytes=24 * 2**20),
        cost_estimate=takes(9),
        name="assemble",
    )(*from_hbm([whole_a, whole_b]))


def skip_kernel(at_ref, own_ref, other_ref, out_ref, gain_ref):
    block = out_ref.shape[3]
    for c in range(2):

        def put(ref, c=c):
            for i in range(2):
                out_ref[i, 0, c] = ref[0, i * block : (i + 1) * block].astype(F32)

            if c == 0:

                @pl.when(pl.program_id(0) == 0)
                def _():
                    gain_ref[...] = ref[0, 2 * block :].astype(F32)

        pl.when(at_ref[1] == c)(partial(put, own_ref))
        pl.when(at_ref[1] != c)(partial(put, other_ref))


def skip_call(at, own, others):
    levels, rows, cols = own.shape
    block = (rows - GAIN_ROWS) // 2

    def place(z, at):
        k = jnp.bitwise_xor(z, at[0])
        return ((k % 2) * 2 + k // 2, 0, 0)

    outs = [shape_of((2, levels, 2, block, cols), F32), shape_of((GAIN_ROWS, cols), F32)]
    return pl.pallas_call(
        skip_kernel,
        grid_spec=pltpu.PrefetchScalarGridSpec(
            num_scalar_prefetch=1,
            grid=(levels,),
            in_specs=[pl.BlockSpec((1, rows, cols), place)] * 2,
            out_specs=[
                pl.BlockSpec((2, 1, 2, block, cols), lambda z, at: (0, z, 0, 0, 0)),
                pl.BlockSpec((GAIN_ROWS, cols), lambda z, at: (0, 0)),
            ],
        ),
        out_shape=in_hbm(outs),
        compiler_params=pltpu.CompilerParams(vmem_limit_bytes=16 * 2**20),
        cost_estimate=takes(4),
        name="skip",
    )(at, *from_hbm([own, others]))


def on_device_grid(
    frames,
    skip_feats,
    w_skip,
    gain_attn,
    w_query,
    w_key,
    w_value,
    w_output,
    gain_ffn,
    w_up,
    w_down,
    cotangent,
    utt_lengths,
    padded_lengths,
):
    row_count, width = frames.shape
    blocks = lax.axis_size("blk")
    shards = lax.axis_size("dp")
    seq_len = row_count * blocks
    pair = width // blocks
    blk = lax.axis_index("blk")
    dp = lax.axis_index("dp")

    joined = jnp.concatenate([frames, skip_feats], axis=1)
    hidden = product("rc,cd->rd", joined, w_skip)
    core, level = blk % 2, blk // 2
    ids = jnp.stack([dp, core]).astype(jnp.int32)

    def behind(values, *others):
        return [after(v, *others) for v in values]

    def exchange(values):
        return lax.all_to_all(values, "blk", 0, 0, tiled=True)

    xhat_attn, scale_attn, normed, send_first, send_second = qkv_call(
        ids, hidden, gain_attn.reshape(1, width), (w_query, w_key, w_value), blocks
    )
    qkv_first = exchange(send_first)
    mine = jnp.bitwise_xor(level, dp) * 2 + core
    slopes = lax.dynamic_slice_in_dim(alibi_slopes(seq_len), mine * 2, 2, 0)
    coefs, qx, kx = attn_tables(utt_lengths[0], padded_lengths[0], slopes, seq_len)
    qkv_second = exchange(after(send_second, qkv_first))
    o_first, low_first, *kept_first = attn_fwd(0, coefs, qkv_first, qx, kx)
    qkv_second = after(qkv_second, low_first)
    came_first = exchange(after(low_first, qkv_second))
    o_second, low_second, *kept_second = attn_fwd(1, coefs, qkv_second, qx, kx)
    came_second = exchange(after(low_second, came_first))
    normed_all = lax.all_gather(after(normed, came_second), "blk", axis=0, tiled=True)

    levels = blocks // 2
    cols = width // shards
    gain_row = gain_ffn.reshape(1, width)

    attn, xhat_ffn, scale_ffn, nf, residual = row_call(
        ids, (came_first, came_second), hidden, w_output, gain_row
    )
    cot = (cotangent, core_swap(cotangent))
    joined_pairs = [(frames, core_swap(frames)), (skip_feats, core_swap(skip_feats))]
    nf = (nf, core_swap(nf))
    mix_a, mix_a_send, gnf_a, gnf_a_send, share_a = ffn_call(ids, nf, cot, w_up, w_down, shards, 0)
    sum_a = lax.psum_scatter(share_a, "dp", scatter_dimension=0)
    gnf_a_came = core_swap(gnf_a_send)
    mix_b, mix_b_send, gnf_b, gnf_b_send, share_b = ffn_call(ids, nf, cot, w_up, w_down, shards, 1)
    grad_residual, grad_branch, grad_attn, ggain_ffn = branch_call(
        ids,
        (gnf_a, gnf_a_came, gnf_b, core_swap(gnf_b_send)),
        xhat_ffn,
        scale_ffn,
        gain_row,
        cotangent,
        w_output,
        blocks,
    )
    grad_attn = after(grad_attn, normed_all)
    grad_attn_came = exchange(grad_attn).reshape(seq_len, pair)
    mix_send = after(mix_a_send, grad_branch) + mix_b_send
    mixed = (residual + mix_a + mix_b + core_swap(mix_send)).astype(BF)
    swapped = core_swap(jnp.stack([attn, grad_branch]))
    sum_b = lax.psum_scatter(share_b, "dp", scatter_dimension=0)

    def bwd(h, go):
        o, (qb, ka, va) = ((o_first, kept_first), (o_second, kept_second))[h]
        return attn_bwd(h, coefs, go, o, qb, ka, va, blocks)

    dq_first = bwd(0, grad_attn_came)
    za, keep_za, send = z_near([after(sum_a, dq_first)], level)
    came_first = exchange(after(dq_first, send))
    dq_second = bwd(1, after(grad_attn_came, send))

    za_far, keep_za, send = z_far(after(za, dq_second), keep_za)
    slab = slab_call(after(normed_all, send), dq_first, dq_second)
    piece_a = add_low(keep_za, after(za_far, slab))
    whole_a = lax.all_gather(piece_a, "blk", axis=0, tiled=False)
    came_second = exchange(after(dq_second, came_first, piece_a))
    heads = lax.ppermute(slab, ("dp", "blk"), TO_OWNERS)
    share_c = wgrad_call(
        ids, [(attn, swapped[0])], (after(grad_branch, slab), swapped[1]), shards, levels, True
    )
    n_out = share_c[0].shape[1]
    xc = dp_send(share_c)
    gh = tail_call(
        ids,
        behind((came_first, came_second), *share_c),
        (w_query, w_key, w_value),
        xhat_attn,
        scale_attn,
        gain_attn.reshape(1, width),
        grad_residual,
        ggain_ffn,
    )
    gh_came = core_swap(gh)
    sum_c = sum_low(behind(xc, gh), share_c[0])
    zb, keep_zb, send = z_near((after(sum_b, slab), sum_c, after(heads, gh)), level)
    share_d = wgrad_call(ids, joined_pairs, (after(gh, send), gh_came), shards, levels, True)
    xd = dp_send(share_d)
    zb_far, keep_zb, send = z_far(after(zb, *share_d), keep_zb)
    grad_joined = product("rd,cd->rc", after(gh, send)[:row_count], w_skip)
    grad_frames = grad_joined[:, :width].astype(BF)
    grad_skip = grad_joined[:, width:].astype(BF)

    sum_d = sum_low(behind(xd, grad_joined), share_d[0])
    zd, keep_zd, send = z_near([sum_d], level)
    zd_far, keep_zd, send = z_far(after(zd, send), keep_zd)
    piece_b = add_low(keep_zb, after(zb_far, send))
    whole_b = lax.all_gather(piece_b, "blk", axis=0, tiled=False)
    piece_d = add_low(keep_zd, after(zd_far, piece_b))
    g_down, g_up, g_output, *g_heads = assemble_call(whole_a, whole_b, n_out)
    own, others = gather_near(piece_d)
    g_skip, g_gains = skip_call(jnp.stack([level, core]).astype(jnp.int32), own, others)
    return (
        mixed,
        grad_frames,
        grad_skip,
        g_skip.reshape(-1, cols),
        g_gains[0],
        g_heads[0],
        g_heads[1],
        g_heads[2],
        g_output,
        g_gains[1],
        g_up,
        g_down.reshape(-1, cols),
    )


def solution(mesh):
    shape = dict(mesh.shape)
    grid = (shape["dp"], shape["blk"])
    body = on_device_grid if grid == (4, 8) else on_device_general
    return jax.shard_map(
        body,
        mesh=mesh,
        in_specs=(
            P(("dp", "blk"), None),
            P(("dp", "blk"), None),
            P(),
            P(),
            P(),
            P(),
            P(),
            P(),
            P(),
            P(),
            P(),
            P(("dp", "blk"), None),
            P("dp", None),
            P("dp", None),
        ),
        out_specs=(
            P(("dp", "blk"), None),
            P(("dp", "blk"), None),
            P(("dp", "blk"), None),
            P(None, "dp"),
            P("dp"),
            P(None, "dp"),
            P(None, "dp"),
            P(None, "dp"),
            P(None, "dp"),
            P("dp"),
            P(None, "dp"),
            P(None, "dp"),
        ),
        check_vma=False,
    )
```

```python
from functools import partial
import math

import jax
import jax.numpy as jnp
from jax import lax
from jax.experimental import pallas as pl
from jax.experimental.pallas import tpu as pltpu
from jax.sharding import PartitionSpec as P

HEADS = 16
HEAD_DIM = 64


NEG_FILL = -1e30
NORM_EPS = 1e-05


def shifted(array, axis, by):
    size = lax.axis_size(axis)
    return lax.ppermute(array, axis, [(i, (i + by) % size) for i in range(size)])


def layer_norm(values, gain_vec):
    centred = values - jnp.mean(values, axis=-1, keepdims=True)
    variance = jnp.mean(centred * centred, axis=-1, keepdims=True)
    return centred * lax.rsqrt(variance + NORM_EPS) * gain_vec


def alibi_slopes(seq_len):
    head_rank = jnp.arange(1, HEADS + 1, dtype=jnp.float32)
    return jnp.exp2(-8.0 * head_rank / HEADS) * (256.0 / seq_len)


def utterance_tables(lengths, padded, positions):
    starts = jnp.cumsum(padded) - padded
    utt_owner = jnp.sum((positions[:, None] >= starts[None, :]).astype(jnp.int32), axis=1) - 1
    is_member = utt_owner[:, None] == jnp.arange(lengths.shape[0], dtype=jnp.int32)[None, :]
    offset_in = positions - jnp.sum(jnp.where(is_member, starts[None, :], 0), axis=1)
    is_live = offset_in < jnp.sum(jnp.where(is_member, lengths[None, :], 0), axis=1)
    return (utt_owner, is_live)


def product(form, left, right):
    return jnp.einsum(form, left, right, preferred_element_type=jnp.float32)


def on_device_general(
    frames,
    skip_feats,
    w_skip,
    gain_attn,
    w_query,
    w_key,
    w_value,
    w_output,
    gain_ffn,
    w_up,
    w_down,
    cotangent,
    utt_lengths,
    padded_lengths,
):
    row_count = frames.shape[0]
    blocks = lax.axis_size("blk")
    seq_len = row_count * blocks
    inv_root = 1.0 / math.sqrt(HEAD_DIM)
    lengths = utt_lengths[0]
    padded = padded_lengths[0]
    my_block = lax.axis_index("blk")
    row_pos = my_block * row_count + jnp.arange(row_count, dtype=jnp.int32)
    row_owner, row_live = utterance_tables(lengths, padded, row_pos)
    slopes = alibi_slopes(seq_len)
    joined = jnp.concatenate([frames, skip_feats], axis=1)
    hidden = product("rc,cd->rd", joined, w_skip)
    normed = layer_norm(hidden, gain_attn).astype(jnp.bfloat16)
    queries = (
        product("rd,de->re", normed, w_query)
        .astype(jnp.bfloat16)
        .reshape(row_count, HEADS, HEAD_DIM)
    )
    key_rows = (
        product("rd,de->re", normed, w_key).astype(jnp.bfloat16).reshape(row_count, HEADS, HEAD_DIM)
    )
    value_rows = (
        product("rd,de->re", normed, w_value)
        .astype(jnp.bfloat16)
        .reshape(row_count, HEADS, HEAD_DIM)
    )

    def score_block(keys_part, key_start):
        key_count = keys_part.shape[0]
        key_pos = key_start + jnp.arange(key_count, dtype=jnp.int32)
        key_owner, key_live = utterance_tables(lengths, padded, key_pos)
        allowed = (row_owner[:, None] == key_owner[None, :]) & key_live[None, :]
        distance = jnp.abs(row_pos[:, None] - key_pos[None, :]).astype(jnp.float32)
        scores = (
            product("qhd,khd->hqk", queries, keys_part) * inv_root
            - slopes[:, None, None] * distance[None]
        )
        return (scores, allowed)

    start_state = (
        jnp.full((HEADS, row_count), NEG_FILL, jnp.float32),
        jnp.zeros((HEADS, row_count), jnp.float32),
        jnp.zeros((row_count, HEADS, HEAD_DIM), jnp.float32),
    )
    pieces = (
        lax.all_gather(key_rows, "blk", axis=0, tiled=True),
        lax.all_gather(value_rows, "blk", axis=0, tiled=True),
    )
    key_count = pieces[0].shape[0]
    step_rows = math.gcd(key_count, 512)

    def one_block(block_index, state_now):
        running_max, running_sum, accumulated = state_now
        offset_rows = block_index * step_rows
        keys_part = lax.dynamic_slice_in_dim(pieces[0], offset_rows, step_rows, 0)
        vals_part = lax.dynamic_slice_in_dim(pieces[1], offset_rows, step_rows, 0)
        scores, allowed = score_block(keys_part, offset_rows)
        masked = jnp.where(allowed[None], scores, NEG_FILL)
        new_max = jnp.maximum(running_max, jnp.max(masked, axis=-1))
        exp_scores = jnp.where(allowed[None], jnp.exp(masked - new_max[:, :, None]), 0.0)
        rescale = jnp.exp(running_max - new_max)
        running_sum = running_sum * rescale + jnp.sum(exp_scores, axis=-1)
        accumulated = accumulated * rescale.T[:, :, None] + product(
            "hqk,khd->qhd", exp_scores.astype(jnp.bfloat16), vals_part
        )
        return (new_max, running_sum, accumulated)

    running_max, running_sum, accumulated = lax.fori_loop(
        0, key_count // step_rows, one_block, start_state
    )
    attn_full = accumulated / running_sum.T[:, :, None]
    log_total = running_max + jnp.log(running_sum)
    attn = attn_full.reshape(row_count, HEADS * HEAD_DIM).astype(jnp.bfloat16)
    residual = hidden + product("rd,de->re", attn, w_output)
    normed_ffn = layer_norm(residual, gain_ffn).astype(jnp.bfloat16)
    pre_act = product("rd,df->rf", normed_ffn, w_up)
    activ = jax.nn.gelu(pre_act, approximate=False).astype(jnp.bfloat16)
    mixed = (residual + product("rf,fd->rd", activ, w_down)).astype(jnp.bfloat16)
    grad_w_down = product("rf,rd->fd", activ, cotangent)
    grad_activ = product("rd,fd->rf", cotangent, w_down)
    gelu_out, gelu_pull = jax.vjp(partial(jax.nn.gelu, approximate=False), pre_act)
    grad_pre = gelu_pull(grad_activ)[0].astype(jnp.bfloat16)
    grad_w_up = product("rd,rf->df", normed_ffn, grad_pre)
    grad_normed_ffn = product("rf,df->rd", grad_pre, w_up)
    norm_out, norm_pull = jax.vjp(layer_norm, residual, gain_ffn)
    grad_resid_rows, grad_gain_ffn = norm_pull(grad_normed_ffn)
    grad_residual = cotangent.astype(jnp.float32) + grad_resid_rows
    grad_branch = grad_residual.astype(jnp.bfloat16)
    grad_w_output = product("rd,re->de", attn, grad_branch)
    grad_attn = (
        product("re,de->rd", grad_branch, w_output)
        .astype(jnp.bfloat16)
        .reshape(row_count, HEADS, HEAD_DIM)
    )
    delta = jnp.sum(grad_attn.astype(jnp.float32) * attn_full, axis=-1).T

    def back_turn(turn_index, state_now):
        keys_now, vals_now, grad_keys, grad_vals, grad_queries = state_now
        source = (my_block - turn_index) % blocks
        scores, allowed = score_block(keys_now, source * row_count)
        probs = jnp.where(allowed[None], jnp.exp(scores - log_total[:, :, None]), 0.0)
        grad_vals = grad_vals + product("hqk,qhd->khd", probs.astype(jnp.bfloat16), grad_attn)
        grad_probs = product("qhd,khd->hqk", grad_attn, vals_now)
        grad_scores = (probs * (grad_probs - delta[:, :, None])).astype(jnp.bfloat16)
        grad_queries = grad_queries + product("hqk,khd->qhd", grad_scores, keys_now) * inv_root
        grad_keys = grad_keys + product("hqk,qhd->khd", grad_scores, queries) * inv_root
        keys_now, vals_now = shifted((keys_now, vals_now), "blk", 1)
        grad_keys, grad_vals = (
            shifted(grad_keys.astype(jnp.bfloat16), "blk", 1).astype(grad_keys.dtype),
            shifted(grad_vals.astype(jnp.bfloat16), "blk", 1).astype(grad_vals.dtype),
        )
        return (keys_now, vals_now, grad_keys, grad_vals, grad_queries)

    zero_heads = jnp.zeros((row_count, HEADS, HEAD_DIM), jnp.float32)
    cycle_state = lax.fori_loop(
        0, blocks, back_turn, (key_rows, value_rows, zero_heads, zero_heads, zero_heads)
    )
    grad_keys_low = cycle_state[2].reshape(row_count, HEADS * HEAD_DIM).astype(jnp.bfloat16)
    grad_vals_low = cycle_state[3].reshape(row_count, HEADS * HEAD_DIM).astype(jnp.bfloat16)
    grad_query_low = cycle_state[4].reshape(row_count, HEADS * HEAD_DIM).astype(jnp.bfloat16)
    grad_w_query = product("rd,re->de", normed, grad_query_low)
    grad_w_key = product("rd,re->de", normed, grad_keys_low)
    grad_w_value = product("rd,re->de", normed, grad_vals_low)
    grad_normed = (
        product("re,de->rd", grad_query_low, w_query)
        + product("re,de->rd", grad_keys_low, w_key)
        + product("re,de->rd", grad_vals_low, w_value)
    )
    norm_first, first_pull = jax.vjp(layer_norm, hidden, gain_attn)
    grad_hidden_rows, grad_gain_attn = first_pull(grad_normed)
    grad_hidden = (grad_residual + grad_hidden_rows).astype(jnp.bfloat16)
    grad_w_skip = product("rc,rd->cd", joined, grad_hidden)
    grad_joined = product("rd,cd->rc", grad_hidden, w_skip)
    model_width = frames.shape[1]
    grad_frames = grad_joined[:, :model_width].astype(jnp.bfloat16)
    grad_skip = grad_joined[:, model_width:].astype(jnp.bfloat16)
    shares = (
        lax.psum_scatter(
            grad_w_skip.astype(jnp.bfloat16), "dp", scatter_dimension=1, tiled=True
        ).astype(jnp.float32),
        lax.psum_scatter(
            grad_w_query.astype(jnp.bfloat16), "dp", scatter_dimension=1, tiled=True
        ).astype(jnp.float32),
        lax.psum_scatter(
            grad_w_key.astype(jnp.bfloat16), "dp", scatter_dimension=1, tiled=True
        ).astype(jnp.float32),
        lax.psum_scatter(
            grad_w_value.astype(jnp.bfloat16), "dp", scatter_dimension=1, tiled=True
        ).astype(jnp.float32),
        lax.psum_scatter(
            grad_w_output.astype(jnp.bfloat16), "dp", scatter_dimension=1, tiled=True
        ).astype(jnp.float32),
        lax.psum_scatter(
            grad_w_up.astype(jnp.bfloat16), "dp", scatter_dimension=1, tiled=True
        ).astype(jnp.float32),
        lax.psum_scatter(
            grad_w_down.astype(jnp.bfloat16), "dp", scatter_dimension=1, tiled=True
        ).astype(jnp.float32),
        lax.psum_scatter(
            grad_gain_attn.astype(jnp.bfloat16), "dp", scatter_dimension=0, tiled=True
        ).astype(jnp.float32),
        lax.psum_scatter(
            grad_gain_ffn.astype(jnp.bfloat16), "dp", scatter_dimension=0, tiled=True
        ).astype(jnp.float32),
    )
    totals = (
        lax.psum(shares[0].astype(jnp.bfloat16), "blk").astype(jnp.float32),
        lax.psum(shares[1].astype(jnp.bfloat16), "blk").astype(jnp.float32),
        lax.psum(shares[2].astype(jnp.bfloat16), "blk").astype(jnp.float32),
        lax.psum(shares[3].astype(jnp.bfloat16), "blk").astype(jnp.float32),
        lax.psum(shares[4].astype(jnp.bfloat16), "blk").astype(jnp.float32),
        lax.psum(shares[5].astype(jnp.bfloat16), "blk").astype(jnp.float32),
        lax.psum(shares[6].astype(jnp.bfloat16), "blk").astype(jnp.float32),
        lax.psum(shares[7].astype(jnp.bfloat16), "blk").astype(jnp.float32),
        lax.psum(shares[8].astype(jnp.bfloat16), "blk").astype(jnp.float32),
    )
    return (
        mixed,
        grad_frames,
        grad_skip,
        totals[0],
        totals[7],
        totals[1],
        totals[2],
        totals[3],
        totals[4],
        totals[8],
        totals[5],
        totals[6],
    )


BF = jnp.bfloat16
F32 = jnp.float32
NT = (((1,), (1,)), ((), ()))
NN = (((1,), (0,)), ((), ()))
TN = (((0,), (0,)), ((), ()))
TILE = 512
LANES = 128
SMEM_SPEC = pl.BlockSpec(memory_space=pltpu.SMEM)


def shape_of(shape, dtype):
    return jax.ShapeDtypeStruct(shape, dtype)


def whole_spec(array):
    return pl.BlockSpec(array.shape, lambda *at: (0,) * len(array.shape))


def takes(micros):
    return pl.CostEstimate(flops=int(micros * 1.15e9), bytes_accessed=0, transcendentals=0)


def in_hbm(shapes):
    return [pltpu.HBM(s.shape, s.dtype) for s in shapes]


def from_hbm(arrays):
    return [pltpu.with_memory_space_constraint(a, pltpu.HBM) for a in arrays]


def mm(left, right, form):
    return lax.dot_general(left, right, form, preferred_element_type=F32)


def split3(value):
    first = value.astype(BF)
    rest = value - first.astype(F32)
    second = rest.astype(BF)
    return first, second, (rest - second.astype(F32)).astype(BF)


def tables_kernel(seg_ref, slope_ref, qx_ref, kx_ref):
    heads = qx_ref.shape[0]
    seq_len = kx_ref.shape[0]
    n_utt = seg_ref.shape[1]

    def one(b, carry):
        rows = pl.ds(pl.multiple_of(b * TILE, TILE), TILE)
        lane = lax.broadcasted_iota(jnp.int32, (TILE, LANES), 1) - HEAD_DIM
        pos = lax.broadcasted_iota(jnp.int32, (TILE, LANES), 0) + b * TILE
        coarse = (pos >> 8).astype(F32)
        fine = (pos & 255).astype(F32)
        first = jnp.zeros_like(lane)
        last = jnp.zeros_like(lane)
        last_live = jnp.zeros_like(lane)
        for u in range(n_utt):
            here = lane == 9 + u
            first = jnp.where(here, seg_ref[0, u], first)
            last = jnp.where(here, seg_ref[1, u], last)
            last_live = jnp.where(here, seg_ref[2, u], last_live)
        member = jnp.where((pos >= first) & (pos < last), 1.0, 0.0)
        is_utt = (lane >= 9) & (lane < 9 + n_utt)
        closed = jnp.where((pos >= first) & (pos < last_live), 0.0, NEG_FILL)
        digits = jnp.where((lane & 1) == 0, coarse, fine)
        keys = jnp.where(is_utt, closed, jnp.where(lane < 6, digits, 1.0))
        keys = jnp.where((lane >= 0) & (lane < 9 + n_utt), keys, 0.0)
        kx_ref[rows, :] = keys.astype(BF)
        for h in range(heads):
            for s in range(2):
                sign = 1.0 if s == 0 else -1.0
                out = jnp.where(is_utt, member, 0.0)
                for e in range(6):
                    out = jnp.where(lane == e, slope_ref[h, e] * sign, out)
                for p, piece in enumerate(split3(pos.astype(F32) * (slope_ref[h, 6] * -sign))):
                    out = jnp.where(lane == 6 + p, piece.astype(F32), out)
                qx_ref[h, s, rows, :] = out.astype(BF)
        return carry

    lax.fori_loop(0, seq_len // TILE, one, 0)


def attn_tables(lengths, padded, slopes, seq_len):
    starts = jnp.cumsum(padded) - padded
    segments = jnp.stack([starts, starts + padded, starts + lengths]).astype(jnp.int32)
    heads = slopes.shape[0]
    cols = []
    rest = slopes
    for _ in range(3):
        piece = lax.reduce_precision(rest, 8, 7)
        rest = rest - piece
        cols += [piece * 256.0, piece]
    coefs = jnp.stack(cols + [slopes], axis=1)
    outs = [shape_of((heads, 2, seq_len, LANES), BF), shape_of((seq_len, LANES), BF)]
    qx, kx = pl.pallas_call(
        tables_kernel,
        grid=(1,),
        out_shape=in_hbm(outs),
        in_specs=[SMEM_SPEC, SMEM_SPEC],
        out_specs=[whole_spec(a) for a in outs],
        compiler_params=pltpu.CompilerParams(vmem_limit_bytes=24 * 2**20),
        name="attn_tables",
    )(segments, coefs)
    return coefs, qx, kx


def head_first(tile, h):
    wide = tile.astype(F32)
    return pltpu.roll(wide, HEAD_DIM, 1) if h else wide


def ahead_of(rows, cols, axis):
    return jnp.maximum(
        lax.broadcasted_iota(jnp.int32, (rows, cols), axis)
        - lax.broadcasted_iota(jnp.int32, (rows, cols), 1 - axis),
        0,
    ).astype(F32)


def qkv_kernel(ids_ref, hidden_ref, gain_ref, wq_ref, wk_ref, wv_ref, *refs):
    xhat_ref, scale_ref, normed_ref, first_ref, second_ref, held_ref, wide_ref, sems = refs
    copies = [
        pltpu.make_async_copy(w_ref, held_ref.at[i], sems.at[i])
        for i, w_ref in enumerate((wq_ref, wk_ref, wv_ref))
    ]
    for copy in copies:
        copy.start()
    xhat, scale = norm_stats(hidden_ref[...])
    xhat_ref[...] = xhat
    scale_ref[...] = scale
    normed = (xhat * gain_ref[...]).astype(BF)
    normed_ref[...] = normed
    half = first_ref.shape[1]
    low_lane = lax.broadcasted_iota(jnp.int32, (half, LANES), 1) < HEAD_DIM
    for i, copy in enumerate(copies):
        copy.wait()
        wide_ref[...] = mm(normed, held_ref[i], NN)
        lanes = slice(i * LANES, (i + 1) * LANES)
        for s in range(first_ref.shape[0]):
            at = pair_lanes(s, ids_ref[0])
            upper, lower = wide_ref[:half, at], wide_ref[half:, at]
            first = jnp.where(low_lane, upper, pltpu.roll(lower, HEAD_DIM, 1))
            second = jnp.where(low_lane, pltpu.roll(upper, HEAD_DIM, 1), lower)
            first_ref[s, :, lanes] = first.astype(BF)
            second_ref[s, :, lanes] = second.astype(BF)


def qkv_call(ids, hidden, gain, weights, blocks):
    rows, width = hidden.shape
    low = shape_of((rows, width), BF)
    packed = shape_of((blocks, rows // 2, 3 * LANES), BF)
    outs = [shape_of((rows, width), F32), shape_of((rows, 1), F32), low, packed, packed]
    return pl.pallas_call(
        qkv_kernel,
        grid=(1,),
        out_shape=in_hbm(outs),
        in_specs=[
            SMEM_SPEC,
            whole_spec(hidden),
            whole_spec(gain),
            *[pl.BlockSpec(memory_space=pl.ANY)] * 3,
        ],
        out_specs=[whole_spec(a) for a in outs],
        scratch_shapes=[
            pltpu.VMEM((3, width, width), BF),
            pltpu.VMEM((rows, width), F32),
            pltpu.SemaphoreType.DMA((3,)),
        ],
        compiler_params=pltpu.CompilerParams(vmem_limit_bytes=24 * 2**20),
        cost_estimate=takes(6),
        name="qkv",
    )(ids, *from_hbm([hidden, gain, *weights]))


def fwd_kernel(h, coef_ref, qkv_ref, qx_ref, kx_ref, o_ref, olow_ref, qb_ref, ka_ref, va_ref, s_ref):
    half = qkv_ref.shape[1]
    seq_len = 2 * half * qkv_ref.shape[0]
    blocks = seq_len // TILE
    slope = coef_ref[h, 6]

    def prepare(b, carry):
        lane = lax.broadcasted_iota(jnp.int32, (half, LANES), 1)
        low_lane = lane < HEAD_DIM
        for side in range(2):
            rows = pl.ds(pl.multiple_of((2 * b + side) * half, half), half)
            q, k, v = (
                head_first(qkv_ref[b, :, i * LANES : (i + 1) * LANES], side) for i in range(3)
            )
            ka_ref[rows, :] = jnp.where(low_lane, k, kx_ref[rows, :].astype(F32)).astype(BF)
            va_ref[rows, :] = jnp.where(
                low_lane, v, jnp.where(lane < HEAD_DIM + 3, 1.0, 0.0)
            ).astype(BF)
            q = (q.astype(BF).astype(F32) * 0.125).astype(BF).astype(F32)
            for s in range(2):
                qb_ref[s, rows, :] = jnp.where(
                    low_lane, q, qx_ref[0, s, rows, :].astype(F32)
                ).astype(BF)
        return carry

    lax.fori_loop(0, qkv_ref.shape[0], prepare, 0)

    def one(qb, carry):
        rows = pl.ds(pl.multiple_of(qb * TILE, TILE), TILE)
        top = None
        for t in range(blocks):
            kb = lax.rem(qb + t, blocks)
            krows = pl.ds(pl.multiple_of(kb * TILE, TILE), TILE)
            side = (kb > qb).astype(jnp.int32)
            scores = mm(qb_ref[side, rows, :], ka_ref[krows, :], NT)
            if t == 0:
                scores = scores - ahead_of(TILE, TILE, 1) * (2.0 * slope)
            s_ref[:, t * TILE : (t + 1) * TILE] = scores
            part = jnp.max(scores, axis=1, keepdims=True)
            top = part if top is None else jnp.maximum(top, part)
        acc = jnp.zeros((TILE, LANES), F32)
        for t in range(blocks):
            kb = lax.rem(qb + t, blocks)
            krows = pl.ds(pl.multiple_of(kb * TILE, TILE), TILE)
            probs = jnp.exp(s_ref[:, t * TILE : (t + 1) * TILE] - top).astype(BF)
            acc = acc + mm(probs, va_ref[krows, :], NN)
        total = acc[:, HEAD_DIM : HEAD_DIM + 1]
        out = acc[:, :HEAD_DIM] / total
        o_ref[rows, :] = out
        pack_rows(olow_ref, qb, 0, out.astype(BF))
        log_total = top + jnp.log(total)
        lane = lax.broadcasted_iota(jnp.int32, (TILE, LANES), 1)
        row_pos = (qb * TILE + lax.broadcasted_iota(jnp.int32, (TILE, 1), 0)).astype(F32)
        for s in range(2):
            base = row_pos * (slope * (1.0 if s else -1.0)) - log_total
            full = qb_ref[s, rows, :].astype(F32)
            for p, piece in enumerate(split3(base)):
                full = jnp.where(lane == HEAD_DIM + 6 + p, piece.astype(F32), full)
            qb_ref[s, rows, :] = full.astype(BF)
        return carry

    lax.fori_loop(0, blocks, one, 0, unroll=True)


def attn_fwd(h, coefs, qkv, qx, kx):
    blocks, half, _ = qkv.shape
    seq_len = 2 * half * blocks
    outs = [
        shape_of((seq_len, HEAD_DIM), F32),
        shape_of((blocks, half, LANES), BF),
        shape_of((2, seq_len, LANES), BF),
        shape_of((seq_len, LANES), BF),
        shape_of((seq_len, LANES), BF),
    ]
    return pl.pallas_call(
        partial(fwd_kernel, h),
        grid=(1,),
        out_shape=in_hbm(outs),
        in_specs=[
            SMEM_SPEC,
            whole_spec(qkv),
            pl.BlockSpec((1, *qx.shape[1:]), lambda i: (h, 0, 0, 0)),
            whole_spec(kx),
        ],
        out_specs=[whole_spec(a) for a in outs],
        scratch_shapes=[pltpu.VMEM((TILE, seq_len), F32)],
        compiler_params=pltpu.CompilerParams(vmem_limit_bytes=36 * 2**20),
        cost_estimate=takes(11),
        name="attn_fwd",
    )(coefs, *from_hbm([qkv, qx, kx]))


def pack_rows(ref, b, part, values):
    half = ref.shape[1]
    for p in range(TILE // half):
        lane = part * LANES + (p % 2) * HEAD_DIM
        ref[b * (TILE // (2 * half)) + p // 2, :, lane : lane + HEAD_DIM] = values[
            p * half : (p + 1) * half
        ]


def unpack_pair(first, second):
    low_lane = lax.broadcasted_iota(jnp.int32, first.shape, 1) < HEAD_DIM
    first, second = first.astype(F32), second.astype(F32)
    upper = jnp.where(low_lane, first, pltpu.roll(second, HEAD_DIM, 1))
    lower = jnp.where(low_lane, pltpu.roll(first, HEAD_DIM, 1), second)
    return upper.astype(BF), lower.astype(BF)


def bwd_kernel(h, coef_ref, go_ref, o_ref, qb_ref, ka_ref, va_ref, out_ref, ga_ref, dq_ref, kt_ref):
    seq_len = go_ref.shape[0]
    blocks = seq_len // TILE
    lo = h * HEAD_DIM
    slope = coef_ref[h, 6]

    def prepare(b, carry):
        rows = pl.ds(pl.multiple_of(b * TILE, TILE), TILE)
        go = go_ref[rows, lo : lo + HEAD_DIM].astype(F32)
        delta = jnp.sum(go * o_ref[rows, :], axis=1, keepdims=True)
        lane = lax.broadcasted_iota(jnp.int32, (TILE, LANES), 1)
        full = jnp.where(lane < HEAD_DIM, head_first(go_ref[rows, :], h), 0.0)
        for p, piece in enumerate(split3(-delta)):
            full = jnp.where(lane == HEAD_DIM + p, piece.astype(F32), full)
        ga_ref[rows, :] = full.astype(BF)
        kt_ref[:, rows] = ka_ref[rows, :].astype(F32).T.astype(BF)
        dq_ref[:, rows] = jnp.zeros((HEAD_DIM, TILE), F32)
        return carry

    lax.fori_loop(0, blocks, prepare, 0)

    def one(kb, carry):
        krows = pl.ds(pl.multiple_of(kb * TILE, TILE), TILE)
        ka = ka_ref[krows, :]
        va = va_ref[krows, :]
        kt = kt_ref[:HEAD_DIM, krows]
        dv = jnp.zeros((TILE, LANES), F32)
        dk = jnp.zeros((TILE, LANES), F32)
        for t in range(blocks):
            qb = lax.rem(kb + t, blocks)
            rows = pl.ds(pl.multiple_of(qb * TILE, TILE), TILE)
            ga = ga_ref[rows, :]
            qa = qb_ref[(kb > qb).astype(jnp.int32), rows, :]
            scores = mm(ka, qa, NT)
            if t == 0:
                scores = scores - ahead_of(TILE, TILE, 0) * (2.0 * slope)
            probs = jnp.exp(scores)
            ds = (probs * mm(va, ga, NT)).astype(BF)
            dv = dv + mm(probs.astype(BF), ga, NN)
            dk = dk + mm(ds, qa, NN)
            dq_ref[:, rows] += mm(kt, ds, NN)
        pack_rows(out_ref, kb, 1, dk[:, :HEAD_DIM].astype(BF))
        pack_rows(out_ref, kb, 2, dv[:, :HEAD_DIM].astype(BF))
        return carry

    lax.fori_loop(0, blocks, one, 0)

    def finish(b, carry):
        rows = pl.ds(pl.multiple_of(b * TILE, TILE), TILE)
        pack_rows(out_ref, b, 0, (dq_ref[:, rows].T * 0.125).astype(BF))
        return carry

    lax.fori_loop(0, blocks, finish, 0)


def attn_bwd(h, coefs, go, o, qb, ka, va, blocks):
    seq_len = go.shape[0]
    half = seq_len // (2 * blocks)

    return pl.pallas_call(
        partial(bwd_kernel, h),
        grid=(1,),
        out_shape=pltpu.HBM((blocks, half, 3 * LANES), BF),
        in_specs=[SMEM_SPEC, *[whole_spec(a) for a in (go, o, qb, ka, va)]],
        out_specs=pl.BlockSpec((blocks, half, 3 * LANES), lambda i: (0, 0, 0)),
        scratch_shapes=[
            pltpu.VMEM((seq_len, LANES), BF),
            pltpu.VMEM((HEAD_DIM, seq_len), F32),
            pltpu.VMEM((LANES, seq_len), BF),
        ],
        compiler_params=pltpu.CompilerParams(vmem_limit_bytes=36 * 2**20),
        cost_estimate=takes(16),
        name="attn_bwd",
    )(coefs, *from_hbm([go, o, qb, ka, va]))


def slab_kernel(left_ref, first_ref, second_ref, out_ref, right_ref):
    @pl.when(pl.program_id(0) == 0)
    def _():
        half = first_ref.shape[1]
        for b in range(first_ref.shape[0]):
            for i in range(3):
                lanes = slice(i * LANES, (i + 1) * LANES)
                upper, lower = unpack_pair(first_ref[b, :, lanes], second_ref[b, :, lanes])
                right_ref[2 * b * half : (2 * b + 1) * half, lanes] = upper
                right_ref[(2 * b + 1) * half : (2 * b + 2) * half, lanes] = lower

    grad = mm(left_ref[...], right_ref[...], TN).astype(BF)
    side = grad.shape[0] // 2
    for i in range(3):
        for p in range(2):
            out_ref[0, i * side : (i + 1) * side, p * LANES : (p + 1) * LANES] = grad[
                p * side : (p + 1) * side, i * LANES : (i + 1) * LANES
            ]


def slab_call(left, first, second):
    seq_len, width = left.shape
    blocks = first.shape[0]
    levels = blocks // 2
    block = width // levels
    out = shape_of((levels, 3 * block // 2, 2 * LANES), BF)
    packed = pl.BlockSpec(first.shape, lambda z: (0, 0, 0))
    return pl.pallas_call(
        slab_kernel,
        grid=(levels,),
        out_shape=pltpu.HBM(out.shape, BF),
        in_specs=[pl.BlockSpec((seq_len, block), lambda z: (0, z)), packed, packed],
        out_specs=pl.BlockSpec((1, *out.shape[1:]), lambda z: (z, 0, 0)),
        scratch_shapes=[pltpu.VMEM((seq_len, 3 * LANES), BF)],
        compiler_params=pltpu.CompilerParams(vmem_limit_bytes=24 * 2**20),
        cost_estimate=takes(9),
        name="slab",
    )(*from_hbm([left, first, second]))


def norm_stats(values):
    centred = values - jnp.mean(values, axis=-1, keepdims=True)
    scale = lax.rsqrt(jnp.mean(centred * centred, axis=-1, keepdims=True) + NORM_EPS)
    return centred * scale, scale


def norm_back(grad, xhat, scale, gain):
    scaled = grad * gain
    inner = jnp.mean(scaled * xhat, axis=-1, keepdims=True)
    rows = scale * (scaled - jnp.mean(scaled, axis=-1, keepdims=True) - xhat * inner)
    return rows, jnp.sum(grad * xhat, axis=0, keepdims=True)


def put_columns(outs, dp, level, first, wide_ref):
    rows = wide_ref.shape[0]
    cols = outs[0].shape[-1]
    if len(outs) == 1:
        for s in range(outs[0].shape[0]):
            outs[0][s, level, first : first + rows, :] = wide_ref[:, s * cols : (s + 1) * cols]
        return
    for k, out in enumerate(outs):
        at = pl.multiple_of(jnp.bitwise_xor(dp, k) * cols, cols)
        out[level, first : first + rows, :] = wide_ref[:, pl.ds(at, cols)]


def pair_lanes(source, dp):
    at = (jnp.bitwise_xor(source // 2, dp) * 2 + source % 2) * LANES
    return pl.ds(pl.multiple_of(at, LANES), LANES)


def row_kernel(ids_ref, first_ref, second_ref, hidden_ref, wo_ref, gain_ref, attn_ref, xhat_ref, scale_ref, nf_ref, res_ref):
    half = first_ref.shape[1]
    for s in range(first_ref.shape[0]):
        upper, lower = unpack_pair(first_ref[s], second_ref[s])
        attn_ref[:half, pair_lanes(s, ids_ref[0])] = upper
        attn_ref[half:, pair_lanes(s, ids_ref[0])] = lower
    residual = hidden_ref[...] + mm(attn_ref[...], wo_ref[...], NN)
    xhat, scale = norm_stats(residual)
    xhat_ref[...] = xhat
    scale_ref[...] = scale
    nf_ref[...] = (xhat * gain_ref[...]).astype(BF)
    res_ref[...] = residual


def row_call(ids, came, hidden, w_output, gain):
    rows, width = hidden.shape
    wide, low = shape_of((rows, width), F32), shape_of((rows, width), BF)
    inputs = [*came, hidden, w_output, gain]
    outs = [low, wide, shape_of((rows, 1), F32), low, wide]
    return pl.pallas_call(
        row_kernel,
        grid=(1,),
        out_shape=in_hbm(outs),
        in_specs=[SMEM_SPEC, *[whole_spec(a) for a in inputs]],
        out_specs=[whole_spec(a) for a in outs],
        compiler_params=pltpu.CompilerParams(vmem_limit_bytes=16 * 2**20),
        cost_estimate=takes(5),
        name="attn_rows",
    )(ids, *from_hbm(inputs))


def ffn_kernel(
    ids_ref, nf_a, nf_b, cot_a, cot_b, up_ref, down_ref, *refs
):
    sums, out, (nf_ref, cot_ref) = refs[:4], refs[4], refs[5:]
    step = pl.program_id(0)
    rows = nf_a.shape[0]

    @pl.when(step == 0)
    def _():
        nf_ref[:rows] = nf_a[...]
        nf_ref[rows:] = nf_b[...]
        cot_ref[:rows] = cot_a[...]
        cot_ref[rows:] = cot_b[...]
        for ref in sums:
            ref[...] = jnp.zeros(ref.shape, F32)

    nf = nf_ref[...]
    cot = cot_ref[...]
    up = up_ref[...]
    down = down_ref[...]
    pre = mm(nf, up, NN)
    phi = 0.5 + 0.5 * lax.erf(pre * math.sqrt(0.5))
    activ = (pre * phi).astype(BF)
    slope = phi + pre * (jnp.exp(-0.5 * pre * pre) * (1.0 / math.sqrt(2.0 * math.pi)))
    grad_pre = (slope * mm(cot, down, NT)).astype(BF)
    mix = mm(activ, down, NN)
    gnf = mm(grad_pre, up, NT)
    for i, part in enumerate((mix[:rows], mix[rows:], gnf[:rows], gnf[rows:])):
        sums[i][...] += part
    gwd = mm(activ, cot, TN).astype(BF)
    gwu = mm(nf, grad_pre, TN).astype(BF)
    shards, levels, _, cols = out.shape
    tile = gwd.shape[0]
    block = gwu.shape[0] // levels
    for s in range(shards):
        out[s, step, :tile, :] = gwd[:, s * cols : (s + 1) * cols]
    for level in range(levels):
        out[step, level, tile:, :] = gwu[level * block : (level + 1) * block]


def ffn_call(ids, nf, cot, w_up, w_down, shards, part):
    rows, width = nf[0].shape
    ff = w_up.shape[1]
    tile = ff // (shards * 4)
    inputs = [*nf, *cot]
    out_sum = shape_of((rows, width), F32)
    out_grad = shape_of((shards, shards, 2 * tile, width // shards), BF)

    def tile_at(d, ids):
        return d * 4 + part * 2 + ids[1]

    return pl.pallas_call(
        ffn_kernel,
        grid_spec=pltpu.PrefetchScalarGridSpec(
            num_scalar_prefetch=1,
            grid=(shards,),
            in_specs=[
                *[whole_spec(array) for array in inputs],
                pl.BlockSpec((width, tile), lambda d, ids: (0, tile_at(d, ids))),
                pl.BlockSpec((tile, width), lambda d, ids: (tile_at(d, ids), 0)),
            ],
            out_specs=[whole_spec(out_sum)] * 4 + [whole_spec(out_grad)],
            scratch_shapes=[
                pltpu.VMEM((2 * rows, width), BF),
                pltpu.VMEM((2 * rows, width), BF),
            ],
        ),
        out_shape=in_hbm([out_sum] * 4 + [out_grad]),
        compiler_params=pltpu.CompilerParams(vmem_limit_bytes=44 * 2**20),
        cost_estimate=takes(13),
        name="ffn",
    )(ids, *from_hbm([*inputs, w_up, w_down]))


def branch_kernel(
    ids_ref, wo_ref, gnf_a, came_a, gnf_b, came_b, xhat_ref, scale_ref, gain_ref, cot_ref,
    resid_ref, branch_ref, gattn_ref, ggain_ref, wide_ref, held_ref, sem,
):
    copy = pltpu.make_async_copy(wo_ref, held_ref, sem)
    copy.start()
    gnf = gnf_a[...] + came_a[...] + gnf_b[...] + came_b[...]
    rows, ggain = norm_back(gnf, xhat_ref[...], scale_ref[...], gain_ref[...])
    ggain_ref[...] = ggain
    resid = cot_ref[...].astype(F32) + rows
    resid_ref[...] = resid
    branch = resid.astype(BF)
    branch_ref[...] = branch
    copy.wait()
    wide_ref[...] = mm(branch, held_ref[...], NT).astype(BF)
    for s in range(gattn_ref.shape[0]):
        gattn_ref[s] = wide_ref[:, pair_lanes(s, ids_ref[0])]


def branch_call(ids, gnf, xhat, scale, gain, cot, w_output, blocks):
    rows, width = xhat.shape
    wide, low = shape_of((rows, width), F32), shape_of((rows, width), BF)
    inputs = [*gnf, xhat, scale, gain, cot]
    outs = [wide, low, shape_of((blocks, rows, width // blocks), BF), shape_of((1, width), F32)]
    return pl.pallas_call(
        branch_kernel,
        grid=(1,),
        out_shape=in_hbm(outs),
        in_specs=[
            SMEM_SPEC,
            pl.BlockSpec(memory_space=pl.ANY),
            *[whole_spec(a) for a in inputs],
        ],
        out_specs=[whole_spec(a) for a in outs],
        scratch_shapes=[
            pltpu.VMEM((rows, width), BF),
            pltpu.VMEM((width, width), BF),
            pltpu.SemaphoreType.DMA,
        ],
        compiler_params=pltpu.CompilerParams(vmem_limit_bytes=20 * 2**20),
        cost_estimate=takes(6),
        name="branch",
    )(ids, *from_hbm([w_output, *inputs]))


GAIN_ROWS = 16


def wgrad_kernel(n_left, ids_ref, *refs):
    lefts = refs[: 2 * n_left]
    rights = refs[2 * n_left : 2 * n_left + 2]
    outs, wide_ref = refs[2 * n_left + 2 : -1], refs[-1]
    dp, core = ids_ref[0], ids_ref[1]
    level = pl.program_id(0)
    rows = lefts[0].shape[0]
    block = wide_ref.shape[0]
    at = pl.ds(pl.multiple_of((level * 2 + core) * block, block), block)
    for i in range(n_left):
        wide_ref[...] = (
            mm(lefts[2 * i][:, at], rights[0][:rows], TN)
            + mm(lefts[2 * i + 1][:, at], rights[1][:rows], TN)
        ).astype(BF)
        put_columns(outs, dp, level, i * block, wide_ref)
    extra = rights[0].shape[0] - rows
    if extra:
        takes = jnp.where((level == 0) & (core == 0), 1.0, 0.0)
        gains = rights[0][rows:].astype(F32) + rights[1][rows:].astype(F32)
        wide_ref[:extra] = (gains * takes).astype(BF)
        put_columns(outs, dp, level, n_left * block, wide_ref.at[:extra])


def wgrad_call(ids, lefts, rights, shards, levels, apart):
    n_left = len(lefts)
    flat = [array for pair in lefts for array in pair]
    width = rights[0].shape[1]
    rows, columns = flat[0].shape
    block = columns // (2 * levels)
    extra = rights[0].shape[0] - rows
    shape = (levels, n_left * block + extra, width // shards)
    outs = [shape_of(shape, BF)] * shards if apart else [shape_of((shards, *shape), BF)]
    return pl.pallas_call(
        partial(wgrad_kernel, n_left),
        grid_spec=pltpu.PrefetchScalarGridSpec(
            num_scalar_prefetch=1,
            grid=(levels,),
            in_specs=[whole_spec(array) for array in (*flat, *rights)],
            out_specs=[whole_spec(out) for out in outs],
            scratch_shapes=[pltpu.VMEM((block, width), BF)],
        ),
        out_shape=in_hbm(outs),
        compiler_params=pltpu.CompilerParams(vmem_limit_bytes=24 * 2**20),
        cost_estimate=takes(6),
        name="wgrad",
    )(ids, *from_hbm([*flat, *rights]))


def tail_kernel(
    ids_ref, wq_ref, wk_ref, wv_ref, first_ref, second_ref, xhat_ref, scale_ref, gain_ref, resid_ref, ggain_ref,
    gh_ref, wide_ref, held_ref, sems,
):
    copies = [
        pltpu.make_async_copy(w_ref, held_ref.at[i], sems.at[i])
        for i, w_ref in enumerate((wq_ref, wk_ref, wv_ref))
    ]
    for copy in copies:
        copy.start()
    total = None
    for i, copy in enumerate(copies):
        half = first_ref.shape[1]
        lanes = slice(i * LANES, (i + 1) * LANES)
        for s in range(first_ref.shape[0]):
            upper, lower = unpack_pair(first_ref[s, :, lanes], second_ref[s, :, lanes])
            wide_ref[:half, pair_lanes(s, ids_ref[0])] = upper
            wide_ref[half:, pair_lanes(s, ids_ref[0])] = lower
        copy.wait()
        term = mm(wide_ref[...], held_ref[i], NT)
        total = term if total is None else total + term
    rows, ggain = norm_back(total, xhat_ref[...], scale_ref[...], gain_ref[...])
    count = wide_ref.shape[0]
    gh_ref[:count] = (resid_ref[...] + rows).astype(BF)
    at = lax.broadcasted_iota(jnp.int32, (GAIN_ROWS, ggain.shape[1]), 0)
    gains = jnp.where(at == 0, ggain, jnp.where(at == 1, ggain_ref[...], 0.0))
    gh_ref[count:] = gains.astype(BF)


def tail_call(ids, came, weights, xhat, scale, gain, resid, ggain):
    rows, width = xhat.shape
    inputs = [*came, xhat, scale, gain, resid, ggain]
    return pl.pallas_call(
        tail_kernel,
        grid=(1,),
        out_shape=pltpu.HBM((rows + GAIN_ROWS, width), BF),
        in_specs=[
            SMEM_SPEC,
            *[pl.BlockSpec(memory_space=pl.ANY)] * 3,
            *[whole_spec(a) for a in inputs],
        ],
        out_specs=whole_spec(shape_of((rows + GAIN_ROWS, width), BF)),
        scratch_shapes=[
            pltpu.VMEM((rows, width), BF),
            pltpu.VMEM((3, width, width), BF),
            pltpu.SemaphoreType.DMA((3,)),
        ],
        compiler_params=pltpu.CompilerParams(vmem_limit_bytes=32 * 2**20),
        cost_estimate=takes(8),
        name="tail",
    )(ids, *from_hbm([*weights, *inputs]))


def add_low(left, right):
    return (left.astype(F32) + right.astype(F32)).astype(BF)


def pick(array, index, axis):
    return lax.dynamic_index_in_dim(array, index, axis, keepdims=False)


def after(value, *others):
    return lax.optimization_barrier((value, *others))[0]


CORE_SWAP = [(i, i ^ 1) for i in range(8)]
TO_OWNERS = [(p * 8 + b, (p ^ (b // 2)) * 8 + b) for p in range(4) for b in range(8)]
DP_STEPS = [[(i, i ^ k) for i in range(4)] for k in (1, 2, 3)]
Z_NEAR = [(i, i ^ 2) for i in range(8)]
Z_FAR = [(i, i ^ 4) for i in range(8)]


def core_swap(values):
    return lax.ppermute(values, "blk", CORE_SWAP)


def dp_send(shares):
    return [lax.ppermute(share, "dp", perm) for share, perm in zip(shares[1:], DP_STEPS)]


def sum_low(came, own):
    total = own.astype(F32)
    for part in came:
        total = total + part.astype(F32)
    return total.astype(BF)


def z_near(totals, level):
    def two(first, second):
        picked = [jnp.stack([pick(t, first, 0), pick(t, second, 0)]) for t in totals]
        return jnp.concatenate(picked, axis=1) if len(picked) > 1 else picked[0]

    send = two(jnp.bitwise_xor(level, 1), jnp.bitwise_xor(level, 3))
    return lax.ppermute(send, "blk", Z_NEAR), two(level, jnp.bitwise_xor(level, 2)), send


def z_far(came, keep):
    send = add_low(keep[1], came[1])
    return lax.ppermute(send, "blk", Z_FAR), add_low(keep[0], came[0]), send


def gather_near(piece):
    two = jnp.stack([piece, lax.ppermute(piece, "blk", Z_FAR)])
    four = jnp.concatenate([two, lax.ppermute(two, "blk", Z_NEAR)])
    return four, core_swap(four)


def assemble_first_kernel(a_ref, down_ref, up_ref):
    core = pl.program_id(1)
    cols = a_ref.shape[2]
    tile = a_ref.shape[1] // 2
    down_ref[0, 0, 0] = a_ref[0, :tile].astype(F32)
    up_ref[:, pl.ds(pl.multiple_of(core * cols, cols), cols)] = a_ref[0, tile:].astype(F32)


def assemble_kernel(
    n_out, at_ref, b_ref, own_ref, other_ref, down_in, up_in, down_ref, up_ref, out_ref, *refs
):
    head_refs, (skip_ref, attn_gain_ref, ffn_gain_ref) = refs[:3], refs[3:]
    core = pl.program_id(1)
    cols = b_ref.shape[2]
    tile = down_ref.shape[3]
    down_ref[0, 0, 0] = b_ref[0, :tile].astype(F32)
    up_ref[:, pl.ds(pl.multiple_of(core * cols, cols), cols)] = b_ref[0, tile : 2 * tile].astype(
        F32
    )
    out_ref[...] = b_ref[0, 2 * tile : 2 * tile + n_out].astype(F32)
    half = head_refs[0].shape[0] // 2
    for i, ref in enumerate(head_refs):
        first = 2 * tile + n_out + i * half
        lanes = pl.ds(pl.multiple_of(core * LANES, LANES), LANES)
        for side in range(2):
            ref[side * half : (side + 1) * half, lanes] = b_ref[
                0, first : first + half, side * LANES : (side + 1) * LANES
            ].astype(F32)

    def put(ref):
        block = skip_ref.shape[3]
        for i in range(2):
            skip_ref[i, 0, core] = ref[0, i * block : (i + 1) * block].astype(F32)

        @pl.when((pl.program_id(0) == 0) & (core == 0))
        def _():
            gains = ref[0, 2 * block :].astype(F32)
            attn_gain_ref[...] = gains[0:1]
            ffn_gain_ref[...] = gains[1:2]

    pl.when(at_ref[1] == core)(partial(put, own_ref))
    pl.when(at_ref[1] != core)(partial(put, other_ref))


def assemble_specs(whole, tile, part):
    cols = whole.shape[2]
    source = pl.BlockSpec((1, *whole.shape[1:]), lambda z, c, *at: (z * 2 + c, 0, 0))
    down = pl.BlockSpec((1, 1, 1, tile, cols), lambda z, c, *at: (z, part, c, 0, 0))
    up = pl.BlockSpec((tile, 2 * cols), lambda z, c, *at: (z, part))
    return source, down, up


def assemble_first(whole_a):
    blocks, rows_a, cols = whole_a.shape
    levels, tile = blocks // 2, rows_a // 2
    outs = [shape_of((levels, 2, 2, tile, cols), F32), shape_of((levels * tile, 4 * cols), F32)]
    source, down, up = assemble_specs(whole_a, tile, 0)
    return pl.pallas_call(
        assemble_first_kernel,
        grid=(levels, 2),
        out_shape=in_hbm(outs),
        in_specs=[source],
        out_specs=[down, up],
        compiler_params=pltpu.CompilerParams(vmem_limit_bytes=16 * 2**20),
        cost_estimate=takes(4),
        name="assemble_first",
    )(*from_hbm([whole_a]))


def assemble_call(at, whole_b, own, others, begun, n_out):
    blocks, _, cols = whole_b.shape
    levels, _, _, tile, _ = begun[0].shape
    rows = own.shape[1]
    block = (rows - GAIN_ROWS) // 2

    def place(z, c, at):
        k = jnp.bitwise_xor(z, at[0])
        return ((k % 2) * 2 + k // 2, 0, 0)

    outs = [
        *[shape_of(a.shape, F32) for a in begun],
        shape_of((blocks * n_out, cols), F32),
        *[shape_of((levels * tile, cols), F32)] * 3,
        shape_of((2, levels, 2, block, cols), F32),
        *[shape_of((1, cols), F32)] * 2,
    ]
    source, down, up = assemble_specs(whole_b, tile, 1)
    return pl.pallas_call(
        partial(assemble_kernel, n_out),
        grid_spec=pltpu.PrefetchScalarGridSpec(
            num_scalar_prefetch=1,
            grid=(levels, 2),
            in_specs=[
                source,
                *[pl.BlockSpec((1, rows, cols), place)] * 2,
                *[pl.BlockSpec(memory_space=pl.ANY)] * 2,
            ],
            out_specs=[
                down,
                up,
                pl.BlockSpec((n_out, cols), lambda z, c, at: (z * 2 + c, 0)),
                *[pl.BlockSpec((tile, cols), lambda z, c, at: (z, 0))] * 3,
                pl.BlockSpec((2, 1, 2, block, cols), lambda z, c, at: (0, z, 0, 0, 0)),
                *[pl.BlockSpec((1, cols), lambda z, c, at: (0, 0))] * 2,
            ],
        ),
        out_shape=in_hbm(outs),
        input_output_aliases={4: 0, 5: 1},
        compiler_params=pltpu.CompilerParams(vmem_limit_bytes=24 * 2**20),
        cost_estimate=takes(8),
        name="assemble",
    )(at, *from_hbm([whole_b, own, others, *begun]))


def on_device_grid(
    frames,
    skip_feats,
    w_skip,
    gain_attn,
    w_query,
    w_key,
    w_value,
    w_output,
    gain_ffn,
    w_up,
    w_down,
    cotangent,
    utt_lengths,
    padded_lengths,
):
    row_count, width = frames.shape
    blocks = lax.axis_size("blk")
    shards = lax.axis_size("dp")
    seq_len = row_count * blocks
    pair = width // blocks
    blk = lax.axis_index("blk")
    dp = lax.axis_index("dp")

    joined = jnp.concatenate([frames, skip_feats], axis=1)
    hidden = product("rc,cd->rd", joined, w_skip)
    core, level = blk % 2, blk // 2
    ids = jnp.stack([dp, core]).astype(jnp.int32)

    def behind(values, *others):
        return [after(v, *others) for v in values]

    def exchange(values):
        return lax.all_to_all(values, "blk", 0, 0, tiled=True)

    xhat_attn, scale_attn, normed, send_first, send_second = qkv_call(
        ids, hidden, gain_attn.reshape(1, width), (w_query, w_key, w_value), blocks
    )
    qkv_first = exchange(send_first)
    mine = jnp.bitwise_xor(level, dp) * 2 + core
    slopes = lax.dynamic_slice_in_dim(alibi_slopes(seq_len), mine * 2, 2, 0)
    coefs, qx, kx = attn_tables(utt_lengths[0], padded_lengths[0], slopes, seq_len)
    qkv_second = exchange(after(send_second, qkv_first))
    o_first, low_first, *kept_first = attn_fwd(0, coefs, qkv_first, qx, kx)
    qkv_second = after(qkv_second, low_first)
    came_first = exchange(after(low_first, qkv_second))
    o_second, low_second, *kept_second = attn_fwd(1, coefs, qkv_second, qx, kx)
    came_second = exchange(after(low_second, came_first))
    normed_all = lax.all_gather(after(normed, came_second), "blk", axis=0, tiled=True)

    levels = blocks // 2
    cols = width // shards
    gain_row = gain_ffn.reshape(1, width)

    attn, xhat_ffn, scale_ffn, nf, residual = row_call(
        ids, (came_first, came_second), hidden, w_output, gain_row
    )
    cot = (cotangent, core_swap(cotangent))
    joined_pairs = [(frames, core_swap(frames)), (skip_feats, core_swap(skip_feats))]
    nf = (nf, core_swap(nf))
    mix_a, mix_a_send, gnf_a, gnf_a_send, share_a = ffn_call(ids, nf, cot, w_up, w_down, shards, 0)
    sum_a = lax.psum_scatter(share_a, "dp", scatter_dimension=0)
    gnf_a_came = core_swap(gnf_a_send)
    mix_b, mix_b_send, gnf_b, gnf_b_send, share_b = ffn_call(ids, nf, cot, w_up, w_down, shards, 1)
    grad_residual, grad_branch, grad_attn, ggain_ffn = branch_call(
        ids,
        (gnf_a, gnf_a_came, gnf_b, core_swap(gnf_b_send)),
        xhat_ffn,
        scale_ffn,
        gain_row,
        cotangent,
        w_output,
        blocks,
    )
    grad_attn = after(grad_attn, normed_all)
    grad_attn_came = exchange(grad_attn).reshape(seq_len, pair)
    mix_send = after(mix_a_send, grad_branch) + mix_b_send
    mixed = (residual + mix_a + mix_b + core_swap(mix_send)).astype(BF)
    swapped = core_swap(jnp.stack([attn, grad_branch]))
    sum_b = lax.psum_scatter(share_b, "dp", scatter_dimension=0)

    def bwd(h, go):
        o, (qb, ka, va) = ((o_first, kept_first), (o_second, kept_second))[h]
        return attn_bwd(h, coefs, go, o, qb, ka, va, blocks)

    dq_first = bwd(0, grad_attn_came)
    za, keep_za, send = z_near([after(sum_a, dq_first)], level)
    came_first = exchange(after(dq_first, send))
    dq_second = bwd(1, after(grad_attn_came, send))

    za_far, keep_za, send = z_far(after(za, dq_second), keep_za)
    slab = slab_call(after(normed_all, send), dq_first, dq_second)
    piece_a = add_low(keep_za, after(za_far, slab))
    whole_a = lax.all_gather(piece_a, "blk", axis=0, tiled=False)
    came_second = exchange(after(dq_second, came_first, piece_a))
    heads = lax.ppermute(slab, ("dp", "blk"), TO_OWNERS)
    share_c = wgrad_call(
        ids, [(attn, swapped[0])], (after(grad_branch, slab), swapped[1]), shards, levels, True
    )
    n_out = share_c[0].shape[1]
    xc = dp_send(share_c)
    gh = tail_call(
        ids,
        behind((came_first, came_second), *share_c),
        (w_query, w_key, w_value),
        xhat_attn,
        scale_attn,
        gain_attn.reshape(1, width),
        grad_residual,
        ggain_ffn,
    )
    gh_came = core_swap(gh)
    sum_c = sum_low(behind(xc, gh), share_c[0])
    zb, keep_zb, send = z_near((after(sum_b, slab), sum_c, after(heads, gh)), level)
    share_d = wgrad_call(ids, joined_pairs, (after(gh, send), gh_came), shards, levels, True)
    xd = dp_send(share_d)
    zb_far, keep_zb, send = z_far(after(zb, *share_d), keep_zb)
    grad_joined = product("rd,cd->rc", after(gh, send)[:row_count], w_skip)
    grad_frames = grad_joined[:, :width].astype(BF)
    grad_skip = grad_joined[:, width:].astype(BF)

    begun = assemble_first(after(whole_a, grad_joined))
    sum_d = sum_low(behind(xd, *begun), share_d[0])
    zd, keep_zd, send = z_near([sum_d], level)
    zd_far, keep_zd, send = z_far(after(zd, send), keep_zd)
    piece_b = add_low(keep_zb, after(zb_far, send))
    whole_b = lax.all_gather(piece_b, "blk", axis=0, tiled=False)
    piece_d = add_low(keep_zd, after(zd_far, piece_b))
    own, others = gather_near(piece_d)
    g_down, g_up, g_output, *g_heads, g_skip, g_attn, g_ffn = assemble_call(
        jnp.stack([level, core]).astype(jnp.int32), whole_b, own, others, begun, n_out
    )
    return (
        mixed,
        grad_frames,
        grad_skip,
        g_skip.reshape(-1, cols),
        g_attn.reshape(-1),
        g_heads[0],
        g_heads[1],
        g_heads[2],
        g_output,
        g_ffn.reshape(-1),
        g_up,
        g_down.reshape(-1, cols),
    )


def solution(mesh):
    shape = dict(mesh.shape)
    grid = (shape["dp"], shape["blk"])
    body = on_device_grid if grid == (4, 8) else on_device_general
    return jax.shard_map(
        body,
        mesh=mesh,
        in_specs=(
            P(("dp", "blk"), None),
            P(("dp", "blk"), None),
            P(),
            P(),
            P(),
            P(),
            P(),
            P(),
            P(),
            P(),
            P(),
            P(("dp", "blk"), None),
            P("dp", None),
            P("dp", None),
        ),
        out_specs=(
            P(("dp", "blk"), None),
            P(("dp", "blk"), None),
            P(("dp", "blk"), None),
            P(None, "dp"),
            P("dp"),
            P(None, "dp"),
            P(None, "dp"),
            P(None, "dp"),
            P(None, "dp"),
            P("dp"),
            P(None, "dp"),
            P(None, "dp"),
        ),
        check_vma=False,
    )
```

```python
from functools import partial
import math

import jax
import jax.numpy as jnp
from jax import lax
from jax.experimental import pallas as pl
from jax.experimental.pallas import tpu as pltpu
from jax.sharding import PartitionSpec as P

HEADS = 16
HEAD_DIM = 64


NEG_FILL = -1e30
NORM_EPS = 1e-05


def shifted(array, axis, by):
    size = lax.axis_size(axis)
    return lax.ppermute(array, axis, [(i, (i + by) % size) for i in range(size)])


def layer_norm(values, gain_vec):
    centred = values - jnp.mean(values, axis=-1, keepdims=True)
    variance = jnp.mean(centred * centred, axis=-1, keepdims=True)
    return centred * lax.rsqrt(variance + NORM_EPS) * gain_vec


def alibi_slopes(seq_len):
    head_rank = jnp.arange(1, HEADS + 1, dtype=jnp.float32)
    return jnp.exp2(-8.0 * head_rank / HEADS) * (256.0 / seq_len)


def utterance_tables(lengths, padded, positions):
    starts = jnp.cumsum(padded) - padded
    utt_owner = jnp.sum((positions[:, None] >= starts[None, :]).astype(jnp.int32), axis=1) - 1
    is_member = utt_owner[:, None] == jnp.arange(lengths.shape[0], dtype=jnp.int32)[None, :]
    offset_in = positions - jnp.sum(jnp.where(is_member, starts[None, :], 0), axis=1)
    is_live = offset_in < jnp.sum(jnp.where(is_member, lengths[None, :], 0), axis=1)
    return (utt_owner, is_live)


def product(form, left, right):
    return jnp.einsum(form, left, right, preferred_element_type=jnp.float32)


def on_device_general(
    frames,
    skip_feats,
    w_skip,
    gain_attn,
    w_query,
    w_key,
    w_value,
    w_output,
    gain_ffn,
    w_up,
    w_down,
    cotangent,
    utt_lengths,
    padded_lengths,
):
    row_count = frames.shape[0]
    blocks = lax.axis_size("blk")
    seq_len = row_count * blocks
    inv_root = 1.0 / math.sqrt(HEAD_DIM)
    lengths = utt_lengths[0]
    padded = padded_lengths[0]
    my_block = lax.axis_index("blk")
    row_pos = my_block * row_count + jnp.arange(row_count, dtype=jnp.int32)
    row_owner, row_live = utterance_tables(lengths, padded, row_pos)
    slopes = alibi_slopes(seq_len)
    joined = jnp.concatenate([frames, skip_feats], axis=1)
    hidden = product("rc,cd->rd", joined, w_skip)
    normed = layer_norm(hidden, gain_attn).astype(jnp.bfloat16)
    queries = (
        product("rd,de->re", normed, w_query)
        .astype(jnp.bfloat16)
        .reshape(row_count, HEADS, HEAD_DIM)
    )
    key_rows = (
        product("rd,de->re", normed, w_key).astype(jnp.bfloat16).reshape(row_count, HEADS, HEAD_DIM)
    )
    value_rows = (
        product("rd,de->re", normed, w_value)
        .astype(jnp.bfloat16)
        .reshape(row_count, HEADS, HEAD_DIM)
    )

    def score_block(keys_part, key_start):
        key_count = keys_part.shape[0]
        key_pos = key_start + jnp.arange(key_count, dtype=jnp.int32)
        key_owner, key_live = utterance_tables(lengths, padded, key_pos)
        allowed = (row_owner[:, None] == key_owner[None, :]) & key_live[None, :]
        distance = jnp.abs(row_pos[:, None] - key_pos[None, :]).astype(jnp.float32)
        scores = (
            product("qhd,khd->hqk", queries, keys_part) * inv_root
            - slopes[:, None, None] * distance[None]
        )
        return (scores, allowed)

    start_state = (
        jnp.full((HEADS, row_count), NEG_FILL, jnp.float32),
        jnp.zeros((HEADS, row_count), jnp.float32),
        jnp.zeros((row_count, HEADS, HEAD_DIM), jnp.float32),
    )
    pieces = (
        lax.all_gather(key_rows, "blk", axis=0, tiled=True),
        lax.all_gather(value_rows, "blk", axis=0, tiled=True),
    )
    key_count = pieces[0].shape[0]
    step_rows = math.gcd(key_count, 512)

    def one_block(block_index, state_now):
        running_max, running_sum, accumulated = state_now
        offset_rows = block_index * step_rows
        keys_part = lax.dynamic_slice_in_dim(pieces[0], offset_rows, step_rows, 0)
        vals_part = lax.dynamic_slice_in_dim(pieces[1], offset_rows, step_rows, 0)
        scores, allowed = score_block(keys_part, offset_rows)
        masked = jnp.where(allowed[None], scores, NEG_FILL)
        new_max = jnp.maximum(running_max, jnp.max(masked, axis=-1))
        exp_scores = jnp.where(allowed[None], jnp.exp(masked - new_max[:, :, None]), 0.0)
        rescale = jnp.exp(running_max - new_max)
        running_sum = running_sum * rescale + jnp.sum(exp_scores, axis=-1)
        accumulated = accumulated * rescale.T[:, :, None] + product(
            "hqk,khd->qhd", exp_scores.astype(jnp.bfloat16), vals_part
        )
        return (new_max, running_sum, accumulated)

    running_max, running_sum, accumulated = lax.fori_loop(
        0, key_count // step_rows, one_block, start_state
    )
    attn_full = accumulated / running_sum.T[:, :, None]
    log_total = running_max + jnp.log(running_sum)
    attn = attn_full.reshape(row_count, HEADS * HEAD_DIM).astype(jnp.bfloat16)
    residual = hidden + product("rd,de->re", attn, w_output)
    normed_ffn = layer_norm(residual, gain_ffn).astype(jnp.bfloat16)
    pre_act = product("rd,df->rf", normed_ffn, w_up)
    activ = jax.nn.gelu(pre_act, approximate=False).astype(jnp.bfloat16)
    mixed = (residual + product("rf,fd->rd", activ, w_down)).astype(jnp.bfloat16)
    grad_w_down = product("rf,rd->fd", activ, cotangent)
    grad_activ = product("rd,fd->rf", cotangent, w_down)
    gelu_out, gelu_pull = jax.vjp(partial(jax.nn.gelu, approximate=False), pre_act)
    grad_pre = gelu_pull(grad_activ)[0].astype(jnp.bfloat16)
    grad_w_up = product("rd,rf->df", normed_ffn, grad_pre)
    grad_normed_ffn = product("rf,df->rd", grad_pre, w_up)
    norm_out, norm_pull = jax.vjp(layer_norm, residual, gain_ffn)
    grad_resid_rows, grad_gain_ffn = norm_pull(grad_normed_ffn)
    grad_residual = cotangent.astype(jnp.float32) + grad_resid_rows
    grad_branch = grad_residual.astype(jnp.bfloat16)
    grad_w_output = product("rd,re->de", attn, grad_branch)
    grad_attn = (
        product("re,de->rd", grad_branch, w_output)
        .astype(jnp.bfloat16)
        .reshape(row_count, HEADS, HEAD_DIM)
    )
    delta = jnp.sum(grad_attn.astype(jnp.float32) * attn_full, axis=-1).T

    def back_turn(turn_index, state_now):
        keys_now, vals_now, grad_keys, grad_vals, grad_queries = state_now
        source = (my_block - turn_index) % blocks
        scores, allowed = score_block(keys_now, source * row_count)
        probs = jnp.where(allowed[None], jnp.exp(scores - log_total[:, :, None]), 0.0)
        grad_vals = grad_vals + product("hqk,qhd->khd", probs.astype(jnp.bfloat16), grad_attn)
        grad_probs = product("qhd,khd->hqk", grad_attn, vals_now)
        grad_scores = (probs * (grad_probs - delta[:, :, None])).astype(jnp.bfloat16)
        grad_queries = grad_queries + product("hqk,khd->qhd", grad_scores, keys_now) * inv_root
        grad_keys = grad_keys + product("hqk,qhd->khd", grad_scores, queries) * inv_root
        keys_now, vals_now = shifted((keys_now, vals_now), "blk", 1)
        grad_keys, grad_vals = (
            shifted(grad_keys.astype(jnp.bfloat16), "blk", 1).astype(grad_keys.dtype),
            shifted(grad_vals.astype(jnp.bfloat16), "blk", 1).astype(grad_vals.dtype),
        )
        return (keys_now, vals_now, grad_keys, grad_vals, grad_queries)

    zero_heads = jnp.zeros((row_count, HEADS, HEAD_DIM), jnp.float32)
    cycle_state = lax.fori_loop(
        0, blocks, back_turn, (key_rows, value_rows, zero_heads, zero_heads, zero_heads)
    )
    grad_keys_low = cycle_state[2].reshape(row_count, HEADS * HEAD_DIM).astype(jnp.bfloat16)
    grad_vals_low = cycle_state[3].reshape(row_count, HEADS * HEAD_DIM).astype(jnp.bfloat16)
    grad_query_low = cycle_state[4].reshape(row_count, HEADS * HEAD_DIM).astype(jnp.bfloat16)
    grad_w_query = product("rd,re->de", normed, grad_query_low)
    grad_w_key = product("rd,re->de", normed, grad_keys_low)
    grad_w_value = product("rd,re->de", normed, grad_vals_low)
    grad_normed = (
        product("re,de->rd", grad_query_low, w_query)
        + product("re,de->rd", grad_keys_low, w_key)
        + product("re,de->rd", grad_vals_low, w_value)
    )
    norm_first, first_pull = jax.vjp(layer_norm, hidden, gain_attn)
    grad_hidden_rows, grad_gain_attn = first_pull(grad_normed)
    grad_hidden = (grad_residual + grad_hidden_rows).astype(jnp.bfloat16)
    grad_w_skip = product("rc,rd->cd", joined, grad_hidden)
    grad_joined = product("rd,cd->rc", grad_hidden, w_skip)
    model_width = frames.shape[1]
    grad_frames = grad_joined[:, :model_width].astype(jnp.bfloat16)
    grad_skip = grad_joined[:, model_width:].astype(jnp.bfloat16)
    shares = (
        lax.psum_scatter(
            grad_w_skip.astype(jnp.bfloat16), "dp", scatter_dimension=1, tiled=True
        ).astype(jnp.float32),
        lax.psum_scatter(
            grad_w_query.astype(jnp.bfloat16), "dp", scatter_dimension=1, tiled=True
        ).astype(jnp.float32),
        lax.psum_scatter(
            grad_w_key.astype(jnp.bfloat16), "dp", scatter_dimension=1, tiled=True
        ).astype(jnp.float32),
        lax.psum_scatter(
            grad_w_value.astype(jnp.bfloat16), "dp", scatter_dimension=1, tiled=True
        ).astype(jnp.float32),
        lax.psum_scatter(
            grad_w_output.astype(jnp.bfloat16), "dp", scatter_dimension=1, tiled=True
        ).astype(jnp.float32),
        lax.psum_scatter(
            grad_w_up.astype(jnp.bfloat16), "dp", scatter_dimension=1, tiled=True
        ).astype(jnp.float32),
        lax.psum_scatter(
            grad_w_down.astype(jnp.bfloat16), "dp", scatter_dimension=1, tiled=True
        ).astype(jnp.float32),
        lax.psum_scatter(
            grad_gain_attn.astype(jnp.bfloat16), "dp", scatter_dimension=0, tiled=True
        ).astype(jnp.float32),
        lax.psum_scatter(
            grad_gain_ffn.astype(jnp.bfloat16), "dp", scatter_dimension=0, tiled=True
        ).astype(jnp.float32),
    )
    totals = (
        lax.psum(shares[0].astype(jnp.bfloat16), "blk").astype(jnp.float32),
        lax.psum(shares[1].astype(jnp.bfloat16), "blk").astype(jnp.float32),
        lax.psum(shares[2].astype(jnp.bfloat16), "blk").astype(jnp.float32),
        lax.psum(shares[3].astype(jnp.bfloat16), "blk").astype(jnp.float32),
        lax.psum(shares[4].astype(jnp.bfloat16), "blk").astype(jnp.float32),
        lax.psum(shares[5].astype(jnp.bfloat16), "blk").astype(jnp.float32),
        lax.psum(shares[6].astype(jnp.bfloat16), "blk").astype(jnp.float32),
        lax.psum(shares[7].astype(jnp.bfloat16), "blk").astype(jnp.float32),
        lax.psum(shares[8].astype(jnp.bfloat16), "blk").astype(jnp.float32),
    )
    return (
        mixed,
        grad_frames,
        grad_skip,
        totals[0],
        totals[7],
        totals[1],
        totals[2],
        totals[3],
        totals[4],
        totals[8],
        totals[5],
        totals[6],
    )


BF = jnp.bfloat16
F32 = jnp.float32
NT = (((1,), (1,)), ((), ()))
NN = (((1,), (0,)), ((), ()))
TN = (((0,), (0,)), ((), ()))
TILE = 512
LANES = 128
SMEM_SPEC = pl.BlockSpec(memory_space=pltpu.SMEM)


def shape_of(shape, dtype):
    return jax.ShapeDtypeStruct(shape, dtype)


def whole_spec(array):
    return pl.BlockSpec(array.shape, lambda *at: (0,) * len(array.shape))


def takes(micros):
    return pl.CostEstimate(flops=int(micros * 1.15e9), bytes_accessed=0, transcendentals=0)


def in_hbm(shapes):
    return [pltpu.HBM(s.shape, s.dtype) for s in shapes]


def from_hbm(arrays):
    return [pltpu.with_memory_space_constraint(a, pltpu.HBM) for a in arrays]


def mm(left, right, form):
    return lax.dot_general(left, right, form, preferred_element_type=F32)


def split3(value):
    first = value.astype(BF)
    rest = value - first.astype(F32)
    second = rest.astype(BF)
    return first, second, (rest - second.astype(F32)).astype(BF)


def tables_kernel(seg_ref, slope_ref, qx_ref, kx_ref):
    heads = qx_ref.shape[0]
    seq_len = kx_ref.shape[0]
    n_utt = seg_ref.shape[1]

    def one(b, carry):
        rows = pl.ds(pl.multiple_of(b * TILE, TILE), TILE)
        lane = lax.broadcasted_iota(jnp.int32, (TILE, LANES), 1) - HEAD_DIM
        pos = lax.broadcasted_iota(jnp.int32, (TILE, LANES), 0) + b * TILE
        coarse = (pos >> 8).astype(F32)
        fine = (pos & 255).astype(F32)
        first = jnp.zeros_like(lane)
        last = jnp.zeros_like(lane)
        last_live = jnp.zeros_like(lane)
        for u in range(n_utt):
            here = lane == 9 + u
            first = jnp.where(here, seg_ref[0, u], first)
            last = jnp.where(here, seg_ref[1, u], last)
            last_live = jnp.where(here, seg_ref[2, u], last_live)
        member = jnp.where((pos >= first) & (pos < last), 1.0, 0.0)
        is_utt = (lane >= 9) & (lane < 9 + n_utt)
        closed = jnp.where((pos >= first) & (pos < last_live), 0.0, NEG_FILL)
        digits = jnp.where((lane & 1) == 0, coarse, fine)
        keys = jnp.where(is_utt, closed, jnp.where(lane < 6, digits, 1.0))
        keys = jnp.where((lane >= 0) & (lane < 9 + n_utt), keys, 0.0)
        kx_ref[rows, :] = keys.astype(BF)
        for h in range(heads):
            for s in range(2):
                sign = 1.0 if s == 0 else -1.0
                out = jnp.where(is_utt, member, 0.0)
                for e in range(6):
                    out = jnp.where(lane == e, slope_ref[h, e] * sign, out)
                for p, piece in enumerate(split3(pos.astype(F32) * (slope_ref[h, 6] * -sign))):
                    out = jnp.where(lane == 6 + p, piece.astype(F32), out)
                qx_ref[h, s, rows, :] = out.astype(BF)
        return carry

    lax.fori_loop(0, seq_len // TILE, one, 0)


def attn_tables(lengths, padded, slopes, seq_len):
    starts = jnp.cumsum(padded) - padded
    segments = jnp.stack([starts, starts + padded, starts + lengths]).astype(jnp.int32)
    heads = slopes.shape[0]
    cols = []
    rest = slopes
    for _ in range(3):
        piece = lax.reduce_precision(rest, 8, 7)
        rest = rest - piece
        cols += [piece * 256.0, piece]
    coefs = jnp.stack(cols + [slopes], axis=1)
    outs = [shape_of((heads, 2, seq_len, LANES), BF), shape_of((seq_len, LANES), BF)]
    qx, kx = pl.pallas_call(
        tables_kernel,
        grid=(1,),
        out_shape=in_hbm(outs),
        in_specs=[SMEM_SPEC, SMEM_SPEC],
        out_specs=[whole_spec(a) for a in outs],
        compiler_params=pltpu.CompilerParams(vmem_limit_bytes=24 * 2**20),
        name="attn_tables",
    )(segments, coefs)
    return coefs, qx, kx


def head_first(tile, h):
    wide = tile.astype(F32)
    return pltpu.roll(wide, HEAD_DIM, 1) if h else wide


def ahead_of(rows, cols, axis):
    return jnp.maximum(
        lax.broadcasted_iota(jnp.int32, (rows, cols), axis)
        - lax.broadcasted_iota(jnp.int32, (rows, cols), 1 - axis),
        0,
    ).astype(F32)


def qkv_kernel(ids_ref, hidden_ref, gain_ref, wq_ref, wk_ref, wv_ref, *refs):
    xhat_ref, scale_ref, normed_ref, first_ref, second_ref, held_ref, wide_ref, sems = refs
    copies = [
        pltpu.make_async_copy(w_ref, held_ref.at[i], sems.at[i])
        for i, w_ref in enumerate((wq_ref, wk_ref, wv_ref))
    ]
    for copy in copies:
        copy.start()
    xhat, scale = norm_stats(hidden_ref[...])
    xhat_ref[...] = xhat
    scale_ref[...] = scale
    normed = (xhat * gain_ref[...]).astype(BF)
    normed_ref[...] = normed
    half = first_ref.shape[1]
    low_lane = lax.broadcasted_iota(jnp.int32, (half, LANES), 1) < HEAD_DIM
    for i, copy in enumerate(copies):
        copy.wait()
        wide_ref[...] = mm(normed, held_ref[i], NN)
        lanes = slice(i * LANES, (i + 1) * LANES)
        for s in range(first_ref.shape[0]):
            at = pair_lanes(s, ids_ref[0])
            upper, lower = wide_ref[:half, at], wide_ref[half:, at]
            first = jnp.where(low_lane, upper, pltpu.roll(lower, HEAD_DIM, 1))
            second = jnp.where(low_lane, pltpu.roll(upper, HEAD_DIM, 1), lower)
            first_ref[s, :, lanes] = first.astype(BF)
            second_ref[s, :, lanes] = second.astype(BF)


def qkv_call(ids, hidden, gain, weights, blocks):
    rows, width = hidden.shape
    low = shape_of((rows, width), BF)
    packed = shape_of((blocks, rows // 2, 3 * LANES), BF)
    outs = [shape_of((rows, width), F32), shape_of((rows, 1), F32), low, packed, packed]
    return pl.pallas_call(
        qkv_kernel,
        grid=(1,),
        out_shape=in_hbm(outs),
        in_specs=[
            SMEM_SPEC,
            whole_spec(hidden),
            whole_spec(gain),
            *[pl.BlockSpec(memory_space=pl.ANY)] * 3,
        ],
        out_specs=[whole_spec(a) for a in outs],
        scratch_shapes=[
            pltpu.VMEM((3, width, width), BF),
            pltpu.VMEM((rows, width), F32),
            pltpu.SemaphoreType.DMA((3,)),
        ],
        compiler_params=pltpu.CompilerParams(vmem_limit_bytes=24 * 2**20),
        cost_estimate=takes(6),
        name="qkv",
    )(ids, *from_hbm([hidden, gain, *weights]))


def fwd_kernel(h, coef_ref, qkv_ref, qx_ref, kx_ref, o_ref, olow_ref, qb_ref, ka_ref, va_ref, s_ref):
    half = qkv_ref.shape[1]
    seq_len = 2 * half * qkv_ref.shape[0]
    blocks = seq_len // TILE
    slope = coef_ref[h, 6]

    def prepare(b, carry):
        lane = lax.broadcasted_iota(jnp.int32, (half, LANES), 1)
        low_lane = lane < HEAD_DIM
        for side in range(2):
            rows = pl.ds(pl.multiple_of((2 * b + side) * half, half), half)
            q, k, v = (
                head_first(qkv_ref[b, :, i * LANES : (i + 1) * LANES], side) for i in range(3)
            )
            ka_ref[rows, :] = jnp.where(low_lane, k, kx_ref[rows, :].astype(F32)).astype(BF)
            va_ref[rows, :] = jnp.where(
                low_lane, v, jnp.where(lane < HEAD_DIM + 3, 1.0, 0.0)
            ).astype(BF)
            q = (q.astype(BF).astype(F32) * 0.125).astype(BF).astype(F32)
            for s in range(2):
                qb_ref[s, rows, :] = jnp.where(
                    low_lane, q, qx_ref[0, s, rows, :].astype(F32)
                ).astype(BF)
        return carry

    lax.fori_loop(0, qkv_ref.shape[0], prepare, 0)

    def one(qb, carry):
        rows = pl.ds(pl.multiple_of(qb * TILE, TILE), TILE)
        top = None
        for t in range(blocks):
            kb = lax.rem(qb + t, blocks)
            krows = pl.ds(pl.multiple_of(kb * TILE, TILE), TILE)
            side = (kb > qb).astype(jnp.int32)
            scores = mm(qb_ref[side, rows, :], ka_ref[krows, :], NT)
            if t == 0:
                scores = scores - ahead_of(TILE, TILE, 1) * (2.0 * slope)
            s_ref[:, t * TILE : (t + 1) * TILE] = scores
            part = jnp.max(scores, axis=1, keepdims=True)
            top = part if top is None else jnp.maximum(top, part)
        acc = jnp.zeros((TILE, LANES), F32)
        for t in range(blocks):
            kb = lax.rem(qb + t, blocks)
            krows = pl.ds(pl.multiple_of(kb * TILE, TILE), TILE)
            probs = jnp.exp(s_ref[:, t * TILE : (t + 1) * TILE] - top).astype(BF)
            acc = acc + mm(probs, va_ref[krows, :], NN)
        total = acc[:, HEAD_DIM : HEAD_DIM + 1]
        out = acc[:, :HEAD_DIM] / total
        o_ref[rows, :] = out
        pack_rows(olow_ref, qb, 0, out.astype(BF))
        log_total = top + jnp.log(total)
        lane = lax.broadcasted_iota(jnp.int32, (TILE, LANES), 1)
        row_pos = (qb * TILE + lax.broadcasted_iota(jnp.int32, (TILE, 1), 0)).astype(F32)
        for s in range(2):
            base = row_pos * (slope * (1.0 if s else -1.0)) - log_total
            full = qb_ref[s, rows, :].astype(F32)
            for p, piece in enumerate(split3(base)):
                full = jnp.where(lane == HEAD_DIM + 6 + p, piece.astype(F32), full)
            qb_ref[s, rows, :] = full.astype(BF)
        return carry

    lax.fori_loop(0, blocks, one, 0)


def attn_fwd(h, coefs, qkv, qx, kx):
    blocks, half, _ = qkv.shape
    seq_len = 2 * half * blocks
    outs = [
        shape_of((seq_len, HEAD_DIM), F32),
        shape_of((blocks, half, LANES), BF),
        shape_of((2, seq_len, LANES), BF),
        shape_of((seq_len, LANES), BF),
        shape_of((seq_len, LANES), BF),
    ]
    return pl.pallas_call(
        partial(fwd_kernel, h),
        grid=(1,),
        out_shape=in_hbm(outs),
        in_specs=[
            SMEM_SPEC,
            whole_spec(qkv),
            pl.BlockSpec((1, *qx.shape[1:]), lambda i: (h, 0, 0, 0)),
            whole_spec(kx),
        ],
        out_specs=[whole_spec(a) for a in outs],
        scratch_shapes=[pltpu.VMEM((TILE, seq_len), F32)],
        compiler_params=pltpu.CompilerParams(vmem_limit_bytes=36 * 2**20),
        cost_estimate=takes(11),
        name="attn_fwd",
    )(coefs, *from_hbm([qkv, qx, kx]))


def pack_rows(ref, b, part, values):
    half = ref.shape[1]
    for p in range(TILE // half):
        lane = part * LANES + (p % 2) * HEAD_DIM
        ref[b * (TILE // (2 * half)) + p // 2, :, lane : lane + HEAD_DIM] = values[
            p * half : (p + 1) * half
        ]


def unpack_pair(first, second):
    low_lane = lax.broadcasted_iota(jnp.int32, first.shape, 1) < HEAD_DIM
    first, second = first.astype(F32), second.astype(F32)
    upper = jnp.where(low_lane, first, pltpu.roll(second, HEAD_DIM, 1))
    lower = jnp.where(low_lane, pltpu.roll(first, HEAD_DIM, 1), second)
    return upper.astype(BF), lower.astype(BF)


def bwd_kernel(h, coef_ref, go_ref, o_ref, qb_ref, ka_ref, va_ref, out_ref, ga_ref, dq_ref, kt_ref):
    seq_len = go_ref.shape[0]
    blocks = seq_len // TILE
    lo = h * HEAD_DIM
    slope = coef_ref[h, 6]

    def prepare(b, carry):
        rows = pl.ds(pl.multiple_of(b * TILE, TILE), TILE)
        go = go_ref[rows, lo : lo + HEAD_DIM].astype(F32)
        delta = jnp.sum(go * o_ref[rows, :], axis=1, keepdims=True)
        lane = lax.broadcasted_iota(jnp.int32, (TILE, LANES), 1)
        full = jnp.where(lane < HEAD_DIM, head_first(go_ref[rows, :], h), 0.0)
        for p, piece in enumerate(split3(-delta)):
            full = jnp.where(lane == HEAD_DIM + p, piece.astype(F32), full)
        ga_ref[rows, :] = full.astype(BF)
        kt_ref[:, rows] = ka_ref[rows, :].astype(F32).T.astype(BF)
        dq_ref[:, rows] = jnp.zeros((HEAD_DIM, TILE), F32)
        return carry

    lax.fori_loop(0, blocks, prepare, 0)

    def one(kb, carry):
        krows = pl.ds(pl.multiple_of(kb * TILE, TILE), TILE)
        ka = ka_ref[krows, :]
        va = va_ref[krows, :]
        kt = kt_ref[:HEAD_DIM, krows]
        dv = jnp.zeros((TILE, LANES), F32)
        dk = jnp.zeros((TILE, LANES), F32)
        for t in range(blocks):
            qb = lax.rem(kb + t, blocks)
            rows = pl.ds(pl.multiple_of(qb * TILE, TILE), TILE)
            ga = ga_ref[rows, :]
            qa = qb_ref[(kb > qb).astype(jnp.int32), rows, :]
            scores = mm(ka, qa, NT)
            if t == 0:
                scores = scores - ahead_of(TILE, TILE, 0) * (2.0 * slope)
            probs = jnp.exp(scores)
            ds = (probs * mm(va, ga, NT)).astype(BF)
            dv = dv + mm(probs.astype(BF), ga, NN)
            dk = dk + mm(ds, qa, NN)
            dq_ref[:, rows] += mm(kt, ds, NN)
        pack_rows(out_ref, kb, 1, dk[:, :HEAD_DIM].astype(BF))
        pack_rows(out_ref, kb, 2, dv[:, :HEAD_DIM].astype(BF))
        return carry

    lax.fori_loop(0, blocks, one, 0)

    def finish(b, carry):
        rows = pl.ds(pl.multiple_of(b * TILE, TILE), TILE)
        pack_rows(out_ref, b, 0, (dq_ref[:, rows].T * 0.125).astype(BF))
        return carry

    lax.fori_loop(0, blocks, finish, 0)


def attn_bwd(h, coefs, go, o, qb, ka, va, blocks):
    seq_len = go.shape[0]
    half = seq_len // (2 * blocks)

    return pl.pallas_call(
        partial(bwd_kernel, h),
        grid=(1,),
        out_shape=pltpu.HBM((blocks, half, 3 * LANES), BF),
        in_specs=[SMEM_SPEC, *[whole_spec(a) for a in (go, o, qb, ka, va)]],
        out_specs=pl.BlockSpec((blocks, half, 3 * LANES), lambda i: (0, 0, 0)),
        scratch_shapes=[
            pltpu.VMEM((seq_len, LANES), BF),
            pltpu.VMEM((HEAD_DIM, seq_len), F32),
            pltpu.VMEM((LANES, seq_len), BF),
        ],
        compiler_params=pltpu.CompilerParams(vmem_limit_bytes=36 * 2**20),
        cost_estimate=takes(16),
        name="attn_bwd",
    )(coefs, *from_hbm([go, o, qb, ka, va]))


def slab_kernel(left_ref, first_ref, second_ref, out_ref, right_ref):
    @pl.when(pl.program_id(0) == 0)
    def _():
        half = first_ref.shape[1]
        for b in range(first_ref.shape[0]):
            for i in range(3):
                lanes = slice(i * LANES, (i + 1) * LANES)
                upper, lower = unpack_pair(first_ref[b, :, lanes], second_ref[b, :, lanes])
                right_ref[2 * b * half : (2 * b + 1) * half, lanes] = upper
                right_ref[(2 * b + 1) * half : (2 * b + 2) * half, lanes] = lower

    grad = mm(left_ref[...], right_ref[...], TN).astype(BF)
    side = grad.shape[0] // 2
    for i in range(3):
        for p in range(2):
            out_ref[0, i * side : (i + 1) * side, p * LANES : (p + 1) * LANES] = grad[
                p * side : (p + 1) * side, i * LANES : (i + 1) * LANES
            ]


def slab_call(left, first, second):
    seq_len, width = left.shape
    blocks = first.shape[0]
    levels = blocks // 2
    block = width // levels
    out = shape_of((levels, 3 * block // 2, 2 * LANES), BF)
    packed = pl.BlockSpec(first.shape, lambda z: (0, 0, 0))
    return pl.pallas_call(
        slab_kernel,
        grid=(levels,),
        out_shape=pltpu.HBM(out.shape, BF),
        in_specs=[pl.BlockSpec((seq_len, block), lambda z: (0, z)), packed, packed],
        out_specs=pl.BlockSpec((1, *out.shape[1:]), lambda z: (z, 0, 0)),
        scratch_shapes=[pltpu.VMEM((seq_len, 3 * LANES), BF)],
        compiler_params=pltpu.CompilerParams(vmem_limit_bytes=24 * 2**20),
        cost_estimate=takes(9),
        name="slab",
    )(*from_hbm([left, first, second]))


def norm_stats(values):
    centred = values - jnp.mean(values, axis=-1, keepdims=True)
    scale = lax.rsqrt(jnp.mean(centred * centred, axis=-1, keepdims=True) + NORM_EPS)
    return centred * scale, scale


def norm_back(grad, xhat, scale, gain):
    scaled = grad * gain
    inner = jnp.mean(scaled * xhat, axis=-1, keepdims=True)
    rows = scale * (scaled - jnp.mean(scaled, axis=-1, keepdims=True) - xhat * inner)
    return rows, jnp.sum(grad * xhat, axis=0, keepdims=True)


def put_columns(outs, dp, level, first, wide_ref):
    rows = wide_ref.shape[0]
    cols = outs[0].shape[-1]
    if len(outs) == 1:
        for s in range(outs[0].shape[0]):
            outs[0][s, level, first : first + rows, :] = wide_ref[:, s * cols : (s + 1) * cols]
        return
    for k, out in enumerate(outs):
        at = pl.multiple_of(jnp.bitwise_xor(dp, k) * cols, cols)
        out[level, first : first + rows, :] = wide_ref[:, pl.ds(at, cols)]


def pair_lanes(source, dp):
    at = (jnp.bitwise_xor(source // 2, dp) * 2 + source % 2) * LANES
    return pl.ds(pl.multiple_of(at, LANES), LANES)


def row_kernel(ids_ref, first_ref, second_ref, hidden_ref, wo_ref, gain_ref, attn_ref, xhat_ref, scale_ref, nf_ref, res_ref):
    half = first_ref.shape[1]
    for s in range(first_ref.shape[0]):
        upper, lower = unpack_pair(first_ref[s], second_ref[s])
        attn_ref[:half, pair_lanes(s, ids_ref[0])] = upper
        attn_ref[half:, pair_lanes(s, ids_ref[0])] = lower
    residual = hidden_ref[...] + mm(attn_ref[...], wo_ref[...], NN)
    xhat, scale = norm_stats(residual)
    xhat_ref[...] = xhat
    scale_ref[...] = scale
    nf_ref[...] = (xhat * gain_ref[...]).astype(BF)
    res_ref[...] = residual


def row_call(ids, came, hidden, w_output, gain):
    rows, width = hidden.shape
    wide, low = shape_of((rows, width), F32), shape_of((rows, width), BF)
    inputs = [*came, hidden, w_output, gain]
    outs = [low, wide, shape_of((rows, 1), F32), low, wide]
    return pl.pallas_call(
        row_kernel,
        grid=(1,),
        out_shape=in_hbm(outs),
        in_specs=[SMEM_SPEC, *[whole_spec(a) for a in inputs]],
        out_specs=[whole_spec(a) for a in outs],
        compiler_params=pltpu.CompilerParams(vmem_limit_bytes=16 * 2**20),
        cost_estimate=takes(5),
        name="attn_rows",
    )(ids, *from_hbm(inputs))


def ffn_kernel(
    ids_ref, nf_a, nf_b, cot_a, cot_b, up_ref, down_ref, *refs
):
    sums, out, (nf_ref, cot_ref) = refs[:4], refs[4], refs[5:]
    step = pl.program_id(0)
    rows = nf_a.shape[0]

    @pl.when(step == 0)
    def _():
        nf_ref[:rows] = nf_a[...]
        nf_ref[rows:] = nf_b[...]
        cot_ref[:rows] = cot_a[...]
        cot_ref[rows:] = cot_b[...]
        for ref in sums:
            ref[...] = jnp.zeros(ref.shape, F32)

    nf = nf_ref[...]
    cot = cot_ref[...]
    up = up_ref[...]
    down = down_ref[...]
    pre = mm(nf, up, NN)
    phi = 0.5 + 0.5 * lax.erf(pre * math.sqrt(0.5))
    activ = (pre * phi).astype(BF)
    slope = phi + pre * (jnp.exp(-0.5 * pre * pre) * (1.0 / math.sqrt(2.0 * math.pi)))
    grad_pre = (slope * mm(cot, down, NT)).astype(BF)
    mix = mm(activ, down, NN)
    gnf = mm(grad_pre, up, NT)
    for i, part in enumerate((mix[:rows], mix[rows:], gnf[:rows], gnf[rows:])):
        sums[i][...] += part
    gwd = mm(activ, cot, TN).astype(BF)
    gwu = mm(nf, grad_pre, TN).astype(BF)
    shards, levels, _, cols = out.shape
    tile = gwd.shape[0]
    block = gwu.shape[0] // levels
    for s in range(shards):
        out[s, step, :tile, :] = gwd[:, s * cols : (s + 1) * cols]
    for level in range(levels):
        out[step, level, tile:, :] = gwu[level * block : (level + 1) * block]


def ffn_call(ids, nf, cot, w_up, w_down, shards, part):
    rows, width = nf[0].shape
    ff = w_up.shape[1]
    tile = ff // (shards * 4)
    inputs = [*nf, *cot]
    out_sum = shape_of((rows, width), F32)
    out_grad = shape_of((shards, shards, 2 * tile, width // shards), BF)

    def tile_at(d, ids):
        return d * 4 + part * 2 + ids[1]

    return pl.pallas_call(
        ffn_kernel,
        grid_spec=pltpu.PrefetchScalarGridSpec(
            num_scalar_prefetch=1,
            grid=(shards,),
            in_specs=[
                *[whole_spec(array) for array in inputs],
                pl.BlockSpec((width, tile), lambda d, ids: (0, tile_at(d, ids))),
                pl.BlockSpec((tile, width), lambda d, ids: (tile_at(d, ids), 0)),
            ],
            out_specs=[whole_spec(out_sum)] * 4 + [whole_spec(out_grad)],
            scratch_shapes=[
                pltpu.VMEM((2 * rows, width), BF),
                pltpu.VMEM((2 * rows, width), BF),
            ],
        ),
        out_shape=in_hbm([out_sum] * 4 + [out_grad]),
        compiler_params=pltpu.CompilerParams(vmem_limit_bytes=44 * 2**20),
        cost_estimate=takes(13),
        name="ffn",
    )(ids, *from_hbm([*inputs, w_up, w_down]))


def branch_kernel(
    ids_ref, wo_ref, gnf_a, came_a, gnf_b, came_b, xhat_ref, scale_ref, gain_ref, cot_ref,
    resid_ref, branch_ref, gattn_ref, ggain_ref, wide_ref, held_ref, sem,
):
    copy = pltpu.make_async_copy(wo_ref, held_ref, sem)
    copy.start()
    gnf = gnf_a[...] + came_a[...] + gnf_b[...] + came_b[...]
    rows, ggain = norm_back(gnf, xhat_ref[...], scale_ref[...], gain_ref[...])
    ggain_ref[...] = ggain
    resid = cot_ref[...].astype(F32) + rows
    resid_ref[...] = resid
    branch = resid.astype(BF)
    branch_ref[...] = branch
    copy.wait()
    wide_ref[...] = mm(branch, held_ref[...], NT).astype(BF)
    for s in range(gattn_ref.shape[0]):
        gattn_ref[s] = wide_ref[:, pair_lanes(s, ids_ref[0])]


def branch_call(ids, gnf, xhat, scale, gain, cot, w_output, blocks):
    rows, width = xhat.shape
    wide, low = shape_of((rows, width), F32), shape_of((rows, width), BF)
    inputs = [*gnf, xhat, scale, gain, cot]
    outs = [wide, low, shape_of((blocks, rows, width // blocks), BF), shape_of((1, width), F32)]
    return pl.pallas_call(
        branch_kernel,
        grid=(1,),
        out_shape=in_hbm(outs),
        in_specs=[
            SMEM_SPEC,
            pl.BlockSpec(memory_space=pl.ANY),
            *[whole_spec(a) for a in inputs],
        ],
        out_specs=[whole_spec(a) for a in outs],
        scratch_shapes=[
            pltpu.VMEM((rows, width), BF),
            pltpu.VMEM((width, width), BF),
            pltpu.SemaphoreType.DMA,
        ],
        compiler_params=pltpu.CompilerParams(vmem_limit_bytes=20 * 2**20),
        cost_estimate=takes(6),
        name="branch",
    )(ids, *from_hbm([w_output, *inputs]))


GAIN_ROWS = 16


def wgrad_kernel(n_left, ids_ref, *refs):
    lefts = refs[: 2 * n_left]
    rights = refs[2 * n_left : 2 * n_left + 2]
    outs, wide_ref = refs[2 * n_left + 2 : -1], refs[-1]
    dp, core = ids_ref[0], ids_ref[1]
    level = pl.program_id(0)
    rows = lefts[0].shape[0]
    block = wide_ref.shape[0]
    at = pl.ds(pl.multiple_of((level * 2 + core) * block, block), block)
    for i in range(n_left):
        wide_ref[...] = (
            mm(lefts[2 * i][:, at], rights[0][:rows], TN)
            + mm(lefts[2 * i + 1][:, at], rights[1][:rows], TN)
        ).astype(BF)
        put_columns(outs, dp, level, i * block, wide_ref)
    extra = rights[0].shape[0] - rows
    if extra:
        takes = jnp.where((level == 0) & (core == 0), 1.0, 0.0)
        gains = rights[0][rows:].astype(F32) + rights[1][rows:].astype(F32)
        wide_ref[:extra] = (gains * takes).astype(BF)
        put_columns(outs, dp, level, n_left * block, wide_ref.at[:extra])


def wgrad_call(ids, lefts, rights, shards, levels, apart):
    n_left = len(lefts)
    flat = [array for pair in lefts for array in pair]
    width = rights[0].shape[1]
    rows, columns = flat[0].shape
    block = columns // (2 * levels)
    extra = rights[0].shape[0] - rows
    shape = (levels, n_left * block + extra, width // shards)
    outs = [shape_of(shape, BF)] * shards if apart else [shape_of((shards, *shape), BF)]
    return pl.pallas_call(
        partial(wgrad_kernel, n_left),
        grid_spec=pltpu.PrefetchScalarGridSpec(
            num_scalar_prefetch=1,
            grid=(levels,),
            in_specs=[whole_spec(array) for array in (*flat, *rights)],
            out_specs=[whole_spec(out) for out in outs],
            scratch_shapes=[pltpu.VMEM((block, width), BF)],
        ),
        out_shape=in_hbm(outs),
        compiler_params=pltpu.CompilerParams(vmem_limit_bytes=24 * 2**20),
        cost_estimate=takes(6),
        name="wgrad",
    )(ids, *from_hbm([*flat, *rights]))


def tail_kernel(
    ids_ref, wq_ref, wk_ref, wv_ref, first_ref, second_ref, xhat_ref, scale_ref, gain_ref, resid_ref, ggain_ref,
    gh_ref, wide_ref, held_ref, sems,
):
    copies = [
        pltpu.make_async_copy(w_ref, held_ref.at[i], sems.at[i])
        for i, w_ref in enumerate((wq_ref, wk_ref, wv_ref))
    ]
    for copy in copies:
        copy.start()
    total = None
    for i, copy in enumerate(copies):
        half = first_ref.shape[1]
        lanes = slice(i * LANES, (i + 1) * LANES)
        for s in range(first_ref.shape[0]):
            upper, lower = unpack_pair(first_ref[s, :, lanes], second_ref[s, :, lanes])
            wide_ref[:half, pair_lanes(s, ids_ref[0])] = upper
            wide_ref[half:, pair_lanes(s, ids_ref[0])] = lower
        copy.wait()
        term = mm(wide_ref[...], held_ref[i], NT)
        total = term if total is None else total + term
    rows, ggain = norm_back(total, xhat_ref[...], scale_ref[...], gain_ref[...])
    count = wide_ref.shape[0]
    gh_ref[:count] = (resid_ref[...] + rows).astype(BF)
    at = lax.broadcasted_iota(jnp.int32, (GAIN_ROWS, ggain.shape[1]), 0)
    gains = jnp.where(at == 0, ggain, jnp.where(at == 1, ggain_ref[...], 0.0))
    gh_ref[count:] = gains.astype(BF)


def tail_call(ids, came, weights, xhat, scale, gain, resid, ggain):
    rows, width = xhat.shape
    inputs = [*came, xhat, scale, gain, resid, ggain]
    return pl.pallas_call(
        tail_kernel,
        grid=(1,),
        out_shape=pltpu.HBM((rows + GAIN_ROWS, width), BF),
        in_specs=[
            SMEM_SPEC,
            *[pl.BlockSpec(memory_space=pl.ANY)] * 3,
            *[whole_spec(a) for a in inputs],
        ],
        out_specs=whole_spec(shape_of((rows + GAIN_ROWS, width), BF)),
        scratch_shapes=[
            pltpu.VMEM((rows, width), BF),
            pltpu.VMEM((3, width, width), BF),
            pltpu.SemaphoreType.DMA((3,)),
        ],
        compiler_params=pltpu.CompilerParams(vmem_limit_bytes=32 * 2**20),
        cost_estimate=takes(8),
        name="tail",
    )(ids, *from_hbm([*weights, *inputs]))


def add_low(left, right):
    return (left.astype(F32) + right.astype(F32)).astype(BF)


def pick(array, index, axis):
    return lax.dynamic_index_in_dim(array, index, axis, keepdims=False)


def after(value, *others):
    return lax.optimization_barrier((value, *others))[0]


CORE_SWAP = [(i, i ^ 1) for i in range(8)]
TO_OWNERS = [(p * 8 + b, (p ^ (b // 2)) * 8 + b) for p in range(4) for b in range(8)]
DP_STEPS = [[(i, i ^ k) for i in range(4)] for k in (1, 2, 3)]
Z_NEAR = [(i, i ^ 2) for i in range(8)]
Z_FAR = [(i, i ^ 4) for i in range(8)]


def core_swap(values):
    return lax.ppermute(values, "blk", CORE_SWAP)


def dp_send(shares):
    return [lax.ppermute(share, "dp", perm) for share, perm in zip(shares[1:], DP_STEPS)]


def sum_low(came, own):
    total = own.astype(F32)
    for part in came:
        total = total + part.astype(F32)
    return total.astype(BF)


def z_near(totals, level):
    def two(first, second):
        picked = [jnp.stack([pick(t, first, 0), pick(t, second, 0)]) for t in totals]
        return jnp.concatenate(picked, axis=1) if len(picked) > 1 else picked[0]

    send = two(jnp.bitwise_xor(level, 1), jnp.bitwise_xor(level, 3))
    return lax.ppermute(send, "blk", Z_NEAR), two(level, jnp.bitwise_xor(level, 2)), send


def z_far(came, keep):
    send = add_low(keep[1], came[1])
    return lax.ppermute(send, "blk", Z_FAR), add_low(keep[0], came[0]), send


def gather_near(piece):
    two = jnp.stack([piece, lax.ppermute(piece, "blk", Z_FAR)])
    four = jnp.concatenate([two, lax.ppermute(two, "blk", Z_NEAR)])
    return four, core_swap(four)


def assemble_first_kernel(a_ref, down_ref, up_ref):
    core = pl.program_id(1)
    cols = a_ref.shape[2]
    tile = a_ref.shape[1] // 2
    down_ref[0, 0, 0] = a_ref[0, :tile].astype(F32)
    up_ref[:, pl.ds(pl.multiple_of(core * cols, cols), cols)] = a_ref[0, tile:].astype(F32)


def assemble_kernel(
    n_out, at_ref, b_ref, own_ref, other_ref, down_in, up_in, down_ref, up_ref, out_ref, *refs
):
    head_refs, (skip_ref, attn_gain_ref, ffn_gain_ref) = refs[:3], refs[3:]
    core = pl.program_id(1)
    cols = b_ref.shape[2]
    tile = down_ref.shape[3]
    down_ref[0, 0, 0] = b_ref[0, :tile].astype(F32)
    up_ref[:, pl.ds(pl.multiple_of(core * cols, cols), cols)] = b_ref[0, tile : 2 * tile].astype(
        F32
    )
    out_ref[...] = b_ref[0, 2 * tile : 2 * tile + n_out].astype(F32)
    half = head_refs[0].shape[0] // 2
    for i, ref in enumerate(head_refs):
        first = 2 * tile + n_out + i * half
        lanes = pl.ds(pl.multiple_of(core * LANES, LANES), LANES)
        for side in range(2):
            ref[side * half : (side + 1) * half, lanes] = b_ref[
                0, first : first + half, side * LANES : (side + 1) * LANES
            ].astype(F32)

    def put(ref):
        block = skip_ref.shape[3]
        for i in range(2):
            skip_ref[i, 0, core] = ref[0, i * block : (i + 1) * block].astype(F32)

        @pl.when((pl.program_id(0) == 0) & (core == 0))
        def _():
            gains = ref[0, 2 * block :].astype(F32)
            attn_gain_ref[...] = gains[0:1]
            ffn_gain_ref[...] = gains[1:2]

    pl.when(at_ref[1] == core)(partial(put, own_ref))
    pl.when(at_ref[1] != core)(partial(put, other_ref))


def assemble_specs(whole, tile, part):
    cols = whole.shape[2]
    source = pl.BlockSpec((1, *whole.shape[1:]), lambda z, c, *at: (z * 2 + c, 0, 0))
    down = pl.BlockSpec((1, 1, 1, tile, cols), lambda z, c, *at: (z, part, c, 0, 0))
    up = pl.BlockSpec((tile, 2 * cols), lambda z, c, *at: (z, part))
    return source, down, up


def assemble_first(whole_a):
    blocks, rows_a, cols = whole_a.shape
    levels, tile = blocks // 2, rows_a // 2
    outs = [shape_of((levels, 2, 2, tile, cols), F32), shape_of((levels * tile, 4 * cols), F32)]
    source, down, up = assemble_specs(whole_a, tile, 0)
    return pl.pallas_call(
        assemble_first_kernel,
        grid=(levels, 2),
        out_shape=in_hbm(outs),
        in_specs=[source],
        out_specs=[down, up],
        compiler_params=pltpu.CompilerParams(vmem_limit_bytes=16 * 2**20),
        cost_estimate=takes(4),
        name="assemble_first",
    )(*from_hbm([whole_a]))


def assemble_call(at, whole_b, own, others, begun, n_out):
    blocks, _, cols = whole_b.shape
    levels, _, _, tile, _ = begun[0].shape
    rows = own.shape[1]
    block = (rows - GAIN_ROWS) // 2

    def place(z, c, at):
        k = jnp.bitwise_xor(z, at[0])
        return ((k % 2) * 2 + k // 2, 0, 0)

    outs = [
        *[shape_of(a.shape, F32) for a in begun],
        shape_of((blocks * n_out, cols), F32),
        *[shape_of((levels * tile, cols), F32)] * 3,
        shape_of((2, levels, 2, block, cols), F32),
        *[shape_of((1, cols), F32)] * 2,
    ]
    source, down, up = assemble_specs(whole_b, tile, 1)
    return pl.pallas_call(
        partial(assemble_kernel, n_out),
        grid_spec=pltpu.PrefetchScalarGridSpec(
            num_scalar_prefetch=1,
            grid=(levels, 2),
            in_specs=[
                source,
                *[pl.BlockSpec((1, rows, cols), place)] * 2,
                *[pl.BlockSpec(memory_space=pl.ANY)] * 2,
            ],
            out_specs=[
                down,
                up,
                pl.BlockSpec((n_out, cols), lambda z, c, at: (z * 2 + c, 0)),
                *[pl.BlockSpec((tile, cols), lambda z, c, at: (z, 0))] * 3,
                pl.BlockSpec((2, 1, 2, block, cols), lambda z, c, at: (0, z, 0, 0, 0)),
                *[pl.BlockSpec((1, cols), lambda z, c, at: (0, 0))] * 2,
            ],
        ),
        out_shape=in_hbm(outs),
        input_output_aliases={4: 0, 5: 1},
        compiler_params=pltpu.CompilerParams(vmem_limit_bytes=24 * 2**20),
        cost_estimate=takes(8),
        name="assemble",
    )(at, *from_hbm([whole_b, own, others, *begun]))


def on_device_grid(
    frames,
    skip_feats,
    w_skip,
    gain_attn,
    w_query,
    w_key,
    w_value,
    w_output,
    gain_ffn,
    w_up,
    w_down,
    cotangent,
    utt_lengths,
    padded_lengths,
):
    row_count, width = frames.shape
    blocks = lax.axis_size("blk")
    shards = lax.axis_size("dp")
    seq_len = row_count * blocks
    pair = width // blocks
    blk = lax.axis_index("blk")
    dp = lax.axis_index("dp")

    joined = jnp.concatenate([frames, skip_feats], axis=1)
    hidden = product("rc,cd->rd", joined, w_skip)
    core, level = blk % 2, blk // 2
    ids = jnp.stack([dp, core]).astype(jnp.int32)

    def behind(values, *others):
        return [after(v, *others) for v in values]

    def exchange(values):
        return lax.all_to_all(values, "blk", 0, 0, tiled=True)

    xhat_attn, scale_attn, normed, send_first, send_second = qkv_call(
        ids, hidden, gain_attn.reshape(1, width), (w_query, w_key, w_value), blocks
    )
    qkv_first = exchange(send_first)
    mine = jnp.bitwise_xor(level, dp) * 2 + core
    slopes = lax.dynamic_slice_in_dim(alibi_slopes(seq_len), mine * 2, 2, 0)
    coefs, qx, kx = attn_tables(utt_lengths[0], padded_lengths[0], slopes, seq_len)
    qkv_second = exchange(after(send_second, qkv_first))
    o_first, low_first, *kept_first = attn_fwd(0, coefs, qkv_first, qx, kx)
    qkv_second = after(qkv_second, low_first)
    came_first = exchange(after(low_first, qkv_second))
    o_second, low_second, *kept_second = attn_fwd(1, coefs, qkv_second, qx, kx)
    came_second = exchange(after(low_second, came_first))
    normed_all = lax.all_gather(after(normed, came_second), "blk", axis=0, tiled=True)

    levels = blocks // 2
    cols = width // shards
    gain_row = gain_ffn.reshape(1, width)

    attn, xhat_ffn, scale_ffn, nf, residual = row_call(
        ids, (came_first, came_second), hidden, w_output, gain_row
    )
    cot = (cotangent, core_swap(cotangent))
    joined_pairs = [(frames, core_swap(frames)), (skip_feats, core_swap(skip_feats))]
    nf = (nf, core_swap(nf))
    mix_a, mix_a_send, gnf_a, gnf_a_send, share_a = ffn_call(ids, nf, cot, w_up, w_down, shards, 0)
    sum_a = lax.psum_scatter(share_a, "dp", scatter_dimension=0)
    gnf_a_came = core_swap(gnf_a_send)
    mix_b, mix_b_send, gnf_b, gnf_b_send, share_b = ffn_call(ids, nf, cot, w_up, w_down, shards, 1)
    grad_residual, grad_branch, grad_attn, ggain_ffn = branch_call(
        ids,
        (gnf_a, gnf_a_came, gnf_b, core_swap(gnf_b_send)),
        xhat_ffn,
        scale_ffn,
        gain_row,
        cotangent,
        w_output,
        blocks,
    )
    grad_attn = after(grad_attn, normed_all)
    grad_attn_came = exchange(grad_attn).reshape(seq_len, pair)
    mix_send = after(mix_a_send, grad_branch) + mix_b_send
    mixed = (residual + mix_a + mix_b + core_swap(mix_send)).astype(BF)
    swapped = core_swap(jnp.stack([attn, grad_branch]))
    sum_b = lax.psum_scatter(share_b, "dp", scatter_dimension=0)

    def bwd(h, go):
        o, (qb, ka, va) = ((o_first, kept_first), (o_second, kept_second))[h]
        return attn_bwd(h, coefs, go, o, qb, ka, va, blocks)

    dq_first = bwd(0, grad_attn_came)
    za, keep_za, send = z_near([after(sum_a, dq_first)], level)
    came_first = exchange(after(dq_first, send))
    dq_second = bwd(1, after(grad_attn_came, send))

    za_far, keep_za, send = z_far(after(za, dq_second), keep_za)
    slab = slab_call(after(normed_all, send), dq_first, dq_second)
    piece_a = add_low(keep_za, after(za_far, slab))
    whole_a = lax.all_gather(piece_a, "blk", axis=0, tiled=False)
    came_second = exchange(after(dq_second, came_first, piece_a))
    heads = lax.ppermute(slab, ("dp", "blk"), TO_OWNERS)
    share_c = wgrad_call(
        ids, [(attn, swapped[0])], (after(grad_branch, slab), swapped[1]), shards, levels, True
    )
    n_out = share_c[0].shape[1]
    xc = dp_send(share_c)
    gh = tail_call(
        ids,
        behind((came_first, came_second), *share_c),
        (w_query, w_key, w_value),
        xhat_attn,
        scale_attn,
        gain_attn.reshape(1, width),
        grad_residual,
        ggain_ffn,
    )
    gh_came = core_swap(gh)
    sum_c = sum_low(behind(xc, gh), share_c[0])
    zb, keep_zb, send = z_near((after(sum_b, slab), sum_c, after(heads, gh)), level)
    share_d = wgrad_call(ids, joined_pairs, (after(gh, send), gh_came), shards, levels, True)
    xd = dp_send(share_d)
    zb_far, keep_zb, send = z_far(after(zb, *share_d), keep_zb)
    grad_joined = product("rd,cd->rc", after(gh, send)[:row_count], w_skip)
    grad_frames = grad_joined[:, :width].astype(BF)
    grad_skip = grad_joined[:, width:].astype(BF)

    begun = assemble_first(after(whole_a, grad_joined))
    sum_d = sum_low(behind(xd, *begun), share_d[0])
    zd, keep_zd, send = z_near([sum_d], level)
    zd_far, keep_zd, send = z_far(after(zd, send), keep_zd)
    piece_b = add_low(keep_zb, after(zb_far, send))
    whole_b = lax.all_gather(piece_b, "blk", axis=0, tiled=False)
    piece_d = add_low(keep_zd, after(zd_far, piece_b))
    own, others = gather_near(piece_d)
    g_down, g_up, g_output, *g_heads, g_skip, g_attn, g_ffn = assemble_call(
        jnp.stack([level, core]).astype(jnp.int32), whole_b, own, others, begun, n_out
    )
    return (
        mixed,
        grad_frames,
        grad_skip,
        g_skip.reshape(-1, cols),
        g_attn.reshape(-1),
        g_heads[0],
        g_heads[1],
        g_heads[2],
        g_output,
        g_ffn.reshape(-1),
        g_up,
        g_down.reshape(-1, cols),
    )


def solution(mesh):
    shape = dict(mesh.shape)
    grid = (shape["dp"], shape["blk"])
    body = on_device_grid if grid == (4, 8) else on_device_general
    return jax.shard_map(
        body,
        mesh=mesh,
        in_specs=(
            P(("dp", "blk"), None),
            P(("dp", "blk"), None),
            P(),
            P(),
            P(),
            P(),
            P(),
            P(),
            P(),
            P(),
            P(),
            P(("dp", "blk"), None),
            P("dp", None),
            P("dp", None),
        ),
        out_specs=(
            P(("dp", "blk"), None),
            P(("dp", "blk"), None),
            P(("dp", "blk"), None),
            P(None, "dp"),
            P("dp"),
            P(None, "dp"),
            P(None, "dp"),
            P(None, "dp"),
            P(None, "dp"),
            P("dp"),
            P(None, "dp"),
            P(None, "dp"),
        ),
        check_vma=False,
    )
```
